32 devices in a mesh: space: 8 (over y, x, core), band: 4 (over z).
Axes of the slice: x: 2, y: 2, z: 4, core: 2. Of those that a mesh axis runs over, the one named last changes fastest.
Arguments:
- psi: float32 [64, 32928], P('band', 'space'), may hold values from -400 to 400
- ham: bfloat16 [96, 512, 512], P('space'), may hold values from -2 to 2, as said below
- conn: int32 [96, 512], P('space'), may hold values from 0 to 4703, as said below
- face_rows: int32 [4704], P('space'), may hold values from 0 to 4115, as said below
Outputs:
- ortho: float32 [64, 32928], P('band', 'space')
The draws below stay inside these ranges and needn't reach their ends.
Inputs may be any that keep to these rules, and one draw needn't show every extreme that they name: `conn`: rows s * 12 to (s + 1) * 12 - 1 are the elements of domain s. Entries at element-local nodes below 448 name the domain's own rows 0 to 4115; entries at and above 448 name ghost slots 4116 + j, where ghost slot j is the node listed at position j of face_rows of domain (s + 1) mod 8. Every own row and every ghost slot of a domain is named by some element. `face_rows`: entries s * 588 to (s + 1) * 588 - 1 are 588 distinct own rows of domain s: the nodes of its lower face. `ham`: each matrix is symmetric.
All inputs are finite; a program needn't handle non-finite values.
Results may differ from the reference program's by a relative error of at most 0.0037.
Values may be sent and summed in bfloat16 or wider, within the bound.
No kernel may reach another device: no remote copies, remote signals or barrier semaphores. Data moves between devices by JAX's collectives and lax.ppermute only.
A program may use at most 64 MiB of HBM per device.

```python
import math
import jax
import jax.numpy as jnp
from jax import lax

P_SIZE = 8
EX = 4
EY = 3
STEPS = 2
NODE_EL = 512
E_DEV = 12
NODES = 4116
FACE = 588
DOMAINS = 8
BANDS = 64
TOTAL_NODES = 32928


def numbering(key):
    domain_keys = jax.random.split(jax.random.fold_in(key, 17), DOMAINS)
    shuffled = jax.vmap(lambda single: jax.random.permutation(single, NODES))(domain_keys)
    shuffled = shuffled.astype(jnp.int32)
    return ((shuffled - shuffled[:, :1] - 1) % NODES).astype(jnp.int32)


def draw_face_rows(key, part):
    local_rows = numbering(key)
    return local_rows[:, :FACE].reshape(DOMAINS * FACE).astype(jnp.int32)


def draw_conn(key, part):
    local_rows = numbering(key)
    element = jnp.arange(E_DEV, dtype=jnp.int32)
    elem_x = element % EX
    elem_y = element // EX
    local_node = jnp.arange(NODE_EL, dtype=jnp.int32)
    node_x = local_node % P_SIZE
    node_y = local_node // P_SIZE % P_SIZE
    node_z = local_node // (P_SIZE * P_SIZE)
    width_x = (P_SIZE - 1) * EX
    width_y = (P_SIZE - 1) * EY
    grid_x = (elem_x[:, None] * (P_SIZE - 1) + node_x[None, :]) % width_x
    grid_y = (elem_y[:, None] * (P_SIZE - 1) + node_y[None, :]) % width_y
    position = grid_y * width_x + grid_x
    canonical = jnp.minimum(node_z[None, :] * FACE + position, NODES - 1)
    owned = local_rows[:, canonical]
    result = jnp.where(node_z[None, None, :] == P_SIZE - 1, NODES + position[None, :, :], owned)
    return result.reshape(DOMAINS * E_DEV, NODE_EL).astype(jnp.int32)


def draw_ham(key, part):
    count = DOMAINS * E_DEV
    key_entries, key_diagonal = jax.random.split(jax.random.fold_in(key, 29))
    spread = 0.4 * (2.0 / NODE_EL) ** 0.5
    entries = jax.random.truncated_normal(key_entries, -4.0, 4.0, (count, NODE_EL, NODE_EL), jnp.float32)
    diagonal = jax.random.uniform(key_diagonal, (count, NODE_EL), jnp.float32, 0.5, 1.5)
    symmetric = (entries + jnp.swapaxes(entries, 1, 2)) * (0.5 * spread)
    identity = jnp.eye(NODE_EL, dtype=jnp.float32)
    result = symmetric * (1.0 - identity) + diagonal[:, :, None] * identity
    return result.astype(jnp.bfloat16)


def draw_psi(key, part):
    key_values, key_rows, key_cols = jax.random.split(jax.random.fold_in(key, 41), 3)
    row_scale = jnp.exp(jax.random.uniform(key_rows, (BANDS, 1), jnp.float32, 0.0, math.log(10.0)))
    col_scale = jnp.exp(jax.random.uniform(key_cols, (1, TOTAL_NODES), jnp.float32, 0.0, math.log(10.0)))
    values = jax.random.truncated_normal(key_values, -4.0, 4.0, (BANDS, TOTAL_NODES), jnp.float32)
    return (values * row_scale * col_scale).astype(jnp.float32)


def setup_inputs(seed: int = 0) -> dict:
    splits = jax.random.split(jax.random.key(seed), 5)
    return {
        "psi": draw_psi(jax.random.fold_in(splits[4], 71), 0),
        "ham": draw_ham(jax.random.fold_in(splits[4], 71), 0),
        "conn": draw_conn(jax.random.fold_in(splits[4], 71), 0),
        "face_rows": draw_face_rows(jax.random.fold_in(splits[4], 71), 0),
    }


CENTER = 6.25
HALF_WIDTH = 7.5

def take_face(field, rows_list):
    return jnp.take(field, rows_list, axis=1)

def add_face(field, values, rows_list):
    return field.at[:, rows_list].add(values)

def domain_product(operands):
    field, ghost, matrices, links = operands
    extended = jnp.concatenate([field, ghost], axis=1)
    flat_links = links.reshape(-1)
    gathered = jnp.take(extended, flat_links, axis=1).reshape(BANDS, E_DEV, NODE_EL).astype(jnp.float32)
    products = jnp.einsum('bem,eml->bel', gathered, matrices.astype(jnp.float32))
    summed = jnp.zeros((BANDS, NODES + FACE), jnp.float32)
    return summed.at[:, flat_links].add(products.reshape(BANDS, E_DEV * NODE_EL))

def apply_operator(fields, ham_domains, conn_domains, face_domains):
    rounded = fields.astype(jnp.bfloat16)
    face_values = jax.vmap(take_face)(rounded, face_domains)
    ghosts = jnp.roll(face_values, -1, axis=0)
    summed = lax.map(domain_product, (rounded, ghosts, ham_domains, conn_domains))
    received = jnp.roll(summed[:, :, NODES:], 1, axis=0)
    return jax.vmap(add_face)(summed[:, :, :NODES], received, face_domains)

def reference(psi, ham, conn, face_rows):
    fields = psi.reshape(BANDS, DOMAINS, NODES).transpose(1, 0, 2)
    ham_domains = ham.reshape(DOMAINS, E_DEV, NODE_EL, NODE_EL)
    conn_domains = conn.reshape(DOMAINS, E_DEV, NODE_EL)
    face_domains = face_rows.reshape(DOMAINS, FACE)
    previous = fields
    current = (apply_operator(fields, ham_domains, conn_domains, face_domains) - CENTER * fields) / HALF_WIDTH
    for iteration in range(STEPS - 1):
        scaled = (apply_operator(current, ham_domains, conn_domains, face_domains) - CENTER * current) / HALF_WIDTH
        following = 2.0 * scaled - previous
        previous = current
        current = following
    filtered = current.transpose(1, 0, 2).reshape(BANDS, TOTAL_NODES)
    correlation = lax.dot_general(filtered.astype(jnp.float32), filtered.astype(jnp.float32), (((1,), (1,)), ((), ())), precision=lax.Precision.HIGHEST, preferred_element_type=jnp.float32) / TOTAL_NODES
    factor = jnp.linalg.cholesky(correlation)
    return jax.scipy.linalg.solve_triangular(factor, filtered, lower=True)
```

```python
import functools

import jax
import jax.numpy as jnp
from jax import lax
from jax.experimental import pallas as pl
from jax.experimental.pallas import tpu as pltpu
from jax.sharding import PartitionSpec as P

FACE_EL = 64
IN_EL = 448
LANES = 256

CENTER = 6.25
HALF_WIDTH = 7.5

F32 = jnp.float32
BF16 = jnp.bfloat16
VMEM = pl.BlockSpec(memory_space=pltpu.VMEM)
ANY = pl.BlockSpec(memory_space=pl.ANY)
LIMIT = 48 * 1024 * 1024


def round_up(count, unit):
    return -(-count // unit) * unit


def one_hot(low):
    rows = lax.broadcasted_iota(jnp.int32, (LANES, low.shape[1]), 0)
    return jnp.where(rows == low, 1.0, 0.0).astype(BF16)


def stacked(field):
    blocks = field.shape[1] // LANES
    return jnp.concatenate([field[:, i * LANES : (i + 1) * LANES] for i in range(blocks)], axis=0)


def unstacked(rows, bands):
    blocks = rows.shape[0] // bands
    return jnp.concatenate([rows[i * bands : (i + 1) * bands] for i in range(blocks)], axis=1)


def pick(rows, high, low_hot, bands, first=0):
    table = jnp.dot(rows, low_hot, preferred_element_type=F32)
    out = jnp.zeros((bands, low_hot.shape[1]), F32)
    for i in range(rows.shape[0] // bands):
        out = jnp.where(high == i + first, table[i * bands : (i + 1) * bands], out)
    return out


def halves(values):
    upper = values.astype(BF16)
    return upper, (values - upper.astype(F32)).astype(BF16)


def spread(values, high, blocks, first=0):
    rows = []
    for part in halves(values):
        wide = part.astype(F32)
        for i in range(blocks):
            rows.append(jnp.where(high == i + first, wide, 0.0).astype(BF16))
    return jnp.concatenate(rows, axis=0)


def gathered_sum(rows, low_hot):
    both = lax.dot_general(rows, low_hot, (((1,), (1,)), ((), ())), preferred_element_type=F32)
    count = both.shape[0] // 2
    return both[:count] + both[count:]


def face_kernel(psi_ref, face_ref, out_ref, pad_ref):
    bands, nodes = psi_ref.shape
    pad_ref[...] = jnp.zeros_like(pad_ref)
    pad_ref[:, :nodes] = psi_ref[...]
    rows = stacked(pad_ref[...]).astype(BF16)
    face = face_ref[...]
    out_ref[...] = pick(rows, face >> 8, one_hot(face & 255), bands).astype(BF16)


def place(conn, nodes, own):
    return jnp.where(conn >= nodes, conn + (own - nodes), conn)


def interior_kernel(psi_ref, conn_ref, ham_ref, out_ref, pad_ref, ham_vmem, sems):
    bands, nodes = psi_ref.shape
    elements, size = conn_ref.shape
    own = pad_ref.shape[1]
    for e in range(elements):
        pltpu.make_async_copy(ham_ref.at[e], ham_vmem.at[e], sems.at[e]).start()
    pad_ref[...] = jnp.zeros_like(pad_ref)
    pad_ref[:, :nodes] = psi_ref[...]
    rows = stacked(pad_ref[...]).astype(BF16)
    for e in range(elements):
        slots = place(conn_ref[e : e + 1, :], nodes, own)
        inside = pick(rows, slots >> 8, one_hot(slots & 255), bands).astype(BF16)
        pltpu.make_async_copy(ham_ref.at[e], ham_vmem.at[e], sems.at[e]).wait()
        out_ref[:, e * size : (e + 1) * size] = jnp.dot(inside, ham_vmem[e], preferred_element_type=F32)


def first_kernel(psi_ref, conn_ref, ham_ref, face_ref, ghost_ref, part_ref, own_ref, upper_ref, low_ref, pad_ref, ham_vmem, sums, hots, sems):
    bands, nodes = psi_ref.shape
    elements, size = conn_ref.shape
    own = pad_ref.shape[1]
    for e in range(elements):
        pltpu.make_async_copy(ham_ref.at[e, pl.ds(IN_EL, FACE_EL)], ham_vmem.at[e], sems.at[e]).start()
    pad_ref[...] = jnp.zeros_like(pad_ref)
    pad_ref[:, :nodes] = psi_ref[...]
    ghost = stacked(ghost_ref[...])
    first = own // LANES
    blocks = first + ghost.shape[0] // bands
    for e in range(elements):
        slots = place(conn_ref[e : e + 1, :], nodes, own)
        high = slots >> 8
        hot = one_hot(slots & 255)
        hots[:, e * size : (e + 1) * size] = hot
        outside = pick(ghost, high[:, IN_EL:], hot[:, IN_EL:], bands, first).astype(BF16)
        pltpu.make_async_copy(ham_ref.at[e, pl.ds(IN_EL, FACE_EL)], ham_vmem.at[e], sems.at[e]).wait()
        product = part_ref[:, e * size : (e + 1) * size] + jnp.dot(outside, ham_vmem[e], preferred_element_type=F32)
        sums[:, e * size : (e + 1) * size] = spread(product, high, blocks)
    total = unstacked(gathered_sum(sums[...], hots[...]), bands)
    current = (total[:, :own] - CENTER * pad_ref[...]) / HALF_WIDTH
    own_ref[...] = current
    upper_ref[...] = total[:, own:] / HALF_WIDTH
    face = face_ref[...]
    face_hot = one_hot(face & 255)
    terms = halves(stacked(current))
    low_ref[...] = pick(terms[0], face >> 8, face_hot, bands) + pick(terms[1], face >> 8, face_hot, bands)


def second_kernel(psi_ref, conn_ref, ham_ref, face_ref, own_in, upper_in, below_in, above_in, own_ref, upper_ref, pad_ref, ham_vmem, sums, hots, sems):
    bands, nodes = psi_ref.shape
    elements, size = conn_ref.shape
    own = pad_ref.shape[1]
    for e in range(elements):
        pltpu.make_async_copy(ham_ref.at[e], ham_vmem.at[e], sems.at[e]).start()
    pad_ref[...] = jnp.zeros_like(pad_ref)
    pad_ref[:, :nodes] = psi_ref[...]
    first = own // LANES
    face = face_ref[...]
    added = gathered_sum(spread(below_in[...], face >> 8, first), one_hot(face & 255))
    current = own_in[...] + unstacked(added, bands)
    ghost = upper_in[...] + above_in[...]
    rows = jnp.concatenate([stacked(current), stacked(ghost)], axis=0).astype(BF16)
    blocks = rows.shape[0] // bands
    for e in range(elements):
        slots = place(conn_ref[e : e + 1, :], nodes, own)
        high = slots >> 8
        hot = one_hot(slots & 255)
        hots[:, e * size : (e + 1) * size] = hot
        inside = pick(rows, high, hot, bands).astype(BF16)
        pltpu.make_async_copy(ham_ref.at[e], ham_vmem.at[e], sems.at[e]).wait()
        product = jnp.dot(inside, ham_vmem[e], preferred_element_type=F32)
        sums[:, e * size : (e + 1) * size] = spread(product, high, blocks)
    total = unstacked(gathered_sum(sums[...], hots[...]), bands)
    own_ref[...] = 2.0 * ((total[:, :own] - CENTER * current) / HALF_WIDTH) - pad_ref[...]
    upper_ref[...] = total[:, own:] * (2.0 / HALF_WIDTH)


def last_kernel(nodes, own_in, face_ref, below_in, out_ref):
    bands, own = own_in.shape
    face = face_ref[...]
    added = gathered_sum(spread(below_in[...], face >> 8, own // LANES), one_hot(face & 255))
    out_ref[...] = (own_in[...] + unstacked(added, bands))[:, :nodes]


def call(kernel, out_shape, inputs, scratch=(), flops=0, moved=0):
    return pl.pallas_call(
        kernel,
        out_shape=out_shape,
        in_specs=[ANY if array.ndim == 3 else VMEM for array in inputs],
        out_specs=jax.tree.map(lambda _: VMEM, out_shape),
        scratch_shapes=list(scratch),
        compiler_params=pltpu.CompilerParams(vmem_limit_bytes=LIMIT),
        cost_estimate=pl.CostEstimate(flops=flops, bytes_accessed=moved, transcendentals=0),
    )(*inputs)


def from_behind(block, axis, distance):
    devices = range(lax.axis_size(axis))
    route = [((i - distance) % len(devices), i) for i in devices]
    return lax.ppermute(block, axis, route)


def filter_field(psi, ham, conn, face_rows):
    bands, nodes = psi.shape
    elements, size = conn.shape
    own = round_up(nodes, LANES)
    slots = round_up(face_rows.shape[0], LANES)
    blocks = (own + slots) // LANES
    face = jnp.pad(face_rows, (0, slots - face_rows.shape[0]), constant_values=-1)[None]
    shape = jax.ShapeDtypeStruct
    pad = pltpu.VMEM((bands, own), F32)
    copies = pltpu.SemaphoreType.DMA((elements,))
    sums = pltpu.VMEM((2 * blocks * bands, elements * size), BF16)
    hots = pltpu.VMEM((LANES, elements * size), BF16)

    with jax.named_scope("face_values"):
        values = call(face_kernel, shape((bands, slots), BF16), (psi, face), (pad,))
    ghost = from_behind(values, "space", -1)
    with jax.named_scope("interior"):
        part = call(
            interior_kernel, shape((bands, elements * size), F32), (psi, conn, ham),
            (pad, pltpu.VMEM((elements, size, size), BF16), copies), flops=4 * 10**9, moved=8 * 10**6,
        )
    with jax.named_scope("first_step"):
        current, upper, low = call(
            first_kernel,
            (shape((bands, own), F32), shape((bands, slots), F32), shape((bands, slots), F32)),
            (psi, conn, ham, face, ghost, part),
            (pad, pltpu.VMEM((elements, FACE_EL, size), BF16), sums, hots, copies), flops=4 * 10**9, moved=10**6,
        )
    below = from_behind(upper, "space", 1)
    above = from_behind(low, "space", -1)
    with jax.named_scope("second_step"):
        following, upper = call(
            second_kernel,
            (shape((bands, own), F32), shape((bands, slots), F32)),
            (psi, conn, ham, face, current, upper, below, above),
            (pad, pltpu.VMEM((elements, size, size), BF16), sums, hots, copies), flops=8 * 10**9, moved=8 * 10**6,
        )
    below = from_behind(upper, "space", 1)
    with jax.named_scope("last_faces"):
        return call(functools.partial(last_kernel, nodes), shape((bands, nodes), F32), (following, face, below))


def per_device(psi, ham, conn, face_rows):
    node_count = psi.shape[1]
    following = filter_field(psi, ham, conn, face_rows)
    node_rows = lax.all_to_all(following, "band", split_axis=1, concat_axis=0, tiled=True)
    partial_value = lax.dot_general(
        node_rows,
        node_rows,
        (((1,), (1,)), ((), ())),
        precision=lax.Precision.HIGHEST,
        preferred_element_type=jnp.float32,
    )
    correlation = lax.psum(partial_value, ("space", "band"))
    correlation = correlation / (node_count * lax.axis_size("space"))
    factor = jnp.linalg.cholesky(correlation)
    orthonormal = jax.scipy.linalg.solve_triangular(factor, node_rows, lower=True)
    return lax.all_to_all(orthonormal, "band", split_axis=0, concat_axis=1, tiled=True)


def solution(mesh):
    placed = (P("band", "space"), P("space", None, None), P("space", None), P("space"))
    return jax.shard_map(
        per_device, mesh=mesh, in_specs=placed, out_specs=P("band", "space"), check_vma=False
    )
```

```python
import functools

import jax
import jax.numpy as jnp
from jax import lax
from jax.experimental import pallas as pl
from jax.experimental.pallas import tpu as pltpu
from jax.sharding import PartitionSpec as P

FACE_EL = 64
IN_EL = 448
LANES = 256

CENTER = 6.25
HALF_WIDTH = 7.5

F32 = jnp.float32
BF16 = jnp.bfloat16
VMEM = pl.BlockSpec(memory_space=pltpu.VMEM)
ANY = pl.BlockSpec(memory_space=pl.ANY)
LIMIT = 48 * 1024 * 1024


def round_up(count, unit):
    return -(-count // unit) * unit


def one_hot(low):
    rows = lax.broadcasted_iota(jnp.int32, (LANES, low.shape[1]), 0)
    return jnp.where(rows == low, 1.0, 0.0).astype(BF16)


def stacked(field):
    blocks = field.shape[1] // LANES
    return jnp.concatenate([field[:, i * LANES : (i + 1) * LANES] for i in range(blocks)], axis=0)


def unstacked(rows, bands):
    blocks = rows.shape[0] // bands
    return jnp.concatenate([rows[i * bands : (i + 1) * bands] for i in range(blocks)], axis=1)


def pick(rows, high, low_hot, bands, first=0):
    table = jnp.dot(rows, low_hot, preferred_element_type=F32)
    out = jnp.zeros((bands, low_hot.shape[1]), F32)
    for i in range(rows.shape[0] // bands):
        out = jnp.where(high == i + first, table[i * bands : (i + 1) * bands], out)
    return out


def halves(values):
    upper = values.astype(BF16)
    return upper, (values - upper.astype(F32)).astype(BF16)


def spread(values, high, blocks, first=0):
    rows = []
    for part in halves(values):
        wide = part.astype(F32)
        for i in range(blocks):
            rows.append(jnp.where(high == i + first, wide, 0.0).astype(BF16))
    return jnp.concatenate(rows, axis=0)


def gathered_sum(rows, low_hot):
    both = lax.dot_general(rows, low_hot, (((1,), (1,)), ((), ())), preferred_element_type=F32)
    count = both.shape[0] // 2
    return both[:count] + both[count:]


def face_kernel(psi_ref, face_ref, out_ref, pad_ref):
    bands, nodes = psi_ref.shape
    pad_ref[...] = jnp.zeros_like(pad_ref)
    pad_ref[:, :nodes] = psi_ref[...]
    rows = stacked(pad_ref[...]).astype(BF16)
    face = face_ref[...]
    out_ref[...] = pick(rows, face >> 8, one_hot(face & 255), bands).astype(BF16)


def place(conn, nodes, own):
    return jnp.where(conn >= nodes, conn + (own - nodes), conn)


def interior_kernel(psi_ref, conn_ref, ham_ref, out_ref, pad_ref, ham_vmem, sems):
    bands, nodes = psi_ref.shape
    elements, size = conn_ref.shape
    own = pad_ref.shape[1]
    for e in range(elements):
        pltpu.make_async_copy(ham_ref.at[e], ham_vmem.at[e], sems.at[e]).start()
    pad_ref[...] = jnp.zeros_like(pad_ref)
    pad_ref[:, :nodes] = psi_ref[...]
    rows = stacked(pad_ref[...]).astype(BF16)
    for e in range(elements):
        slots = place(conn_ref[e : e + 1, :], nodes, own)
        inside = pick(rows, slots >> 8, one_hot(slots & 255), bands).astype(BF16)
        pltpu.make_async_copy(ham_ref.at[e], ham_vmem.at[e], sems.at[e]).wait()
        out_ref[:, e * size : (e + 1) * size] = jnp.dot(inside, ham_vmem[e], preferred_element_type=F32)


def first_kernel(psi_ref, conn_ref, ham_ref, face_ref, ghost_ref, part_ref, own_ref, upper_ref, low_ref, pad_ref, ham_vmem, sums, hots, sems):
    bands, nodes = psi_ref.shape
    elements, size = conn_ref.shape
    own = pad_ref.shape[1]
    for e in range(elements):
        pltpu.make_async_copy(ham_ref.at[e, pl.ds(IN_EL, FACE_EL)], ham_vmem.at[e], sems.at[e]).start()
    pad_ref[...] = jnp.zeros_like(pad_ref)
    pad_ref[:, :nodes] = psi_ref[...]
    ghost = stacked(ghost_ref[...])
    first = own // LANES
    blocks = first + ghost.shape[0] // bands
    for e in range(elements):
        slots = place(conn_ref[e : e + 1, :], nodes, own)
        high = slots >> 8
        hot = one_hot(slots & 255)
        hots[:, e * size : (e + 1) * size] = hot
        outside = pick(ghost, high[:, IN_EL:], hot[:, IN_EL:], bands, first).astype(BF16)
        pltpu.make_async_copy(ham_ref.at[e, pl.ds(IN_EL, FACE_EL)], ham_vmem.at[e], sems.at[e]).wait()
        product = part_ref[:, e * size : (e + 1) * size] + jnp.dot(outside, ham_vmem[e], preferred_element_type=F32)
        sums[:, e * size : (e + 1) * size] = spread(product, high, blocks)
    total = unstacked(gathered_sum(sums[...], hots[...]), bands)
    current = (total[:, :own] - CENTER * pad_ref[...]) / HALF_WIDTH
    own_ref[...] = current
    upper_ref[...] = total[:, own:] / HALF_WIDTH
    face = face_ref[...]
    face_hot = one_hot(face & 255)
    terms = halves(stacked(current))
    low_ref[...] = pick(terms[0], face >> 8, face_hot, bands) + pick(terms[1], face >> 8, face_hot, bands)


def second_kernel(psi_ref, conn_ref, ham_ref, face_ref, own_in, upper_in, below_in, above_in, own_ref, upper_ref, pad_ref, ham_vmem, sums, hots, sems):
    bands, nodes = psi_ref.shape
    elements, size = conn_ref.shape
    own = pad_ref.shape[1]
    for e in range(elements):
        pltpu.make_async_copy(ham_ref.at[e], ham_vmem.at[e], sems.at[e]).start()
    pad_ref[...] = jnp.zeros_like(pad_ref)
    pad_ref[:, :nodes] = psi_ref[...]
    first = own // LANES
    face = face_ref[...]
    added = gathered_sum(spread(below_in[...], face >> 8, first), one_hot(face & 255))
    current = own_in[...] + unstacked(added, bands)
    ghost = upper_in[...] + above_in[...]
    rows = jnp.concatenate([stacked(current), stacked(ghost)], axis=0).astype(BF16)
    blocks = rows.shape[0] // bands
    for e in range(elements):
        slots = place(conn_ref[e : e + 1, :], nodes, own)
        high = slots >> 8
        hot = one_hot(slots & 255)
        hots[:, e * size : (e + 1) * size] = hot
        inside = pick(rows, high, hot, bands).astype(BF16)
        pltpu.make_async_copy(ham_ref.at[e], ham_vmem.at[e], sems.at[e]).wait()
        product = jnp.dot(inside, ham_vmem[e], preferred_element_type=F32)
        sums[:, e * size : (e + 1) * size] = spread(product, high, blocks)
    total = unstacked(gathered_sum(sums[...], hots[...]), bands)
    own_ref[...] = 2.0 * ((total[:, :own] - CENTER * current) / HALF_WIDTH) - pad_ref[...]
    upper_ref[...] = total[:, own:] * (2.0 / HALF_WIDTH)


def last_kernel(nodes, own_in, face_ref, below_in, out_ref):
    bands, own = own_in.shape
    face = face_ref[...]
    added = gathered_sum(spread(below_in[...], face >> 8, own // LANES), one_hot(face & 255))
    out_ref[...] = (own_in[...] + unstacked(added, bands))[:, :nodes]


def call(kernel, out_shape, inputs, scratch=(), flops=0, moved=0):
    return pl.pallas_call(
        kernel,
        out_shape=out_shape,
        in_specs=[ANY if array.ndim == 3 else VMEM for array in inputs],
        out_specs=jax.tree.map(lambda _: VMEM, out_shape),
        scratch_shapes=list(scratch),
        compiler_params=pltpu.CompilerParams(vmem_limit_bytes=LIMIT),
        cost_estimate=pl.CostEstimate(flops=flops, bytes_accessed=moved, transcendentals=0),
    )(*inputs)


def from_behind(block, axis, distance):
    devices = range(lax.axis_size(axis))
    route = [((i - distance) % len(devices), i) for i in devices]
    return lax.ppermute(block, axis, route)


def filter_field(psi, ham, conn, face_rows):
    bands, nodes = psi.shape
    elements, size = conn.shape
    own = round_up(nodes, LANES)
    slots = round_up(face_rows.shape[0], LANES)
    blocks = (own + slots) // LANES
    face = jnp.pad(face_rows, (0, slots - face_rows.shape[0]), constant_values=-1)[None]
    shape = jax.ShapeDtypeStruct
    pad = pltpu.VMEM((bands, own), F32)
    copies = pltpu.SemaphoreType.DMA((elements,))
    sums = pltpu.VMEM((2 * blocks * bands, elements * size), BF16)
    hots = pltpu.VMEM((LANES, elements * size), BF16)

    with jax.named_scope("face_values"):
        values = call(face_kernel, shape((bands, slots), BF16), (psi, face), (pad,))
    ghost = from_behind(values, "space", -1)
    with jax.named_scope("interior"):
        part = call(
            interior_kernel, shape((bands, elements * size), F32), (psi, conn, ham),
            (pad, pltpu.VMEM((elements, size, size), BF16), copies), flops=4 * 10**9, moved=8 * 10**6,
        )
    with jax.named_scope("first_step"):
        current, upper, low = call(
            first_kernel,
            (shape((bands, own), F32), shape((bands, slots), F32), shape((bands, slots), F32)),
            (psi, conn, ham, face, ghost, part),
            (pad, pltpu.VMEM((elements, FACE_EL, size), BF16), sums, hots, copies), flops=4 * 10**9, moved=10**6,
        )
    below = from_behind(upper, "space", 1)
    above = from_behind(low, "space", -1)
    with jax.named_scope("second_step"):
        following, upper = call(
            second_kernel,
            (shape((bands, own), F32), shape((bands, slots), F32)),
            (psi, conn, ham, face, current, upper, below, above),
            (pad, pltpu.VMEM((elements, size, size), BF16), sums, hots, copies), flops=8 * 10**9, moved=8 * 10**6,
        )
    below = from_behind(upper, "space", 1)
    with jax.named_scope("last_faces"):
        return call(functools.partial(last_kernel, nodes), shape((bands, nodes), F32), (following, face, below))


def gram_kernel(*refs):
    *blocks, terms_ref, gram_ref = refs
    bands, nodes = blocks[0].shape
    total = bands * len(blocks)
    me = lax.axis_index("band")
    terms_ref[:, nodes - nodes % 128 :] = jnp.zeros_like(terms_ref[:, nodes - nodes % 128 :])
    for distance, block in enumerate(blocks):
        source = pl.multiple_of(lax.rem(me - distance + len(blocks), len(blocks)) * bands, bands)
        upper, lower = halves(block[...])
        terms_ref[pl.ds(source, bands), :nodes] = upper
        terms_ref[pl.ds(total + source, bands), :nodes] = lower
    terms = terms_ref[...]
    both = lax.dot_general(terms, terms, (((1,), (1,)), ((), ())), preferred_element_type=F32)
    gram_ref[...] = both[:total, :total] + (both[:total, total:] + both[total:, :total]) + both[total:, total:]


def inverse_factor(matrix, block=4):
    size = matrix.shape[0]
    width = 2 * size
    lane = lax.broadcasted_iota(jnp.int32, (8, width), 1)
    row = lax.broadcasted_iota(jnp.int32, (8, width), 0)
    zero = jnp.zeros((size, size), F32)
    wide = jnp.concatenate([matrix, zero], axis=1)
    groups = [wide[8 * g : 8 * g + 8] + jnp.where(lane == row + (size + 8 * g), 1.0, 0.0) for g in range(size // 8)]
    for k in range(0, size, block):
        start = k // 8
        columns = [
            [jnp.broadcast_to(groups[g][:, k + q : k + q + 1], (8, width)) for g in range(start, size // 8)]
            for q in range(block)
        ]
        for q in range(block):
            at = k + q - 8 * start
            scale = 1.0 / columns[q][0][at : at + 1]
            column = [jnp.where(row > at, columns[q][0], 0.0)] + columns[q][1:]
            for p in range(q + 1, block):
                factor = columns[p][0][at : at + 1] * scale
                columns[p] = [value - weight * factor for value, weight in zip(columns[p], column)]
            factor = groups[start][at : at + 1] * scale
            for g, weight in enumerate(column):
                groups[start + g] = groups[start + g] - weight * factor
    out = []
    for g, rows in enumerate(groups):
        pivot = jnp.sum(jnp.where(lane == row + 8 * g, rows, 0.0), axis=1, keepdims=True)
        out.append(rows[:, size:] / jnp.sqrt(pivot))
    return jnp.concatenate(out, axis=0)


def ortho_kernel(nodes, count, gram_ref, terms_ref, out_ref, inverse_ref):
    bands = out_ref.shape[0]
    inverse_ref[...] = inverse_factor(gram_ref[...] / count)
    first = pl.multiple_of(lax.axis_index("band") * bands, bands)
    upper, lower = halves(inverse_ref[pl.ds(first, bands), :])
    rows = jnp.concatenate(
        [jnp.concatenate([upper, upper], axis=1), jnp.concatenate([lower, lower], axis=1)], axis=0
    )
    both = jnp.dot(rows, terms_ref[...], preferred_element_type=F32)
    out_ref[...] = (both[:bands] + both[bands:])[:, :nodes]


def space_sum(block):
    size = lax.axis_size("space")
    if size & (size - 1):
        return lax.psum(block, "space")
    step = 1
    while step < size:
        span = 2 if step == 1 or step * 2 == size else 4
        parts = [
            lax.ppermute(block, "space", [(i, i ^ (step * k)) for i in range(size)]) for k in range(1, span)
        ]
        block = sum(parts, block)
        step *= span
    return block


def per_device(psi, ham, conn, face_rows):
    bands, nodes = psi.shape
    following = filter_field(psi, ham, conn, face_rows)
    groups = lax.axis_size("band")
    total = groups * bands
    own = round_up(nodes, LANES)
    shape = jax.ShapeDtypeStruct
    blocks = [following] + [from_behind(following, "band", i) for i in range(1, groups)]
    with jax.named_scope("gram"):
        terms, gram = call(gram_kernel, (shape((2 * total, own), BF16), shape((total, total), F32)), blocks)
    with jax.named_scope("gram_sum"):
        gram = space_sum(gram)
    with jax.named_scope("orthonormal"):
        return call(
            functools.partial(ortho_kernel, nodes, nodes * lax.axis_size("space")),
            shape((bands, nodes), F32), (gram, terms), (pltpu.VMEM((total, total), F32),),
        )


def solution(mesh):
    placed = (P("band", "space"), P("space", None, None), P("space", None), P("space"))
    return jax.shard_map(
        per_device, mesh=mesh, in_specs=placed, out_specs=P("band", "space"), check_vma=False
    )
```

```python
import functools

import jax
import jax.numpy as jnp
from jax import lax
from jax.experimental import pallas as pl
from jax.experimental.pallas import tpu as pltpu
from jax.sharding import PartitionSpec as P

FACE_EL = 64
IN_EL = 448
STRIDE = 4
LANES = 256

CENTER = 6.25
HALF_WIDTH = 7.5

F32 = jnp.float32
BF16 = jnp.bfloat16
VMEM = pl.BlockSpec(memory_space=pltpu.VMEM)
HBM = pl.BlockSpec(memory_space=pltpu.HBM)
LIMIT = 40 * 1024 * 1024


def round_up(count, unit):
    return -(-count // unit) * unit


def one_hot(low):
    rows = lax.broadcasted_iota(jnp.int32, (LANES, low.shape[1]), 0)
    return jnp.where(rows == low, 1.0, 0.0).astype(BF16)


def stacked(field):
    blocks = field.shape[1] // LANES
    return jnp.concatenate([field[:, i * LANES : (i + 1) * LANES] for i in range(blocks)], axis=0)


def unstacked(rows, bands):
    blocks = rows.shape[0] // bands
    return jnp.concatenate([rows[i * bands : (i + 1) * bands] for i in range(blocks)], axis=1)


def pick(rows, high, low_hot, bands, first=0):
    table = jnp.dot(rows, low_hot, preferred_element_type=F32)
    out = jnp.zeros((bands, low_hot.shape[1]), F32)
    for i in range(rows.shape[0] // bands):
        out = jnp.where(high == i + first, table[i * bands : (i + 1) * bands], out)
    return out


def halves(values):
    upper = values.astype(BF16)
    return upper, (values - upper.astype(F32)).astype(BF16)


def spread(values, high, blocks, first=0):
    rows = []
    for part in halves(values):
        wide = part.astype(F32)
        for i in range(blocks):
            rows.append(jnp.where(high == i + first, wide, 0.0).astype(BF16))
    return jnp.concatenate(rows, axis=0)


def gathered_sum(rows, low_hot):
    both = lax.dot_general(rows, low_hot, (((1,), (1,)), ((), ())), preferred_element_type=F32)
    count = both.shape[0] // 2
    return both[:count] + both[count:]


def chunks(elements):
    return [range(e, min(e + STRIDE, elements)) for e in range(0, elements, STRIDE)]


def packed(ref, width, first, last):
    return jnp.concatenate([ref[e : e + 1, first:last] for e in range(width)], axis=1)


def face_kernel(psi_hbm, conn_hbm, face_hbm, values_ref, psi_out, conn_out, face_out, psi_ref, face_ref, sems):
    bands, nodes = psi_hbm.shape
    copies = [
        pltpu.make_async_copy(face_hbm, face_ref, sems.at[0]),
        pltpu.make_async_copy(psi_hbm, psi_ref, sems.at[1]),
        pltpu.make_async_copy(conn_hbm, conn_out, sems.at[2]),
    ]
    for copy in copies:
        copy.start()
    psi_out[...] = jnp.zeros_like(psi_out)
    face_out[...] = jnp.full_like(face_out, -1)
    copies[0].wait()
    face_out[:, : face_ref.shape[1]] = face_ref[...]
    face = face_out[...]
    hot = one_hot(face & 255)
    copies[1].wait()
    psi_out[:, :nodes] = psi_ref[...]
    values_ref[...] = pick(stacked(psi_out[...]).astype(BF16), face >> 8, hot, bands).astype(BF16)
    copies[2].wait()


def interior_kernel(nodes, psi_ref, conn_ref, ham_hbm, part_ref, ham_ref, slots_ref, ghosts_ref, hots_ref, hosts_ref, sems):
    bands = psi_ref.shape[0]
    elements, size = conn_ref.shape
    copies = [pltpu.make_async_copy(ham_hbm.at[e], ham_ref.at[e], sems.at[e]) for e in range(elements)]
    for copy in copies:
        copy.start()
    slots_ref[...] = packed(conn_ref, elements, 0, IN_EL)
    ghosts_ref[...] = packed(conn_ref, elements, IN_EL, size) - nodes
    hosts_ref[...] = one_hot(ghosts_ref[...] & 255)
    rows = stacked(psi_ref[...]).astype(BF16)
    for group in chunks(elements):
        span = slice(group[0] * IN_EL, (group[-1] + 1) * IN_EL)
        slots = slots_ref[:, span]
        hot = one_hot(slots & 255)
        hots_ref[:, span] = hot
        inside = pick(rows, slots >> 8, hot, bands).astype(BF16)
        for i, e in enumerate(group):
            copies[e].wait()
            part_ref[:, e * size : (e + 1) * size] = jnp.dot(
                inside[:, i * IN_EL : (i + 1) * IN_EL], ham_ref[e, :IN_EL, :], preferred_element_type=F32
            )


def widened(values):
    bands, count = values.shape
    return jnp.concatenate([values, jnp.zeros((bands, round_up(count, LANES) - count), values.dtype)], axis=1)


def first_kernel(
    psi_ref, slots_ref, ghosts_ref, hots_ref, hosts_ref, ham_ref, face_ref, ghost_ref, part_ref,
    own_ref, upper_ref, low_ref, sums,
):
    bands, own = psi_ref.shape
    elements, size = ham_ref.shape[:2]
    face_count = ghost_ref.shape[1]
    ghosts = ghosts_ref[...]
    outside = pick(stacked(widened(ghost_ref[...])), ghosts >> 8, hosts_ref[...], bands).astype(BF16)
    top = []
    for group in chunks(elements):
        inner = []
        for e in group:
            product = part_ref[:, e * size : (e + 1) * size] + jnp.dot(
                outside[:, e * FACE_EL : (e + 1) * FACE_EL], ham_ref[e, IN_EL:, :], preferred_element_type=F32
            )
            inner.append(product[:, :IN_EL])
            top.append(product[:, IN_EL:])
        span = slice(group[0] * IN_EL, (group[-1] + 1) * IN_EL)
        sums[:, span] = spread(jnp.concatenate(inner, axis=1), slots_ref[:, span] >> 8, own // LANES)
    rows = spread(jnp.concatenate(top, axis=1), ghosts >> 8, round_up(face_count, LANES) // LANES)
    upper_ref[...] = unstacked(gathered_sum(rows, hosts_ref[...]), bands)[:, :face_count] / HALF_WIDTH
    total = unstacked(gathered_sum(sums[...], hots_ref[...]), bands)
    current = (total - CENTER * psi_ref[...]) / HALF_WIDTH
    own_ref[...] = current
    face = face_ref[...]
    face_hot = one_hot(face & 255)
    terms = halves(stacked(current))
    low_ref[...] = pick(terms[0], face >> 8, face_hot, bands) + pick(terms[1], face >> 8, face_hot, bands)


def second_kernel(
    slots_ref, ghosts_ref, hots_ref, hosts_ref, ham_ref, face_ref, own_in, upper_in, below_in, above_in,
    own_ref, field_ref, upper_ref,
):
    bands, own = own_in.shape
    elements, size = ham_ref.shape[:2]
    face_count = upper_in.shape[1]
    face = face_ref[...]
    added = gathered_sum(spread(below_in[...], face >> 8, own // LANES), one_hot(face & 255))
    current = own_in[...] + unstacked(added, bands)
    own_ref[...] = current
    rows = stacked(current).astype(BF16)
    ghost = stacked(widened(upper_in[...] + above_in[...])).astype(BF16)
    ghosts = ghosts_ref[...]
    outside = pick(ghost, ghosts >> 8, hosts_ref[...], bands).astype(BF16)
    top = []
    for group in chunks(elements):
        span = slice(group[0] * IN_EL, (group[-1] + 1) * IN_EL)
        inside = pick(rows, slots_ref[:, span] >> 8, hots_ref[:, span], bands).astype(BF16)
        for i, e in enumerate(group):
            values = jnp.concatenate(
                [inside[:, i * IN_EL : (i + 1) * IN_EL], outside[:, e * FACE_EL : (e + 1) * FACE_EL]], axis=1
            )
            field_ref[:, e * size : (e + 1) * size] = values
            product = jnp.dot(values, ham_ref[e, :, size - 128 :], preferred_element_type=F32)
            top.append(product[:, 128 - FACE_EL :])
    sums = spread(jnp.concatenate(top, axis=1), ghosts >> 8, round_up(face_count, LANES) // LANES)
    upper_ref[...] = unstacked(gathered_sum(sums, hosts_ref[...]), bands)[:, :face_count] * (2.0 / HALF_WIDTH)


def third_kernel(psi_ref, slots_ref, hots_ref, ham_ref, own_in, field_ref, own_ref, sums):
    bands, own = own_in.shape
    elements, size = ham_ref.shape[:2]
    for group in chunks(elements):
        inner = []
        for e in group:
            product = jnp.dot(field_ref[:, e * size : (e + 1) * size], ham_ref[e], preferred_element_type=F32)
            inner.append(product[:, :IN_EL])
        span = slice(group[0] * IN_EL, (group[-1] + 1) * IN_EL)
        sums[:, span] = spread(jnp.concatenate(inner, axis=1), slots_ref[:, span] >> 8, own // LANES)
    total = unstacked(gathered_sum(sums[...], hots_ref[...]), bands)
    own_ref[...] = 2.0 * ((total - CENTER * own_in[...]) / HALF_WIDTH) - psi_ref[...]


def last_kernel(own_in, face_ref, below_in, out_ref, short_ref):
    bands, own = own_in.shape
    face = face_ref[...]
    added = gathered_sum(spread(below_in[...], face >> 8, own // LANES), one_hot(face & 255))
    total = own_in[...] + unstacked(added, bands)
    out_ref[...] = total
    short_ref[...] = total.astype(BF16)


def call(kernel, out_shape, inputs, scratch=(), flops=0, moved=0, far=()):
    return pl.pallas_call(
        kernel,
        out_shape=out_shape,
        in_specs=[HBM if i in far else VMEM for i in range(len(inputs))],
        out_specs=jax.tree.map(lambda _: VMEM, out_shape),
        scratch_shapes=list(scratch),
        compiler_params=pltpu.CompilerParams(vmem_limit_bytes=LIMIT),
        cost_estimate=pl.CostEstimate(flops=flops, bytes_accessed=moved, transcendentals=0),
    )(*inputs)


def from_behind(block, axis, distance):
    devices = range(lax.axis_size(axis))
    route = [((i - distance) % len(devices), i) for i in devices]
    return lax.ppermute(block, axis, route)


def filter_field(psi, ham, conn, face_rows):
    bands, nodes = psi.shape
    elements, size = conn.shape
    own = round_up(nodes, LANES)
    faces = round_up(face_rows.shape[0], 128)
    face_count = elements * (size - IN_EL)
    inner_count = elements * IN_EL
    shape = jax.ShapeDtypeStruct
    face_field = shape((bands, faces), F32)
    own_field = shape((bands, own), F32)
    sums = pltpu.VMEM((2 * own // LANES * bands, inner_count), BF16)

    with jax.named_scope("face_values"):
        values, wide, conn, face = call(
            face_kernel,
            (shape((bands, faces), BF16), own_field, shape(conn.shape, jnp.int32), shape((1, faces), jnp.int32)),
            (psi, conn, face_rows[None]),
            (pltpu.VMEM(psi.shape, F32), pltpu.VMEM((1, face_rows.shape[0]), jnp.int32), pltpu.SemaphoreType.DMA((3,))),
            far=(0, 1, 2),
        )
    ghost = from_behind(values, "space", -1)
    with jax.named_scope("interior"):
        part, near, slots, ghosts, hots, hosts = call(
            functools.partial(interior_kernel, nodes),
            (
                shape((bands, elements * size), F32), shape(ham.shape, BF16),
                shape((1, inner_count), jnp.int32), shape((1, face_count), jnp.int32),
                shape((LANES, inner_count), BF16), shape((LANES, face_count), BF16),
            ),
            (wide, conn, ham), (pltpu.SemaphoreType.DMA((elements,)),), flops=4 * 10**9, moved=8 * 10**6, far=(2,),
        )
    with jax.named_scope("first_step"):
        current, upper, low = call(
            first_kernel, (own_field, face_field, face_field),
            (wide, slots, ghosts, hots, hosts, near, face, ghost, part), (sums,), flops=4 * 10**9, moved=10**6,
        )
    below = from_behind(upper, "space", 1)
    above = from_behind(low, "space", -1)
    with jax.named_scope("second_step"):
        current, field, upper = call(
            second_kernel, (own_field, shape((bands, elements * size), BF16), face_field),
            (slots, ghosts, hots, hosts, near, face, current, upper, below, above), flops=4 * 10**9, moved=10**6,
        )
    below = from_behind(upper, "space", 1)
    with jax.named_scope("second_sums"):
        following = call(
            third_kernel, own_field, (wide, slots, hots, near, current, field), (sums,), flops=4 * 10**9, moved=8 * 10**6
        )
    with jax.named_scope("last_faces"):
        return call(last_kernel, (own_field, shape(own_field.shape, BF16)), (following, face, below))


def gram_kernel(*refs):
    *blocks, terms_ref, gram_ref = refs
    bands = blocks[0].shape[0]
    total = bands * len(blocks)
    me = lax.axis_index("band")
    for distance, block in enumerate(blocks):
        source = pl.multiple_of(lax.rem(me - distance + len(blocks), len(blocks)) * bands, bands)
        upper, lower = halves(block[...].astype(F32))
        terms_ref[pl.ds(source, bands), :] = upper
        terms_ref[pl.ds(total + source, bands), :] = lower
    terms = terms_ref[...]
    both = lax.dot_general(terms, terms, (((1,), (1,)), ((), ())), preferred_element_type=F32)
    gram_ref[...] = both[:total, :total] + (both[:total, total:] + both[total:, :total]) + both[total:, total:]


def inverse_factor(matrix, block=8):
    size = matrix.shape[0]
    width = 2 * size
    lane = lax.broadcasted_iota(jnp.int32, (8, width), 1)
    row = lax.broadcasted_iota(jnp.int32, (8, width), 0)
    zero = jnp.zeros((size, size), F32)
    wide = jnp.concatenate([matrix, zero], axis=1)
    groups = [wide[8 * g : 8 * g + 8] + jnp.where(lane == row + (size + 8 * g), 1.0, 0.0) for g in range(size // 8)]
    for k in range(0, size, block):
        start = k // 8
        columns = [
            [jnp.broadcast_to(groups[g][:, k + q : k + q + 1], (8, width)) for g in range(start, size // 8)]
            for q in range(block)
        ]
        for q in range(block):
            at = k + q - 8 * start
            scale = 1.0 / columns[q][0][at : at + 1]
            column = [jnp.where(row > at, columns[q][0], 0.0)] + columns[q][1:]
            for p in range(q + 1, block):
                factor = columns[p][0][at : at + 1] * scale
                columns[p] = [value - weight * factor for value, weight in zip(columns[p], column)]
            factor = groups[start][at : at + 1] * scale
            for g, weight in enumerate(column):
                groups[start + g] = groups[start + g] - weight * factor
    out = []
    for g, rows in enumerate(groups):
        pivot = jnp.sum(jnp.where(lane == row + 8 * g, rows, 0.0), axis=1, keepdims=True)
        out.append(rows[:, size:] / jnp.sqrt(pivot))
    return jnp.concatenate(out, axis=0)


def ortho_kernel(nodes, count, gram_ref, terms_ref, out_ref, inverse_ref):
    bands = out_ref.shape[0]
    inverse_ref[...] = inverse_factor(gram_ref[...] / count)
    first = pl.multiple_of(lax.axis_index("band") * bands, bands)
    upper, lower = halves(inverse_ref[pl.ds(first, bands), :])
    rows = jnp.concatenate(
        [jnp.concatenate([upper, upper], axis=1), jnp.concatenate([lower, lower], axis=1)], axis=0
    )
    both = jnp.dot(rows, terms_ref[...], preferred_element_type=F32)
    out_ref[...] = (both[:bands] + both[bands:])[:, :nodes]


def space_sum(block):
    size = lax.axis_size("space")
    if size & (size - 1):
        return lax.psum(block, "space")
    step = 1
    while step < size:
        span = 2 if step == 1 or step * 2 == size else 4
        parts = [
            lax.ppermute(block, "space", [(i, i ^ (step * k)) for i in range(size)]) for k in range(1, span)
        ]
        block = sum(parts, block)
        step *= span
    return block


def per_device(psi, ham, conn, face_rows):
    bands, nodes = psi.shape
    following, short = filter_field(psi, ham, conn, face_rows)
    groups = lax.axis_size("band")
    total = groups * bands
    own = round_up(nodes, LANES)
    shape = jax.ShapeDtypeStruct
    blocks = [following] + [from_behind(short, "band", i) for i in range(1, groups)]
    with jax.named_scope("gram"):
        terms, gram = call(gram_kernel, (shape((2 * total, own), BF16), shape((total, total), F32)), blocks)
    with jax.named_scope("gram_sum"):
        gram = space_sum(gram)
    with jax.named_scope("orthonormal"):
        return call(
            functools.partial(ortho_kernel, nodes, nodes * lax.axis_size("space")),
            shape((bands, nodes), F32), (gram, terms), (pltpu.VMEM((total, total), F32),),
        )


def solution(mesh):
    placed = (P("band", "space"), P("space", None, None), P("space", None), P("space"))
    return jax.shard_map(
        per_device, mesh=mesh, in_specs=placed, out_specs=P("band", "space"), check_vma=False
    )
```

```python
import functools

import jax
import jax.numpy as jnp
from jax import lax
from jax.experimental import pallas as pl
from jax.experimental.pallas import tpu as pltpu
from jax.sharding import PartitionSpec as P

FACE_EL = 64
IN_EL = 448
LANES = 256

CENTER = 6.25
HALF_WIDTH = 7.5

F32 = jnp.float32
BF16 = jnp.bfloat16
VMEM = pl.BlockSpec(memory_space=pltpu.VMEM)
HBM = pl.BlockSpec(memory_space=pltpu.HBM)
LIMIT = 40 * 1024 * 1024


def round_up(count, unit):
    return -(-count // unit) * unit


def one_hot(low):
    rows = lax.broadcasted_iota(jnp.int32, (LANES, low.shape[1]), 0)
    return jnp.where(rows == low, 1.0, 0.0).astype(BF16)


def stacked(field):
    blocks = field.shape[1] // LANES
    return jnp.concatenate([field[:, i * LANES : (i + 1) * LANES] for i in range(blocks)], axis=0)


def unstacked(rows, bands):
    blocks = rows.shape[0] // bands
    return jnp.concatenate([rows[i * bands : (i + 1) * bands] for i in range(blocks)], axis=1)


def pick(rows, high, low_hot, bands, first=0):
    table = jnp.dot(rows, low_hot, preferred_element_type=F32)
    out = jnp.zeros((bands, low_hot.shape[1]), F32)
    for i in range(rows.shape[0] // bands):
        out = jnp.where(high == i + first, table[i * bands : (i + 1) * bands], out)
    return out


def halves(values):
    upper = values.astype(BF16)
    return upper, (values - upper.astype(F32)).astype(BF16)


def spread(values, high, blocks, first=0):
    rows = []
    for part in halves(values):
        wide = part.astype(F32)
        for i in range(blocks):
            rows.append(jnp.where(high == i + first, wide, 0.0).astype(BF16))
    return jnp.concatenate(rows, axis=0)


def gathered_sum(rows, low_hot):
    both = lax.dot_general(rows, low_hot, (((1,), (1,)), ((), ())), preferred_element_type=F32)
    count = both.shape[0] // 2
    return both[:count] + both[count:]


def tiles(count, width=LANES):
    return [slice(start, min(start + width, count)) for start in range(0, count, width)]


def hot_into(hots_ref, low):
    for tile in tiles(low.shape[1]):
        hots_ref[:, tile] = one_hot(low[:, tile])


def pick_into(out_ref, rows, high, hots_ref):
    for tile in tiles(high.shape[1]):
        out_ref[:, tile] = pick(rows, high[:, tile], hots_ref[:, tile], out_ref.shape[0]).astype(out_ref.dtype)


def spread_into(sums_ref, values_ref, high):
    bands = values_ref.shape[0]
    blocks = sums_ref.shape[0] // (2 * bands)
    for tile in tiles(high.shape[1]):
        at = high[:, tile]
        upper, lower = (part.astype(F32) for part in halves(values_ref[:, tile]))
        for i in range(blocks):
            here = at == i
            sums_ref[i * bands : (i + 1) * bands, tile] = jnp.where(here, upper, 0.0).astype(BF16)
            sums_ref[(blocks + i) * bands : (blocks + i + 1) * bands, tile] = jnp.where(here, lower, 0.0).astype(BF16)


def split_products(products, inner_ref, top_ref, first):
    inner = jnp.concatenate([product[:, :IN_EL] for product in products], axis=1)
    top = jnp.concatenate([product[:, IN_EL:] for product in products], axis=1)
    inner_ref[:, first * IN_EL : first * IN_EL + inner.shape[1]] = inner
    if top_ref is not None:
        top_ref[:, first * FACE_EL : first * FACE_EL + top.shape[1]] = top


def pairs(elements):
    return [range(e, min(e + 2, elements)) for e in range(0, elements, 2)]


def packed(ref, width, first, last):
    return jnp.concatenate([ref[e : e + 1, first:last] for e in range(width)], axis=1)


def face_kernel(psi_hbm, conn_hbm, face_hbm, values_ref, psi_out, conn_out, face_out, psi_ref, face_ref, sems):
    bands, nodes = psi_hbm.shape
    copies = [
        pltpu.make_async_copy(face_hbm, face_ref, sems.at[0]),
        pltpu.make_async_copy(psi_hbm, psi_ref, sems.at[1]),
        pltpu.make_async_copy(conn_hbm, conn_out, sems.at[2]),
    ]
    for copy in copies:
        copy.start()
    psi_out[...] = jnp.zeros_like(psi_out)
    face_out[...] = jnp.full_like(face_out, -1)
    copies[0].wait()
    face_out[:, : face_ref.shape[0]] = face_ref[...].reshape(1, face_ref.shape[0])
    face = face_out[...]
    hot = one_hot(face & 255)
    copies[1].wait()
    psi_out[:, :nodes] = psi_ref[...]
    values_ref[...] = pick(stacked(psi_out[...]).astype(BF16), face >> 8, hot, bands).astype(BF16)
    copies[2].wait()


def interior_kernel(
    nodes, psi_ref, conn_ref, ham_hbm, part_ref, ham_ref, slots_ref, ghosts_ref, hots_ref, hosts_ref, inside_ref, sems
):
    elements, size = conn_ref.shape
    copies = [pltpu.make_async_copy(ham_hbm.at[e], ham_ref.at[e], sems.at[e]) for e in range(elements)]
    for copy in copies:
        copy.start()
    slots_ref[...] = packed(conn_ref, elements, 0, IN_EL)
    ghosts_ref[...] = packed(conn_ref, elements, IN_EL, size) - nodes
    hot_into(hosts_ref, ghosts_ref[...] & 255)
    slots = slots_ref[...]
    hot_into(hots_ref, slots & 255)
    pick_into(inside_ref, stacked(psi_ref[...]).astype(BF16), slots >> 8, hots_ref)
    for e in range(elements):
        copies[e].wait()
        part_ref[:, e * size : (e + 1) * size] = jnp.dot(
            inside_ref[:, e * IN_EL : (e + 1) * IN_EL], ham_ref[e, :IN_EL, :], preferred_element_type=F32
        )


def widened(values):
    bands, count = values.shape
    if count % LANES == 0:
        return values
    return jnp.concatenate([values, jnp.zeros((bands, round_up(count, LANES) - count), values.dtype)], axis=1)


def first_kernel(
    psi_ref, slots_ref, ghosts_ref, hots_ref, hosts_ref, ham_ref, face_ref, ghost_ref, part_ref,
    own_ref, upper_ref, low_ref, sums, top_sums, inner, top, outside,
):
    bands, own = psi_ref.shape
    elements, size = ham_ref.shape[:2]
    face_count = ghost_ref.shape[1]
    ghosts = ghosts_ref[...]
    pick_into(outside, stacked(widened(ghost_ref[...])), ghosts >> 8, hosts_ref)
    for pair in pairs(elements):
        products = [
            part_ref[:, e * size : (e + 1) * size]
            + jnp.dot(outside[:, e * FACE_EL : (e + 1) * FACE_EL], ham_ref[e, IN_EL:, :], preferred_element_type=F32)
            for e in pair
        ]
        split_products(products, inner, top, pair[0])
    spread_into(sums, inner, slots_ref[...] >> 8)
    spread_into(top_sums, top, ghosts >> 8)
    upper_ref[...] = unstacked(gathered_sum(top_sums[...], hosts_ref[...]), bands)[:, :face_count] / HALF_WIDTH
    total = unstacked(gathered_sum(sums[...], hots_ref[...]), bands)
    current = (total - CENTER * psi_ref[...]) / HALF_WIDTH
    own_ref[...] = current
    face = face_ref[...]
    face_hot = one_hot(face & 255)
    terms = halves(stacked(current))
    low_ref[...] = pick(terms[0], face >> 8, face_hot, bands) + pick(terms[1], face >> 8, face_hot, bands)


def far_kernel(own_in, slots_ref, hots_ref, face_ref, inside_ref, high_ref, faces_ref):
    bands, own = own_in.shape
    blocks = round_up(own // LANES, 16)
    face = face_ref[...]
    number = lax.broadcasted_iota(jnp.int32, (blocks, face.shape[1]), 1)
    held = lax.broadcasted_iota(jnp.int32, number.shape, 0) == (face >> 8)
    digits = [jnp.where(held, digit, 0).astype(F32).astype(BF16) for digit in ((number >> 8) + 1, number & 255)]
    table = lax.dot_general(
        jnp.concatenate(digits, axis=0), one_hot(face & 255), (((1,), (1,)), ((), ())), preferred_element_type=F32
    ).astype(BF16)
    rows = stacked(own_in[...]).astype(BF16)
    for tile in tiles(slots_ref.shape[1]):
        high = slots_ref[:, tile] >> 8
        hot = hots_ref[:, tile]
        both = jnp.dot(table, hot, preferred_element_type=F32)
        held = lax.broadcasted_iota(jnp.int32, (blocks, both.shape[1]), 0) == high
        block = jnp.sum(jnp.where(held, both[:blocks], 0.0), axis=0, keepdims=True).astype(jnp.int32)
        lane = jnp.sum(jnp.where(held, both[blocks:], 0.0), axis=0, keepdims=True).astype(jnp.int32)
        high_ref[:, tile] = block - 1
        faces_ref[:, tile] = one_hot(jnp.where(block > 0, lane, -1))
        inside_ref[:, tile] = jnp.where(block > 0, 0.0, pick(rows, high, hot, bands)).astype(BF16)


def second_kernel(
    inside_ref, high_ref, faces_ref, ghosts_ref, hosts_ref, ham_ref, low_in, upper_in, below_in, above_in,
    field_ref, upper_ref, top_sums, inside, top, outside,
):
    bands, face_count = upper_in.shape
    elements, size = ham_ref.shape[:2]
    faces = stacked(widened(low_in[...] + below_in[...])).astype(BF16)
    ghost = stacked(widened(upper_in[...] + above_in[...])).astype(BF16)
    ghosts = ghosts_ref[...]
    pick_into(outside, ghost, ghosts >> 8, hosts_ref)
    for tile in tiles(high_ref.shape[1]):
        extra = pick(faces, high_ref[:, tile], faces_ref[:, tile], bands)
        inside[:, tile] = inside_ref[:, tile] + extra.astype(BF16)
    for pair in pairs(elements):
        products = []
        for e in pair:
            values = jnp.concatenate(
                [inside[:, e * IN_EL : (e + 1) * IN_EL], outside[:, e * FACE_EL : (e + 1) * FACE_EL]], axis=1
            )
            field_ref[:, e * size : (e + 1) * size] = values
            product = jnp.dot(values, ham_ref[e, :, size - 128 :], preferred_element_type=F32)
            products.append(product[:, 128 - FACE_EL :])
        top[:, pair[0] * FACE_EL : (pair[-1] + 1) * FACE_EL] = jnp.concatenate(products, axis=1)
    spread_into(top_sums, top, ghosts >> 8)
    total = unstacked(gathered_sum(top_sums[...], hosts_ref[...]), bands)
    upper_ref[...] = total[:, :face_count] * (2.0 / HALF_WIDTH)


def third_kernel(psi_ref, slots_ref, hots_ref, ham_ref, face_ref, own_in, below_in, field_ref, own_ref, sums, inner):
    bands, own = own_in.shape
    elements, size = ham_ref.shape[:2]
    face = face_ref[...]
    added = gathered_sum(spread(below_in[...], face >> 8, own // LANES), one_hot(face & 255))
    for pair in pairs(elements):
        products = [
            jnp.dot(field_ref[:, e * size : (e + 1) * size], ham_ref[e], preferred_element_type=F32) for e in pair
        ]
        split_products(products, inner, None, pair[0])
    spread_into(sums, inner, slots_ref[...] >> 8)
    total = unstacked(gathered_sum(sums[...], hots_ref[...]), bands)
    current = own_in[...] + unstacked(added, bands)
    own_ref[...] = 2.0 * ((total - CENTER * current) / HALF_WIDTH) - psi_ref[...]


def last_kernel(own_in, face_ref, below_in, out_ref, short_ref):
    bands, own = own_in.shape
    face = face_ref[...]
    added = gathered_sum(spread(below_in[...], face >> 8, own // LANES), one_hot(face & 255))
    total = own_in[...] + unstacked(added, bands)
    out_ref[...] = total
    short_ref[...] = total[:, : short_ref.shape[1]].astype(BF16)


def call(kernel, out_shape, inputs, scratch=(), flops=0, moved=0, far=()):
    return pl.pallas_call(
        kernel,
        out_shape=out_shape,
        in_specs=[HBM if i in far else VMEM for i in range(len(inputs))],
        out_specs=jax.tree.map(lambda _: VMEM, out_shape),
        scratch_shapes=list(scratch),
        compiler_params=pltpu.CompilerParams(vmem_limit_bytes=LIMIT),
        cost_estimate=pl.CostEstimate(flops=flops, bytes_accessed=moved, transcendentals=0),
    )(*inputs)


def from_behind(block, axis, distance):
    devices = range(lax.axis_size(axis))
    route = [((i - distance) % len(devices), i) for i in devices]
    return lax.ppermute(block, axis, route)


def filter_field(psi, ham, conn, face_rows):
    bands, nodes = psi.shape
    elements, size = conn.shape
    own = round_up(nodes, LANES)
    faces = round_up(face_rows.shape[0], 128)
    trimmed = round_up(nodes, 128)
    face_count = elements * (size - IN_EL)
    inner_count = elements * IN_EL
    shape = jax.ShapeDtypeStruct
    face_field = shape((bands, faces), F32)
    own_field = shape((bands, own), F32)
    sums = pltpu.VMEM((2 * own // LANES * bands, inner_count), BF16)
    top_sums = pltpu.VMEM((2 * round_up(faces, LANES) // LANES * bands, face_count), BF16)
    inner = pltpu.VMEM((bands, inner_count), F32)
    top = pltpu.VMEM((bands, face_count), F32)
    inside_field = pltpu.VMEM((bands, inner_count), BF16)
    outside = pltpu.VMEM((bands, face_count), BF16)

    with jax.named_scope("face_values"):
        values, wide, conn, face = call(
            face_kernel,
            (shape((bands, faces), BF16), own_field, shape(conn.shape, jnp.int32), shape((1, faces), jnp.int32)),
            [pltpu.with_memory_space_constraint(array, pltpu.HBM) for array in (psi, conn, face_rows)],
            (pltpu.VMEM(psi.shape, F32), pltpu.VMEM(face_rows.shape, jnp.int32), pltpu.SemaphoreType.DMA((3,))),
            far=(0, 1, 2),
        )
    ghost = from_behind(values, "space", -1)
    with jax.named_scope("interior"):
        part, near, slots, ghosts, hots, hosts = call(
            functools.partial(interior_kernel, nodes),
            (
                shape((bands, elements * size), F32), shape(ham.shape, BF16),
                shape((1, inner_count), jnp.int32), shape((1, face_count), jnp.int32),
                shape((LANES, inner_count), BF16), shape((LANES, face_count), BF16),
            ),
            (wide, conn, ham), (inside_field, pltpu.SemaphoreType.DMA((elements,))), flops=4 * 10**9, moved=8 * 10**6, far=(2,),
        )
    with jax.named_scope("first_step"):
        current, upper, low = call(
            first_kernel, (own_field, face_field, face_field),
            (wide, slots, ghosts, hots, hosts, near, face, ghost, part), (sums, top_sums, inner, top, outside),
            flops=4 * 10**9, moved=10**6,
        )
    below = from_behind(upper, "space", 1)
    above = from_behind(low, "space", -1)
    with jax.named_scope("off_face"):
        inside, high, faces = call(
            far_kernel,
            (shape((bands, inner_count), BF16), shape((1, inner_count), jnp.int32), shape((LANES, inner_count), BF16)),
            (current, slots, hots, face), flops=4 * 10**9, moved=10**6,
        )
    with jax.named_scope("second_step"):
        field, upper = call(
            second_kernel, (shape((bands, elements * size), BF16), face_field),
            (inside, high, faces, ghosts, hosts, near, low, upper, below, above), (top_sums, inside_field, top, outside),
            flops=4 * 10**9, moved=10**6,
        )
    from_below = from_behind(upper, "space", 1)
    with jax.named_scope("second_sums"):
        following = call(
            third_kernel, own_field, (wide, slots, hots, near, face, current, below, field), (sums, inner),
            flops=4 * 10**9, moved=8 * 10**6,
        )
    with jax.named_scope("last_faces"):
        return call(last_kernel, (own_field, shape((bands, trimmed), BF16)), (following, face, from_below))


def gram_kernel(*refs):
    *blocks, terms_ref, gram_ref = refs
    bands = blocks[0].shape[0]
    total = bands * len(blocks)
    me = lax.axis_index("band")
    for distance, block in enumerate(blocks):
        source = pl.multiple_of(lax.rem(me - distance + len(blocks), len(blocks)) * bands, bands)
        upper, lower = halves(widened(block[...].astype(F32)))
        terms_ref[pl.ds(source, bands), :] = upper
        terms_ref[pl.ds(total + source, bands), :] = lower
    terms = terms_ref[...]
    both = lax.dot_general(terms, terms, (((1,), (1,)), ((), ())), preferred_element_type=F32)
    gram_ref[...] = both[:total, :total] + (both[:total, total:] + both[total:, :total]) + both[total:, total:]


def inverse_factor(matrix, block=8):
    size = matrix.shape[0]
    width = 2 * size
    lane = lax.broadcasted_iota(jnp.int32, (8, width), 1)
    row = lax.broadcasted_iota(jnp.int32, (8, width), 0)
    zero = jnp.zeros((size, size), F32)
    wide = jnp.concatenate([matrix, zero], axis=1)
    groups = [wide[8 * g : 8 * g + 8] + jnp.where(lane == row + (size + 8 * g), 1.0, 0.0) for g in range(size // 8)]
    for k in range(0, size, block):
        start = k // 8
        columns = [
            [jnp.broadcast_to(groups[g][:, k + q : k + q + 1], (8, width)) for g in range(start, size // 8)]
            for q in range(block)
        ]
        for q in range(block):
            at = k + q - 8 * start
            scale = 1.0 / columns[q][0][at : at + 1]
            column = [jnp.where(row > at, columns[q][0], 0.0)] + columns[q][1:]
            for p in range(q + 1, block):
                factor = columns[p][0][at : at + 1] * scale
                columns[p] = [value - weight * factor for value, weight in zip(columns[p], column)]
            factor = groups[start][at : at + 1] * scale
            for g, weight in enumerate(column):
                groups[start + g] = groups[start + g] - weight * factor
    out = []
    for g, rows in enumerate(groups):
        pivot = jnp.sum(jnp.where(lane == row + 8 * g, rows, 0.0), axis=1, keepdims=True)
        out.append(rows[:, size:] / jnp.sqrt(pivot))
    return jnp.concatenate(out, axis=0)


def ortho_kernel(nodes, count, gram_ref, terms_ref, out_ref, inverse_ref):
    bands = out_ref.shape[0]
    inverse_ref[...] = inverse_factor(gram_ref[...] / count)
    first = pl.multiple_of(lax.axis_index("band") * bands, bands)
    upper, lower = halves(inverse_ref[pl.ds(first, bands), :])
    rows = jnp.concatenate(
        [jnp.concatenate([upper, upper], axis=1), jnp.concatenate([lower, lower], axis=1)], axis=0
    )
    both = jnp.dot(rows, terms_ref[...], preferred_element_type=F32)
    out_ref[...] = (both[:bands] + both[bands:])[:, :nodes]


def space_sum(block):
    size = lax.axis_size("space")
    if size & (size - 1):
        return lax.psum(block, "space")
    step = 1
    while step < size:
        span = 2 if step == 1 or step * 2 == size else 4
        parts = [
            lax.ppermute(block, "space", [(i, i ^ (step * k)) for i in range(size)]) for k in range(1, span)
        ]
        block = sum(parts, block)
        step *= span
    return block


def per_device(psi, ham, conn, face_rows):
    bands, nodes = psi.shape
    following, short = filter_field(psi, ham, conn, face_rows)
    groups = lax.axis_size("band")
    total = groups * bands
    own = round_up(nodes, LANES)
    shape = jax.ShapeDtypeStruct
    blocks = [following] + [from_behind(short, "band", i) for i in range(1, groups)]
    with jax.named_scope("gram"):
        terms, gram = call(gram_kernel, (shape((2 * total, own), BF16), shape((total, total), F32)), blocks)
    with jax.named_scope("gram_sum"):
        gram = space_sum(gram)
    with jax.named_scope("orthonormal"):
        return call(
            functools.partial(ortho_kernel, nodes, nodes * lax.axis_size("space")),
            shape((bands, nodes), F32), (gram, terms), (pltpu.VMEM((total, total), F32),),
        )


def solution(mesh):
    placed = (P("band", "space"), P("space", None, None), P("space", None), P("space"))
    return jax.shard_map(
        per_device, mesh=mesh, in_specs=placed, out_specs=P("band", "space"), check_vma=False
    )
```

```python
import functools

import jax
import jax.numpy as jnp
from jax import lax
from jax.experimental import pallas as pl
from jax.experimental.pallas import tpu as pltpu
from jax.sharding import PartitionSpec as P

FACE_EL = 64
IN_EL = 448
LANES = 256

CENTER = 6.25
HALF_WIDTH = 7.5

F32 = jnp.float32
BF16 = jnp.bfloat16
VMEM = pl.BlockSpec(memory_space=pltpu.VMEM)
HBM = pl.BlockSpec(memory_space=pltpu.HBM)
LIMIT = 40 * 1024 * 1024


def round_up(count, unit):
    return -(-count // unit) * unit


def one_hot(low):
    rows = lax.broadcasted_iota(jnp.int32, (LANES, low.shape[1]), 0)
    return jnp.where(rows == low, 1.0, 0.0).astype(BF16)


def stacked(field):
    blocks = field.shape[1] // LANES
    return jnp.concatenate([field[:, i * LANES : (i + 1) * LANES] for i in range(blocks)], axis=0)


def unstacked(rows, bands):
    blocks = rows.shape[0] // bands
    return jnp.concatenate([rows[i * bands : (i + 1) * bands] for i in range(blocks)], axis=1)


def pick(rows, high, low_hot, bands, first=0):
    table = jnp.dot(rows, low_hot, preferred_element_type=F32)
    out = jnp.zeros((bands, low_hot.shape[1]), F32)
    for i in range(rows.shape[0] // bands):
        out = jnp.where(high == i + first, table[i * bands : (i + 1) * bands], out)
    return out


def halves(values):
    upper = values.astype(BF16)
    return upper, (values - upper.astype(F32)).astype(BF16)


def spread(values, high, blocks, first=0):
    rows = []
    for part in halves(values):
        wide = part.astype(F32)
        for i in range(blocks):
            rows.append(jnp.where(high == i + first, wide, 0.0).astype(BF16))
    return jnp.concatenate(rows, axis=0)


def gathered_sum(rows, low_hot):
    both = lax.dot_general(rows, low_hot, (((1,), (1,)), ((), ())), preferred_element_type=F32)
    count = both.shape[0] // 2
    return both[:count] + both[count:]


def tiles(count, width=LANES):
    return [slice(start, min(start + width, count)) for start in range(0, count, width)]


def hot_into(hots_ref, low):
    for tile in tiles(low.shape[1]):
        hots_ref[:, tile] = one_hot(low[:, tile])


def pick_into(out_ref, rows, high, hots_ref):
    for tile in tiles(high.shape[1]):
        out_ref[:, tile] = pick(rows, high[:, tile], hots_ref[:, tile], out_ref.shape[0]).astype(out_ref.dtype)


def spread_into(sums_ref, values_ref, high):
    bands = values_ref.shape[0]
    blocks = sums_ref.shape[0] // (2 * bands)
    for tile in tiles(high.shape[1]):
        at = high[:, tile]
        upper, lower = (part.astype(F32) for part in halves(values_ref[:, tile]))
        for i in range(blocks):
            here = at == i
            sums_ref[i * bands : (i + 1) * bands, tile] = jnp.where(here, upper, 0.0).astype(BF16)
            sums_ref[(blocks + i) * bands : (blocks + i + 1) * bands, tile] = jnp.where(here, lower, 0.0).astype(BF16)


def split_products(products, inner_ref, top_ref, first):
    inner = jnp.concatenate([product[:, :IN_EL] for product in products], axis=1)
    top = jnp.concatenate([product[:, IN_EL:] for product in products], axis=1)
    inner_ref[:, first * IN_EL : first * IN_EL + inner.shape[1]] = inner
    if top_ref is not None:
        top_ref[:, first * FACE_EL : first * FACE_EL + top.shape[1]] = top


def pairs(elements):
    return [range(e, min(e + 2, elements)) for e in range(0, elements, 2)]


def packed(ref, width, first, last):
    return jnp.concatenate([ref[e : e + 1, first:last] for e in range(width)], axis=1)


def face_kernel(psi_hbm, conn_hbm, face_hbm, values_ref, psi_out, conn_out, face_out, psi_ref, face_ref, sems):
    bands, nodes = psi_hbm.shape
    copies = [
        pltpu.make_async_copy(face_hbm, face_ref, sems.at[0]),
        pltpu.make_async_copy(psi_hbm, psi_ref, sems.at[1]),
        pltpu.make_async_copy(conn_hbm, conn_out, sems.at[2]),
    ]
    for copy in copies:
        copy.start()
    psi_out[...] = jnp.zeros_like(psi_out)
    face_out[...] = jnp.full_like(face_out, -1)
    copies[0].wait()
    face_out[:, : face_ref.shape[0]] = face_ref[...].reshape(1, face_ref.shape[0])
    face = face_out[...]
    hot = one_hot(face & 255)
    copies[1].wait()
    psi_out[:, :nodes] = psi_ref[...]
    values_ref[...] = pick(stacked(psi_out[...]).astype(BF16), face >> 8, hot, bands).astype(BF16)
    copies[2].wait()


def interior_kernel(
    nodes, psi_ref, conn_ref, ham_ref, part_ref, slots_ref, ghosts_ref, hots_ref, hosts_ref, inside_ref
):
    elements, size = conn_ref.shape
    slots_ref[...] = packed(conn_ref, elements, 0, IN_EL)
    ghosts_ref[...] = packed(conn_ref, elements, IN_EL, size) - nodes
    hot_into(hosts_ref, ghosts_ref[...] & 255)
    slots = slots_ref[...]
    hot_into(hots_ref, slots & 255)
    pick_into(inside_ref, stacked(psi_ref[...]).astype(BF16), slots >> 8, hots_ref)
    for e in range(elements):
        part_ref[:, e * size : (e + 1) * size] = jnp.dot(
            inside_ref[:, e * IN_EL : (e + 1) * IN_EL], ham_ref[e, :IN_EL, :], preferred_element_type=F32
        )


def widened(values):
    bands, count = values.shape
    if count % LANES == 0:
        return values
    return jnp.concatenate([values, jnp.zeros((bands, round_up(count, LANES) - count), values.dtype)], axis=1)


def odd_domain():
    return lax.rem(lax.axis_index("space"), 2) == 1


def first_kernel(
    psi_ref, slots_ref, ghosts_ref, hots_ref, hosts_ref, ham_ref, face_ref, ghost_ref, part_ref,
    own_ref, upper_ref, low_ref, near_ref, far_ref, sums, top_sums, inner, top, outside,
):
    bands, own = psi_ref.shape
    elements, size = ham_ref.shape[:2]
    face_count = ghost_ref.shape[1]
    ghosts = ghosts_ref[...]
    pick_into(outside, stacked(widened(ghost_ref[...])), ghosts >> 8, hosts_ref)
    for pair in pairs(elements):
        products = [
            part_ref[:, e * size : (e + 1) * size]
            + jnp.dot(outside[:, e * FACE_EL : (e + 1) * FACE_EL], ham_ref[e, IN_EL:, :], preferred_element_type=F32)
            for e in pair
        ]
        split_products(products, inner, top, pair[0])
    spread_into(sums, inner, slots_ref[...] >> 8)
    spread_into(top_sums, top, ghosts >> 8)
    upper = unstacked(gathered_sum(top_sums[...], hosts_ref[...]), bands)[:, :face_count] / HALF_WIDTH
    upper_ref[...] = upper
    total = unstacked(gathered_sum(sums[...], hots_ref[...]), bands)
    current = (total - CENTER * psi_ref[...]) / HALF_WIDTH
    own_ref[...] = current
    face = face_ref[...]
    face_hot = one_hot(face & 255)
    terms = halves(stacked(current))
    low = pick(terms[0], face >> 8, face_hot, bands) + pick(terms[1], face >> 8, face_hot, bands)
    low_ref[...] = low
    odd = odd_domain()
    near_ref[...] = jnp.where(odd, low, upper)
    far_ref[...] = jnp.where(odd, upper, low)


def far_kernel(own_in, slots_ref, hots_ref, face_ref, inside_ref, high_ref, faces_ref):
    bands, own = own_in.shape
    blocks = round_up(own // LANES, 16)
    face = face_ref[...]
    number = lax.broadcasted_iota(jnp.int32, (blocks, face.shape[1]), 1)
    held = lax.broadcasted_iota(jnp.int32, number.shape, 0) == (face >> 8)
    digits = [jnp.where(held, digit, 0).astype(F32).astype(BF16) for digit in ((number >> 8) + 1, number & 255)]
    table = lax.dot_general(
        jnp.concatenate(digits, axis=0), one_hot(face & 255), (((1,), (1,)), ((), ())), preferred_element_type=F32
    ).astype(BF16)
    rows = stacked(own_in[...]).astype(BF16)
    for tile in tiles(slots_ref.shape[1]):
        high = slots_ref[:, tile] >> 8
        hot = hots_ref[:, tile]
        both = jnp.dot(table, hot, preferred_element_type=F32)
        held = lax.broadcasted_iota(jnp.int32, (blocks, both.shape[1]), 0) == high
        block = jnp.sum(jnp.where(held, both[:blocks], 0.0), axis=0, keepdims=True).astype(jnp.int32)
        lane = jnp.sum(jnp.where(held, both[blocks:], 0.0), axis=0, keepdims=True).astype(jnp.int32)
        high_ref[:, tile] = block - 1
        faces_ref[:, tile] = one_hot(jnp.where(block > 0, lane, -1))
        inside_ref[:, tile] = jnp.where(block > 0, 0.0, pick(rows, high, hot, bands)).astype(BF16)


def second_kernel(
    inside_ref, high_ref, faces_ref, ghosts_ref, hosts_ref, ham_ref, low_in, upper_in, near_in, far_in,
    field_ref, upper_ref, top_sums, inside, top, outside,
):
    bands, face_count = upper_in.shape
    elements, size = ham_ref.shape[:2]
    odd = odd_domain()
    below = jnp.where(odd, near_in[...], far_in[...])
    above = jnp.where(odd, far_in[...], near_in[...])
    faces = stacked(widened(low_in[...] + below)).astype(BF16)
    ghost = stacked(widened(upper_in[...] + above)).astype(BF16)
    ghosts = ghosts_ref[...]
    pick_into(outside, ghost, ghosts >> 8, hosts_ref)
    for tile in tiles(high_ref.shape[1]):
        extra = pick(faces, high_ref[:, tile], faces_ref[:, tile], bands)
        inside[:, tile] = inside_ref[:, tile] + extra.astype(BF16)
    for pair in pairs(elements):
        products = []
        for e in pair:
            values = jnp.concatenate(
                [inside[:, e * IN_EL : (e + 1) * IN_EL], outside[:, e * FACE_EL : (e + 1) * FACE_EL]], axis=1
            )
            field_ref[:, e * size : (e + 1) * size] = values
            product = jnp.dot(values, ham_ref[e, :, size - 128 :], preferred_element_type=F32)
            products.append(product[:, 128 - FACE_EL :])
        top[:, pair[0] * FACE_EL : (pair[-1] + 1) * FACE_EL] = jnp.concatenate(products, axis=1)
    spread_into(top_sums, top, ghosts >> 8)
    total = unstacked(gathered_sum(top_sums[...], hosts_ref[...]), bands)
    upper_ref[...] = total[:, :face_count] * (2.0 / HALF_WIDTH)


def third_kernel(
    psi_ref, slots_ref, hots_ref, ham_ref, face_ref, own_in, near_in, far_in, field_ref, own_ref, sums, inner
):
    bands, own = own_in.shape
    elements, size = ham_ref.shape[:2]
    face = face_ref[...]
    below = jnp.where(odd_domain(), near_in[...], far_in[...])
    added = gathered_sum(spread(below, face >> 8, own // LANES), one_hot(face & 255))
    for pair in pairs(elements):
        products = [
            jnp.dot(field_ref[:, e * size : (e + 1) * size], ham_ref[e], preferred_element_type=F32) for e in pair
        ]
        split_products(products, inner, None, pair[0])
    spread_into(sums, inner, slots_ref[...] >> 8)
    total = unstacked(gathered_sum(sums[...], hots_ref[...]), bands)
    current = own_in[...] + unstacked(added, bands)
    own_ref[...] = 2.0 * ((total - CENTER * current) / HALF_WIDTH) - psi_ref[...]


def last_kernel(own_in, face_ref, below_in, out_ref, short_ref):
    bands, own = own_in.shape
    face = face_ref[...]
    added = gathered_sum(spread(below_in[...], face >> 8, own // LANES), one_hot(face & 255))
    total = own_in[...] + unstacked(added, bands)
    out_ref[...] = total
    short_ref[...] = total[:, : short_ref.shape[1]].astype(BF16)


def call(kernel, out_shape, inputs, scratch=(), flops=0, moved=0, far=()):
    return pl.pallas_call(
        kernel,
        out_shape=out_shape,
        in_specs=[HBM if i in far else VMEM for i in range(len(inputs))],
        out_specs=jax.tree.map(lambda _: VMEM, out_shape),
        scratch_shapes=list(scratch),
        compiler_params=pltpu.CompilerParams(vmem_limit_bytes=LIMIT),
        cost_estimate=pl.CostEstimate(flops=flops, bytes_accessed=moved, transcendentals=0),
    )(*inputs)


def from_behind(block, axis, distance):
    devices = range(lax.axis_size(axis))
    route = [((i - distance) % len(devices), i) for i in devices]
    return lax.ppermute(block, axis, route)


def filter_field(psi, ham, conn, face_rows):
    bands, nodes = psi.shape
    elements, size = conn.shape
    own = round_up(nodes, LANES)
    faces = round_up(face_rows.shape[0], 128)
    trimmed = round_up(nodes, 128)
    face_count = elements * (size - IN_EL)
    inner_count = elements * IN_EL
    shape = jax.ShapeDtypeStruct
    face_field = shape((bands, faces), F32)
    own_field = shape((bands, own), F32)
    sums = pltpu.VMEM((2 * own // LANES * bands, inner_count), BF16)
    top_sums = pltpu.VMEM((2 * round_up(faces, LANES) // LANES * bands, face_count), BF16)
    inner = pltpu.VMEM((bands, inner_count), F32)
    top = pltpu.VMEM((bands, face_count), F32)
    inside_field = pltpu.VMEM((bands, inner_count), BF16)
    outside = pltpu.VMEM((bands, face_count), BF16)

    with jax.named_scope("face_values"):
        values, wide, conn, face = call(
            face_kernel,
            (shape((bands, faces), BF16), own_field, shape(conn.shape, jnp.int32), shape((1, faces), jnp.int32)),
            [pltpu.with_memory_space_constraint(array, pltpu.HBM) for array in (psi, conn, face_rows)],
            (pltpu.VMEM(psi.shape, F32), pltpu.VMEM(face_rows.shape, jnp.int32), pltpu.SemaphoreType.DMA((3,))),
            far=(0, 1, 2), flops=2 * 10**10, moved=4 * 10**7,
        )
    ghost = from_behind(values, "space", -1)
    with jax.named_scope("interior"):
        part, slots, ghosts, hots, hosts = call(
            functools.partial(interior_kernel, nodes),
            (
                shape((bands, elements * size), F32),
                shape((1, inner_count), jnp.int32), shape((1, face_count), jnp.int32),
                shape((LANES, inner_count), BF16), shape((LANES, face_count), BF16),
            ),
            (wide, conn, ham), (inside_field,), flops=4 * 10**9, moved=8 * 10**6,
        )
    with jax.named_scope("first_step"):
        current, upper, low, to_near, to_far = call(
            first_kernel, (own_field, *[face_field] * 4),
            (wide, slots, ghosts, hots, hosts, ham, face, ghost, part), (sums, top_sums, inner, top, outside),
            flops=4 * 10**9, moved=10**6,
        )
    domains = lax.axis_size("space")
    from_near = lax.ppermute(to_near, "space", [(i, i ^ 1) for i in range(domains)])
    from_far = lax.ppermute(to_far, "space", [(i, ((i + 1 ^ 1) - 1) % domains) for i in range(domains)])
    with jax.named_scope("off_face"):
        inside, high, faces = call(
            far_kernel,
            (shape((bands, inner_count), BF16), shape((1, inner_count), jnp.int32), shape((LANES, inner_count), BF16)),
            (current, slots, hots, face), flops=4 * 10**9, moved=10**6,
        )
    with jax.named_scope("second_step"):
        field, upper = call(
            second_kernel, (shape((bands, elements * size), BF16), face_field),
            (inside, high, faces, ghosts, hosts, ham, low, upper, from_near, from_far), (top_sums, inside_field, top, outside),
            flops=4 * 10**9, moved=10**6,
        )
    from_below = from_behind(upper, "space", 1)
    with jax.named_scope("second_sums"):
        following = call(
            third_kernel, own_field, (wide, slots, hots, ham, face, current, from_near, from_far, field), (sums, inner),
            flops=4 * 10**9, moved=8 * 10**6,
        )
    with jax.named_scope("last_faces"):
        return call(last_kernel, (own_field, shape((bands, trimmed), BF16)), (following, face, from_below))


def gram_kernel(*refs):
    *blocks, terms_ref, gram_ref = refs
    bands = blocks[0].shape[0]
    total = bands * len(blocks)
    me = lax.axis_index("band")
    for distance, block in enumerate(blocks):
        source = pl.multiple_of(lax.rem(me - distance + len(blocks), len(blocks)) * bands, bands)
        upper, lower = halves(widened(block[...].astype(F32)))
        terms_ref[pl.ds(source, bands), :] = upper
        terms_ref[pl.ds(total + source, bands), :] = lower
    terms = terms_ref[...]
    both = lax.dot_general(terms, terms, (((1,), (1,)), ((), ())), preferred_element_type=F32)
    gram = both[:total, :total] + (both[:total, total:] + both[total:, :total]) + both[total:, total:]
    gram_ref[...] = jnp.concatenate([gram[: total // 2], gram[total // 2 :]], axis=1)


def inverse_factor(matrix, block=8):
    size = matrix.shape[0]
    width = 2 * size
    lane = lax.broadcasted_iota(jnp.int32, (8, width), 1)
    row = lax.broadcasted_iota(jnp.int32, (8, width), 0)
    zero = jnp.zeros((size, size), F32)
    wide = jnp.concatenate([matrix, zero], axis=1)
    groups = [wide[8 * g : 8 * g + 8] + jnp.where(lane == row + (size + 8 * g), 1.0, 0.0) for g in range(size // 8)]
    for k in range(0, size, block):
        start = k // 8
        columns = [
            [jnp.broadcast_to(groups[g][:, k + q : k + q + 1], (8, width)) for g in range(start, size // 8)]
            for q in range(block)
        ]
        for q in range(block):
            at = k + q - 8 * start
            scale = 1.0 / columns[q][0][at : at + 1]
            column = [jnp.where(row > at, columns[q][0], 0.0)] + columns[q][1:]
            for p in range(q + 1, block):
                factor = columns[p][0][at : at + 1] * scale
                columns[p] = [value - weight * factor for value, weight in zip(columns[p], column)]
            factor = groups[start][at : at + 1] * scale
            for g, weight in enumerate(column):
                groups[start + g] = groups[start + g] - weight * factor
    out = []
    for g, rows in enumerate(groups):
        pivot = jnp.sum(jnp.where(lane == row + 8 * g, rows, 0.0), axis=1, keepdims=True)
        out.append(rows[:, size:] / jnp.sqrt(pivot))
    return jnp.concatenate(out, axis=0)


def ortho_kernel(nodes, count, gram_ref, terms_ref, out_ref, inverse_ref):
    bands = out_ref.shape[0]
    total = inverse_ref.shape[0]
    gram = jnp.concatenate([gram_ref[:, :total], gram_ref[:, total:]], axis=0)
    inverse_ref[...] = inverse_factor(gram / count)
    first = pl.multiple_of(lax.axis_index("band") * bands, bands)
    upper, lower = halves(inverse_ref[pl.ds(first, bands), :])
    rows = jnp.concatenate(
        [jnp.concatenate([upper, upper], axis=1), jnp.concatenate([lower, lower], axis=1)], axis=0
    )
    both = jnp.dot(rows, terms_ref[...], preferred_element_type=F32)
    out_ref[...] = (both[:bands] + both[bands:])[:, :nodes]


def space_sum(block):
    size = lax.axis_size("space")
    if size & (size - 1):
        return lax.psum(block, "space")
    step = 1
    while step < size:
        span = 2 if step == 1 or step * 2 == size else 4
        parts = [
            lax.ppermute(block, "space", [(i, i ^ (step * k)) for i in range(size)]) for k in range(1, span)
        ]
        block = sum(parts, block)
        step *= span
    return block


def per_device(psi, ham, conn, face_rows):
    bands, nodes = psi.shape
    following, short = filter_field(psi, ham, conn, face_rows)
    groups = lax.axis_size("band")
    total = groups * bands
    own = round_up(nodes, LANES)
    shape = jax.ShapeDtypeStruct
    blocks = [following] + [from_behind(short, "band", i) for i in range(1, groups)]
    with jax.named_scope("gram"):
        terms, gram = call(gram_kernel, (shape((2 * total, own), BF16), shape((total // 2, 2 * total), F32)), blocks)
    with jax.named_scope("gram_sum"):
        gram = space_sum(gram)
    with jax.named_scope("orthonormal"):
        return call(
            functools.partial(ortho_kernel, nodes, nodes * lax.axis_size("space")),
            shape((bands, nodes), F32), (gram, terms), (pltpu.VMEM((total, total), F32),),
        )


def solution(mesh):
    placed = (P("band", "space"), P("space", None, None), P("space", None), P("space"))
    return jax.shard_map(
        per_device, mesh=mesh, in_specs=placed, out_specs=P("band", "space"), check_vma=False
    )
```

```python
import functools

import jax
import jax.numpy as jnp
from jax import lax
from jax.experimental import pallas as pl
from jax.experimental.pallas import tpu as pltpu
from jax.sharding import PartitionSpec as P

FACE_EL = 64
IN_EL = 448
LANES = 256

CENTER = 6.25
HALF_WIDTH = 7.5

F32 = jnp.float32
BF16 = jnp.bfloat16
VMEM = pl.BlockSpec(memory_space=pltpu.VMEM)
HBM = pl.BlockSpec(memory_space=pltpu.HBM)
LIMIT = 24 * 1024 * 1024


def round_up(count, unit):
    return -(-count // unit) * unit


def one_hot(low):
    rows = lax.broadcasted_iota(jnp.int32, (LANES, low.shape[1]), 0)
    return jnp.where(rows == low, 1.0, 0.0).astype(BF16)


def stacked(field):
    blocks = field.shape[1] // LANES
    return jnp.concatenate([field[:, i * LANES : (i + 1) * LANES] for i in range(blocks)], axis=0)


def unstacked(rows, bands):
    blocks = rows.shape[0] // bands
    return jnp.concatenate([rows[i * bands : (i + 1) * bands] for i in range(blocks)], axis=1)


def pick(rows, high, low_hot, bands, first=0):
    table = jnp.dot(rows, low_hot, preferred_element_type=F32)
    out = jnp.zeros((bands, low_hot.shape[1]), F32)
    for i in range(rows.shape[0] // bands):
        out = jnp.where(high == i + first, table[i * bands : (i + 1) * bands], out)
    return out


def halves(values):
    upper = values.astype(BF16)
    return upper, (values - upper.astype(F32)).astype(BF16)


def spread(values, high, blocks, first=0):
    rows = []
    for part in halves(values):
        wide = part.astype(F32)
        for i in range(blocks):
            rows.append(jnp.where(high == i + first, wide, 0.0).astype(BF16))
    return jnp.concatenate(rows, axis=0)


def gathered_sum(rows, low_hot):
    both = lax.dot_general(rows, low_hot, (((1,), (1,)), ((), ())), preferred_element_type=F32)
    count = both.shape[0] // 2
    return both[:count] + both[count:]


def tiles(count, width=LANES):
    return [slice(start, min(start + width, count)) for start in range(0, count, width)]


def hot_into(hots_ref, low):
    for tile in tiles(low.shape[1]):
        hots_ref[:, tile] = one_hot(low[:, tile])


def pick_into(out_ref, rows, high, hots_ref):
    for tile in tiles(high.shape[1]):
        out_ref[:, tile] = pick(rows, high[:, tile], hots_ref[:, tile], out_ref.shape[0]).astype(out_ref.dtype)


def spread_into(sums_ref, values_ref, high):
    bands = values_ref.shape[0]
    blocks = sums_ref.shape[0] // (2 * bands)
    for tile in tiles(high.shape[1]):
        at = high[:, tile]
        upper, lower = (part.astype(F32) for part in halves(values_ref[:, tile]))
        for i in range(blocks):
            here = at == i
            sums_ref[i * bands : (i + 1) * bands, tile] = jnp.where(here, upper, 0.0).astype(BF16)
            sums_ref[(blocks + i) * bands : (blocks + i + 1) * bands, tile] = jnp.where(here, lower, 0.0).astype(BF16)


def split_products(products, inner_ref, top_ref, first):
    inner = jnp.concatenate([product[:, :IN_EL] for product in products], axis=1)
    top = jnp.concatenate([product[:, IN_EL:] for product in products], axis=1)
    inner_ref[:, first * IN_EL : first * IN_EL + inner.shape[1]] = inner
    if top_ref is not None:
        top_ref[:, first * FACE_EL : first * FACE_EL + top.shape[1]] = top


def pairs(elements):
    return [range(e, min(e + 2, elements)) for e in range(0, elements, 2)]


def packed(ref, width, first, last):
    return jnp.concatenate([ref[e : e + 1, first:last] for e in range(width)], axis=1)


def face_kernel(psi_hbm, conn_hbm, face_hbm, values_ref, psi_out, conn_out, face_out, psi_ref, face_ref, sems):
    bands, nodes = psi_hbm.shape
    copies = [
        pltpu.make_async_copy(face_hbm, face_ref, sems.at[0]),
        pltpu.make_async_copy(psi_hbm, psi_ref, sems.at[1]),
        pltpu.make_async_copy(conn_hbm, conn_out, sems.at[2]),
    ]
    for copy in copies:
        copy.start()
    psi_out[...] = jnp.zeros_like(psi_out)
    face_out[...] = jnp.full_like(face_out, -1)
    copies[0].wait()
    face_out[:, : face_ref.shape[0]] = face_ref[...].reshape(1, face_ref.shape[0])
    face = face_out[...]
    hot = one_hot(face & 255)
    copies[1].wait()
    psi_out[:, :nodes] = psi_ref[...]
    values_ref[...] = pick(stacked(psi_out[...]).astype(BF16), face >> 8, hot, bands).astype(BF16)
    copies[2].wait()


def interior_kernel(
    nodes, psi_ref, conn_ref, ham_ref, part_ref, slots_ref, ghosts_ref, hots_ref, hosts_ref, inside_ref
):
    elements, size = conn_ref.shape
    slots_ref[...] = packed(conn_ref, elements, 0, IN_EL)
    ghosts_ref[...] = packed(conn_ref, elements, IN_EL, size) - nodes
    hot_into(hosts_ref, ghosts_ref[...] & 255)
    slots = slots_ref[...]
    hot_into(hots_ref, slots & 255)
    pick_into(inside_ref, stacked(psi_ref[...]).astype(BF16), slots >> 8, hots_ref)
    for e in range(elements):
        part_ref[:, e * size : (e + 1) * size] = jnp.dot(
            inside_ref[:, e * IN_EL : (e + 1) * IN_EL], ham_ref[e, :IN_EL, :], preferred_element_type=F32
        )


def widened(values):
    bands, count = values.shape
    if count % LANES == 0:
        return values
    return jnp.concatenate([values, jnp.zeros((bands, round_up(count, LANES) - count), values.dtype)], axis=1)


def odd_domain():
    return lax.rem(lax.axis_index("space"), 2) == 1


def first_kernel(
    psi_ref, slots_ref, ghosts_ref, hots_ref, hosts_ref, ham_ref, face_ref, ghost_ref, part_ref,
    own_ref, upper_ref, low_ref, near_ref, far_ref, sums, top_sums, inner, top, outside,
):
    bands, own = psi_ref.shape
    elements, size = ham_ref.shape[:2]
    face_count = ghost_ref.shape[1]
    ghosts = ghosts_ref[...]
    pick_into(outside, stacked(widened(ghost_ref[...])), ghosts >> 8, hosts_ref)
    for pair in pairs(elements):
        products = [
            part_ref[:, e * size : (e + 1) * size]
            + jnp.dot(outside[:, e * FACE_EL : (e + 1) * FACE_EL], ham_ref[e, IN_EL:, :], preferred_element_type=F32)
            for e in pair
        ]
        split_products(products, inner, top, pair[0])
    spread_into(sums, inner, slots_ref[...] >> 8)
    spread_into(top_sums, top, ghosts >> 8)
    upper = unstacked(gathered_sum(top_sums[...], hosts_ref[...]), bands)[:, :face_count] / HALF_WIDTH
    upper_ref[...] = upper
    total = unstacked(gathered_sum(sums[...], hots_ref[...]), bands)
    current = (total - CENTER * psi_ref[...]) / HALF_WIDTH
    own_ref[...] = current
    face = face_ref[...]
    face_hot = one_hot(face & 255)
    terms = halves(stacked(current))
    low = pick(terms[0], face >> 8, face_hot, bands) + pick(terms[1], face >> 8, face_hot, bands)
    low_ref[...] = low
    odd = odd_domain()
    near_ref[...] = jnp.where(odd, low, upper)
    far_ref[...] = jnp.where(odd, upper, low)


def far_kernel(own_in, slots_ref, hots_ref, face_ref, inside_ref, high_ref, faces_ref):
    bands, own = own_in.shape
    blocks = round_up(own // LANES, 16)
    face = face_ref[...]
    number = lax.broadcasted_iota(jnp.int32, (blocks, face.shape[1]), 1)
    held = lax.broadcasted_iota(jnp.int32, number.shape, 0) == (face >> 8)
    digits = [jnp.where(held, digit, 0).astype(F32).astype(BF16) for digit in ((number >> 8) + 1, number & 255)]
    table = lax.dot_general(
        jnp.concatenate(digits, axis=0), one_hot(face & 255), (((1,), (1,)), ((), ())), preferred_element_type=F32
    ).astype(BF16)
    rows = stacked(own_in[...]).astype(BF16)
    for tile in tiles(slots_ref.shape[1]):
        high = slots_ref[:, tile] >> 8
        hot = hots_ref[:, tile]
        both = jnp.dot(table, hot, preferred_element_type=F32)
        held = lax.broadcasted_iota(jnp.int32, (blocks, both.shape[1]), 0) == high
        block = jnp.sum(jnp.where(held, both[:blocks], 0.0), axis=0, keepdims=True).astype(jnp.int32)
        lane = jnp.sum(jnp.where(held, both[blocks:], 0.0), axis=0, keepdims=True).astype(jnp.int32)
        high_ref[:, tile] = block - 1
        faces_ref[:, tile] = one_hot(jnp.where(block > 0, lane, -1))
        inside_ref[:, tile] = jnp.where(block > 0, 0.0, pick(rows, high, hot, bands)).astype(BF16)


def second_kernel(
    inside_ref, high_ref, faces_ref, ghosts_ref, hosts_ref, ham_ref, low_in, upper_in, near_in, far_in,
    field_ref, upper_ref, top_sums, inside, top, outside,
):
    bands, face_count = upper_in.shape
    elements, size = ham_ref.shape[:2]
    odd = odd_domain()
    below = jnp.where(odd, near_in[...], far_in[...])
    above = jnp.where(odd, far_in[...], near_in[...])
    faces = stacked(widened(low_in[...] + below)).astype(BF16)
    ghost = stacked(widened(upper_in[...] + above)).astype(BF16)
    ghosts = ghosts_ref[...]
    pick_into(outside, ghost, ghosts >> 8, hosts_ref)
    for tile in tiles(high_ref.shape[1]):
        extra = pick(faces, high_ref[:, tile], faces_ref[:, tile], bands)
        inside[:, tile] = inside_ref[:, tile] + extra.astype(BF16)
    for pair in pairs(elements):
        products = []
        for e in pair:
            values = jnp.concatenate(
                [inside[:, e * IN_EL : (e + 1) * IN_EL], outside[:, e * FACE_EL : (e + 1) * FACE_EL]], axis=1
            )
            field_ref[:, e * size : (e + 1) * size] = values
            product = jnp.dot(values, ham_ref[e, :, size - 128 :], preferred_element_type=F32)
            products.append(product[:, 128 - FACE_EL :])
        top[:, pair[0] * FACE_EL : (pair[-1] + 1) * FACE_EL] = jnp.concatenate(products, axis=1)
    spread_into(top_sums, top, ghosts >> 8)
    total = unstacked(gathered_sum(top_sums[...], hosts_ref[...]), bands)
    upper_ref[...] = total[:, :face_count] * (2.0 / HALF_WIDTH)


def third_kernel(
    psi_ref, slots_ref, hots_ref, ham_ref, face_ref, own_in, near_in, far_in, field_ref, own_ref, sums, inner
):
    bands, own = own_in.shape
    elements, size = ham_ref.shape[:2]
    face = face_ref[...]
    below = jnp.where(odd_domain(), near_in[...], far_in[...])
    added = gathered_sum(spread(below, face >> 8, own // LANES), one_hot(face & 255))
    for pair in pairs(elements):
        products = [
            jnp.dot(field_ref[:, e * size : (e + 1) * size], ham_ref[e], preferred_element_type=F32) for e in pair
        ]
        split_products(products, inner, None, pair[0])
    spread_into(sums, inner, slots_ref[...] >> 8)
    total = unstacked(gathered_sum(sums[...], hots_ref[...]), bands)
    current = own_in[...] + unstacked(added, bands)
    own_ref[...] = 2.0 * ((total - CENTER * current) / HALF_WIDTH) - psi_ref[...]


def last_kernel(own_in, face_ref, below_in, out_ref, short_ref):
    bands, own = own_in.shape
    face = face_ref[...]
    added = gathered_sum(spread(below_in[...], face >> 8, own // LANES), one_hot(face & 255))
    total = own_in[...] + unstacked(added, bands)
    out_ref[...] = total
    short_ref[...] = total[:, : short_ref.shape[1]].astype(BF16)


def call(kernel, out_shape, inputs, scratch=(), flops=0, moved=0, far=()):
    return pl.pallas_call(
        kernel,
        out_shape=out_shape,
        in_specs=[HBM if i in far else VMEM for i in range(len(inputs))],
        out_specs=jax.tree.map(lambda _: VMEM, out_shape),
        scratch_shapes=list(scratch),
        compiler_params=pltpu.CompilerParams(vmem_limit_bytes=LIMIT),
        cost_estimate=pl.CostEstimate(flops=flops, bytes_accessed=moved, transcendentals=0),
    )(*inputs)


def from_behind(block, axis, distance):
    devices = range(lax.axis_size(axis))
    route = [((i - distance) % len(devices), i) for i in devices]
    return lax.ppermute(block, axis, route)


def paired(groups):
    return groups & (groups - 1) == 0


def partner(block, axis, distance):
    size = lax.axis_size(axis)
    if paired(size):
        return lax.ppermute(block, axis, [(i, i ^ distance) for i in range(size)])
    return from_behind(block, axis, distance)


def filter_field(psi, ham, conn, face_rows):
    bands, nodes = psi.shape
    elements, size = conn.shape
    own = round_up(nodes, LANES)
    faces = round_up(face_rows.shape[0], 128)
    trimmed = round_up(nodes, 128)
    face_count = elements * (size - IN_EL)
    inner_count = elements * IN_EL
    shape = jax.ShapeDtypeStruct
    face_field = shape((bands, faces), F32)
    own_field = shape((bands, own), F32)
    sums = pltpu.VMEM((2 * own // LANES * bands, inner_count), BF16)
    top_sums = pltpu.VMEM((2 * round_up(faces, LANES) // LANES * bands, face_count), BF16)
    inner = pltpu.VMEM((bands, inner_count), F32)
    top = pltpu.VMEM((bands, face_count), F32)
    inside_field = pltpu.VMEM((bands, inner_count), BF16)
    outside = pltpu.VMEM((bands, face_count), BF16)

    with jax.named_scope("face_values"):
        values, wide, conn, face = call(
            face_kernel,
            (shape((bands, faces), BF16), own_field, shape(conn.shape, jnp.int32), shape((1, faces), jnp.int32)),
            [pltpu.with_memory_space_constraint(array, pltpu.HBM) for array in (psi, conn, face_rows)],
            (pltpu.VMEM(psi.shape, F32), pltpu.VMEM(face_rows.shape, jnp.int32), pltpu.SemaphoreType.DMA((3,))),
            far=(0, 1, 2), flops=2 * 10**10, moved=4 * 10**7,
        )
    ghost = from_behind(values, "space", -1)
    with jax.named_scope("interior"):
        part, slots, ghosts, hots, hosts = call(
            functools.partial(interior_kernel, nodes),
            (
                shape((bands, elements * size), F32),
                shape((1, inner_count), jnp.int32), shape((1, face_count), jnp.int32),
                shape((LANES, inner_count), BF16), shape((LANES, face_count), BF16),
            ),
            (wide, conn, ham), (inside_field,), flops=4 * 10**9, moved=8 * 10**6,
        )
    with jax.named_scope("first_step"):
        current, upper, low, to_near, to_far = call(
            first_kernel, (own_field, *[face_field] * 4),
            (wide, slots, ghosts, hots, hosts, ham, face, ghost, part), (sums, top_sums, inner, top, outside),
            flops=4 * 10**9, moved=10**6,
        )
    domains = lax.axis_size("space")
    from_far = lax.ppermute(to_far, "space", [(i, ((i + 1 ^ 1) - 1) % domains) for i in range(domains)])
    from_near = lax.ppermute(to_near, "space", [(i, i ^ 1) for i in range(domains)])
    with jax.named_scope("off_face"):
        inside, high, faces = call(
            far_kernel,
            (shape((bands, inner_count), BF16), shape((1, inner_count), jnp.int32), shape((LANES, inner_count), BF16)),
            (current, slots, hots, face), flops=4 * 10**9, moved=10**6,
        )
    with jax.named_scope("second_step"):
        field, upper = call(
            second_kernel, (shape((bands, elements * size), BF16), face_field),
            (inside, high, faces, ghosts, hosts, ham, low, upper, from_near, from_far), (top_sums, inside_field, top, outside),
            flops=4 * 10**9, moved=10**6,
        )
    from_below = from_behind(upper, "space", 1)
    with jax.named_scope("second_sums"):
        following = call(
            third_kernel, own_field, (wide, slots, hots, ham, face, current, from_near, from_far, field), (sums, inner),
            flops=4 * 10**9, moved=8 * 10**6,
        )
    with jax.named_scope("last_faces"):
        return call(last_kernel, (own_field, shape((bands, trimmed), BF16)), (following, face, from_below))


def gram_kernel(*refs):
    *blocks, terms_ref, gram_ref = refs
    bands = blocks[0].shape[0]
    total = bands * len(blocks)
    me = lax.axis_index("band")
    for distance, block in enumerate(blocks):
        source = me ^ distance if paired(len(blocks)) else lax.rem(me - distance + len(blocks), len(blocks))
        source = pl.multiple_of(source * bands, bands)
        if distance == 0:
            upper, lower = halves(block[...])
            terms_ref[total:, :] = lower
        else:
            upper = widened(block[...])
        terms_ref[pl.ds(source, bands), :] = upper
    terms = terms_ref[...]
    both = lax.dot_general(terms, terms, (((1,), (1,)), ((), ())), preferred_element_type=F32)
    down = jnp.concatenate([both[total:]] * len(blocks), axis=0)
    across = jnp.concatenate([both[:, total:]] * len(blocks), axis=1)
    corner = jnp.concatenate([down[:, total:]] * len(blocks), axis=1)
    own_row = lax.broadcasted_iota(jnp.int32, (total, total), 0) // bands == me
    own_column = lax.broadcasted_iota(jnp.int32, (total, total), 1) // bands == me
    cross = jnp.where(own_row, down[:, :total], 0.0) + jnp.where(own_column, across[:total], 0.0)
    gram = both[:total, :total] + (cross + jnp.where(own_row & own_column, corner, 0.0))
    gram_ref[...] = jnp.concatenate([gram[: total // 2], gram[total // 2 :]], axis=1)


def inverse_factor(matrix, block=8):
    size = matrix.shape[0]
    width = 2 * size
    lane = lax.broadcasted_iota(jnp.int32, (8, width), 1)
    row = lax.broadcasted_iota(jnp.int32, (8, width), 0)
    zero = jnp.zeros((size, size), F32)
    wide = jnp.concatenate([matrix, zero], axis=1)
    groups = [wide[8 * g : 8 * g + 8] + jnp.where(lane == row + (size + 8 * g), 1.0, 0.0) for g in range(size // 8)]
    for k in range(0, size, block):
        start = k // 8
        columns = [
            [jnp.broadcast_to(groups[g][:, k + q : k + q + 1], (8, width)) for g in range(start, size // 8)]
            for q in range(block)
        ]
        for q in range(block):
            at = k + q - 8 * start
            scale = 1.0 / columns[q][0][at : at + 1]
            column = [jnp.where(row > at, columns[q][0], 0.0)] + columns[q][1:]
            for p in range(q + 1, block):
                factor = columns[p][0][at : at + 1] * scale
                columns[p] = [value - weight * factor for value, weight in zip(columns[p], column)]
            factor = groups[start][at : at + 1] * scale
            for g, weight in enumerate(column):
                groups[start + g] = groups[start + g] - weight * factor
    out = []
    for g, rows in enumerate(groups):
        pivot = jnp.sum(jnp.where(lane == row + 8 * g, rows, 0.0), axis=1, keepdims=True)
        out.append(rows[:, size:] / jnp.sqrt(pivot))
    return jnp.concatenate(out, axis=0)


def ortho_kernel(nodes, count, gram_ref, terms_ref, out_ref, inverse_ref):
    bands = out_ref.shape[0]
    total = inverse_ref.shape[0]
    gram = jnp.concatenate([gram_ref[:, :total], gram_ref[:, total:]], axis=0)
    inverse_ref[...] = inverse_factor(gram / count)
    first = pl.multiple_of(lax.axis_index("band") * bands, bands)
    own = inverse_ref[pl.ds(first, bands), :]
    column = lax.broadcasted_iota(jnp.int32, own.shape, 1)
    diagonal = jnp.where(column // bands == lax.axis_index("band"), own, 0.0)
    diagonal = sum(diagonal[:, i : i + bands] for i in range(0, total, bands))
    rows = jnp.concatenate(halves(jnp.concatenate([own, diagonal], axis=1)), axis=0)
    both = jnp.dot(rows, terms_ref[...], preferred_element_type=F32)
    out_ref[...] = (both[:bands] + both[bands:])[:, :nodes]


def space_sum(block):
    size = lax.axis_size("space")
    if size & (size - 1):
        return lax.psum(block, "space")
    step = 1
    while step < size:
        span = 2 if step == 1 or step * 2 == size else 4
        parts = [
            lax.ppermute(block, "space", [(i, i ^ (step * k)) for i in range(size)]) for k in range(1, span)
        ]
        block = sum(parts, block)
        step *= span
    return block


def per_device(psi, ham, conn, face_rows):
    bands, nodes = psi.shape
    following, short = filter_field(psi, ham, conn, face_rows)
    groups = lax.axis_size("band")
    total = groups * bands
    own = round_up(nodes, LANES)
    shape = jax.ShapeDtypeStruct
    blocks = [following] + [partner(short, "band", i) for i in range(1, groups)]
    with jax.named_scope("gram"):
        terms, gram = call(gram_kernel, (shape((total + bands, own), BF16), shape((total // 2, 2 * total), F32)), blocks)
    with jax.named_scope("gram_sum"):
        gram = space_sum(gram)
    with jax.named_scope("orthonormal"):
        return call(
            functools.partial(ortho_kernel, nodes, nodes * lax.axis_size("space")),
            shape((bands, nodes), F32), (gram, terms), (pltpu.VMEM((total, total), F32),),
        )


def solution(mesh):
    placed = (P("band", "space"), P("space", None, None), P("space", None), P("space"))
    return jax.shard_map(
        per_device, mesh=mesh, in_specs=placed, out_specs=P("band", "space"), check_vma=False
    )
```

```python
import functools

import jax
import jax.numpy as jnp
from jax import lax
from jax.experimental import pallas as pl
from jax.experimental.pallas import tpu as pltpu
from jax.sharding import PartitionSpec as P

FACE_EL = 64
IN_EL = 448
LANES = 256

CENTER = 6.25
HALF_WIDTH = 7.5

F32 = jnp.float32
BF16 = jnp.bfloat16
VMEM = pl.BlockSpec(memory_space=pltpu.VMEM)
HBM = pl.BlockSpec(memory_space=pltpu.HBM)
LIMIT = 24 * 1024 * 1024


def round_up(count, unit):
    return -(-count // unit) * unit


def one_hot(low):
    rows = lax.broadcasted_iota(jnp.int32, (LANES, low.shape[1]), 0)
    return jnp.where(rows == low, 1.0, 0.0).astype(BF16)


def stacked(field):
    blocks = field.shape[1] // LANES
    return jnp.concatenate([field[:, i * LANES : (i + 1) * LANES] for i in range(blocks)], axis=0)


def unstacked(rows, bands):
    blocks = rows.shape[0] // bands
    return jnp.concatenate([rows[i * bands : (i + 1) * bands] for i in range(blocks)], axis=1)


def pick(rows, high, low_hot, bands, first=0):
    table = jnp.dot(rows, low_hot, preferred_element_type=F32)
    out = jnp.zeros((bands, low_hot.shape[1]), F32)
    for i in range(rows.shape[0] // bands):
        out = jnp.where(high == i + first, table[i * bands : (i + 1) * bands], out)
    return out


def halves(values):
    upper = values.astype(BF16)
    return upper, (values - upper.astype(F32)).astype(BF16)


def spread(values, high, blocks, first=0):
    rows = []
    for part in halves(values):
        wide = part.astype(F32)
        for i in range(blocks):
            rows.append(jnp.where(high == i + first, wide, 0.0).astype(BF16))
    return jnp.concatenate(rows, axis=0)


def gathered_sum(rows, low_hot):
    both = lax.dot_general(rows, low_hot, (((1,), (1,)), ((), ())), preferred_element_type=F32)
    count = both.shape[0] // 2
    return both[:count] + both[count:]


def tiles(count, width=LANES):
    return [slice(start, min(start + width, count)) for start in range(0, count, width)]


def hot_into(hots_ref, low):
    for tile in tiles(low.shape[1]):
        hots_ref[:, tile] = one_hot(low[:, tile])


def pick_into(out_ref, rows, high, hots_ref):
    for tile in tiles(high.shape[1]):
        out_ref[:, tile] = pick(rows, high[:, tile], hots_ref[:, tile], out_ref.shape[0]).astype(out_ref.dtype)


def spread_once(values, high, blocks):
    return jnp.concatenate([jnp.where(high == i, values, 0.0).astype(BF16) for i in range(blocks)], axis=0)


def scatter_sum(values_ref, high, hots_ref, blocks, once=False):
    total = None
    for tile in tiles(high.shape[1], 2 * LANES):
        rows = (spread_once if once else spread)(values_ref[:, tile], high[:, tile], blocks)
        part = lax.dot_general(
            rows, hots_ref[:, tile],
            (((1,), (1,)), ((), ())), preferred_element_type=F32,
        )
        total = part if total is None else total + part
    if once:
        return total
    count = total.shape[0] // 2
    return total[:count] + total[count:]


def split_products(products, inner_ref, top_ref, first):
    inner = jnp.concatenate([product[:, :IN_EL] for product in products], axis=1)
    top = jnp.concatenate([product[:, IN_EL:] for product in products], axis=1)
    inner_ref[:, first * IN_EL : first * IN_EL + inner.shape[1]] = inner
    if top_ref is not None:
        top_ref[:, first * FACE_EL : first * FACE_EL + top.shape[1]] = top


def pairs(elements):
    return [range(e, min(e + 2, elements)) for e in range(0, elements, 2)]


def packed(ref, width, first, last):
    return jnp.concatenate([ref[e : e + 1, first:last] for e in range(width)], axis=1)


def face_kernel(psi_hbm, conn_hbm, face_hbm, values_ref, psi_out, conn_out, face_out, psi_ref, face_ref, sems):
    bands, nodes = psi_hbm.shape
    copies = [
        pltpu.make_async_copy(face_hbm, face_ref, sems.at[0]),
        pltpu.make_async_copy(psi_hbm, psi_ref, sems.at[1]),
        pltpu.make_async_copy(conn_hbm, conn_out, sems.at[2]),
    ]
    for copy in copies:
        copy.start()
    psi_out[...] = jnp.zeros_like(psi_out)
    face_out[...] = jnp.full_like(face_out, -1)
    copies[0].wait()
    face_out[:, : face_ref.shape[0]] = face_ref[...].reshape(1, face_ref.shape[0])
    face = face_out[...]
    hot = one_hot(face & 255)
    copies[1].wait()
    psi_out[:, :nodes] = psi_ref[...]
    values_ref[...] = pick(stacked(psi_out[...]).astype(BF16), face >> 8, hot, bands).astype(BF16)
    copies[2].wait()


def interior_kernel(
    nodes, psi_ref, conn_ref, ham_ref, part_ref, slots_ref, ghosts_ref, hots_ref, hosts_ref, inside_ref
):
    elements, size = conn_ref.shape
    slots_ref[...] = packed(conn_ref, elements, 0, IN_EL)
    ghosts_ref[...] = packed(conn_ref, elements, IN_EL, size) - nodes
    hot_into(hosts_ref, ghosts_ref[...] & 255)
    slots = slots_ref[...]
    hot_into(hots_ref, slots & 255)
    pick_into(inside_ref, stacked(psi_ref[...]).astype(BF16), slots >> 8, hots_ref)
    for e in range(elements):
        part_ref[:, e * size : (e + 1) * size] = jnp.dot(
            inside_ref[:, e * IN_EL : (e + 1) * IN_EL], ham_ref[e, :IN_EL, :], preferred_element_type=F32
        )


def widened(values):
    bands, count = values.shape
    if count % LANES == 0:
        return values
    return jnp.concatenate([values, jnp.zeros((bands, round_up(count, LANES) - count), values.dtype)], axis=1)


def odd_domain():
    return lax.rem(lax.axis_index("space"), 2) == 1


def first_kernel(
    psi_ref, slots_ref, ghosts_ref, hots_ref, hosts_ref, ham_ref, face_ref, ghost_ref, part_ref,
    own_ref, upper_ref, low_ref, near_ref, far_ref, inner, top, outside,
):
    bands, own = psi_ref.shape
    elements, size = ham_ref.shape[:2]
    face_count = ghost_ref.shape[1]
    ghosts = ghosts_ref[...]
    pick_into(outside, stacked(widened(ghost_ref[...])), ghosts >> 8, hosts_ref)
    for pair in pairs(elements):
        products = [
            part_ref[:, e * size : (e + 1) * size]
            + jnp.dot(outside[:, e * FACE_EL : (e + 1) * FACE_EL], ham_ref[e, IN_EL:, :], preferred_element_type=F32)
            for e in pair
        ]
        split_products(products, inner, top, pair[0])
    upper = scatter_sum(top, ghosts >> 8, hosts_ref, round_up(face_count, LANES) // LANES)
    upper = unstacked(upper, bands)[:, :face_count] / HALF_WIDTH
    upper_ref[...] = upper
    total = unstacked(scatter_sum(inner, slots_ref[...] >> 8, hots_ref, own // LANES, True), bands)
    current = (total - CENTER * psi_ref[...]) / HALF_WIDTH
    own_ref[...] = current
    face = face_ref[...]
    face_hot = one_hot(face & 255)
    terms = halves(stacked(current))
    low = pick(terms[0], face >> 8, face_hot, bands) + pick(terms[1], face >> 8, face_hot, bands)
    low_ref[...] = low
    odd = odd_domain()
    near_ref[...] = jnp.where(odd, low, upper)
    far_ref[...] = jnp.where(odd, upper, low)


def far_kernel(own_in, slots_ref, hots_ref, face_ref, inside_ref, high_ref, faces_ref):
    bands, own = own_in.shape
    blocks = round_up(own // LANES, 16)
    face = face_ref[...]
    number = lax.broadcasted_iota(jnp.int32, (blocks, face.shape[1]), 1)
    held = lax.broadcasted_iota(jnp.int32, number.shape, 0) == (face >> 8)
    digits = [jnp.where(held, digit, 0).astype(F32).astype(BF16) for digit in ((number >> 8) + 1, number & 255)]
    table = lax.dot_general(
        jnp.concatenate(digits, axis=0), one_hot(face & 255), (((1,), (1,)), ((), ())), preferred_element_type=F32
    ).astype(BF16)
    rows = stacked(own_in[...]).astype(BF16)
    for tile in tiles(slots_ref.shape[1]):
        high = slots_ref[:, tile] >> 8
        hot = hots_ref[:, tile]
        both = jnp.dot(table, hot, preferred_element_type=F32)
        held = lax.broadcasted_iota(jnp.int32, (blocks, both.shape[1]), 0) == high
        block = jnp.sum(jnp.where(held, both[:blocks], 0.0), axis=0, keepdims=True).astype(jnp.int32)
        lane = jnp.sum(jnp.where(held, both[blocks:], 0.0), axis=0, keepdims=True).astype(jnp.int32)
        high_ref[:, tile] = block - 1
        faces_ref[:, tile] = one_hot(jnp.where(block > 0, lane, -1))
        inside_ref[:, tile] = jnp.where(block > 0, 0.0, pick(rows, high, hot, bands)).astype(BF16)


def second_kernel(
    inside_ref, high_ref, faces_ref, ghosts_ref, hosts_ref, ham_ref, low_in, upper_in, near_in, far_in,
    field_ref, upper_ref, inside, top, outside,
):
    bands, face_count = upper_in.shape
    elements, size = ham_ref.shape[:2]
    odd = odd_domain()
    below = jnp.where(odd, near_in[...], far_in[...])
    above = jnp.where(odd, far_in[...], near_in[...])
    faces = stacked(widened(low_in[...] + below)).astype(BF16)
    ghost = stacked(widened(upper_in[...] + above)).astype(BF16)
    ghosts = ghosts_ref[...]
    pick_into(outside, ghost, ghosts >> 8, hosts_ref)
    for tile in tiles(high_ref.shape[1]):
        extra = pick(faces, high_ref[:, tile], faces_ref[:, tile], bands)
        inside[:, tile] = inside_ref[:, tile] + extra.astype(BF16)
    for pair in pairs(elements):
        products = []
        for e in pair:
            values = jnp.concatenate(
                [inside[:, e * IN_EL : (e + 1) * IN_EL], outside[:, e * FACE_EL : (e + 1) * FACE_EL]], axis=1
            )
            field_ref[:, e * size : (e + 1) * size] = values
            product = jnp.dot(values, ham_ref[e, :, size - 128 :], preferred_element_type=F32)
            products.append(product[:, 128 - FACE_EL :])
        top[:, pair[0] * FACE_EL : (pair[-1] + 1) * FACE_EL] = jnp.concatenate(products, axis=1)
    total = unstacked(scatter_sum(top, ghosts >> 8, hosts_ref, round_up(face_count, LANES) // LANES), bands)
    upper_ref[...] = total[:, :face_count] * (2.0 / HALF_WIDTH)


def third_kernel(
    psi_ref, slots_ref, hots_ref, ham_ref, face_ref, own_in, near_in, far_in, field_ref, own_ref, inner
):
    bands, own = own_in.shape
    elements, size = ham_ref.shape[:2]
    face = face_ref[...]
    below = jnp.where(odd_domain(), near_in[...], far_in[...])
    added = gathered_sum(spread(below, face >> 8, own // LANES), one_hot(face & 255))
    for pair in pairs(elements):
        products = [
            jnp.dot(field_ref[:, e * size : (e + 1) * size], ham_ref[e], preferred_element_type=F32) for e in pair
        ]
        split_products(products, inner, None, pair[0])
    total = unstacked(scatter_sum(inner, slots_ref[...] >> 8, hots_ref, own // LANES, True), bands)
    current = own_in[...] + unstacked(added, bands)
    own_ref[...] = 2.0 * ((total - CENTER * current) / HALF_WIDTH) - psi_ref[...]


def last_kernel(own_in, face_ref, below_in, out_ref, short_ref):
    bands, own = own_in.shape
    face = face_ref[...]
    added = gathered_sum(spread(below_in[...], face >> 8, own // LANES), one_hot(face & 255))
    total = own_in[...] + unstacked(added, bands)
    out_ref[...] = total
    short_ref[...] = total[:, : short_ref.shape[1]].astype(BF16)


def call(kernel, out_shape, inputs, scratch=(), flops=0, moved=0, far=()):
    return pl.pallas_call(
        kernel,
        out_shape=out_shape,
        in_specs=[HBM if i in far else VMEM for i in range(len(inputs))],
        out_specs=jax.tree.map(lambda _: VMEM, out_shape),
        scratch_shapes=list(scratch),
        compiler_params=pltpu.CompilerParams(vmem_limit_bytes=LIMIT),
        cost_estimate=pl.CostEstimate(flops=flops, bytes_accessed=moved, transcendentals=0),
    )(*inputs)


def from_behind(block, axis, distance):
    devices = range(lax.axis_size(axis))
    route = [((i - distance) % len(devices), i) for i in devices]
    return lax.ppermute(block, axis, route)


def paired(groups):
    return groups & (groups - 1) == 0


def partner(block, axis, distance):
    size = lax.axis_size(axis)
    if paired(size):
        return lax.ppermute(block, axis, [(i, i ^ distance) for i in range(size)])
    return from_behind(block, axis, distance)


def filter_field(psi, ham, conn, face_rows):
    bands, nodes = psi.shape
    elements, size = conn.shape
    own = round_up(nodes, LANES)
    faces = round_up(face_rows.shape[0], 128)
    trimmed = round_up(nodes, 128)
    face_count = elements * (size - IN_EL)
    inner_count = elements * IN_EL
    shape = jax.ShapeDtypeStruct
    face_field = shape((bands, faces), F32)
    own_field = shape((bands, own), F32)
    inner = pltpu.VMEM((bands, inner_count), F32)
    top = pltpu.VMEM((bands, face_count), F32)
    inside_field = pltpu.VMEM((bands, inner_count), BF16)
    outside = pltpu.VMEM((bands, face_count), BF16)

    with jax.named_scope("face_values"):
        values, wide, conn, face = call(
            face_kernel,
            (shape((bands, faces), BF16), own_field, shape(conn.shape, jnp.int32), shape((1, faces), jnp.int32)),
            [pltpu.with_memory_space_constraint(array, pltpu.HBM) for array in (psi, conn, face_rows)],
            (pltpu.VMEM(psi.shape, F32), pltpu.VMEM(face_rows.shape, jnp.int32), pltpu.SemaphoreType.DMA((3,))),
            far=(0, 1, 2), flops=2 * 10**10, moved=4 * 10**7,
        )
    ghost = from_behind(values, "space", -1)
    with jax.named_scope("interior"):
        part, slots, ghosts, hots, hosts = call(
            functools.partial(interior_kernel, nodes),
            (
                shape((bands, elements * size), F32),
                shape((1, inner_count), jnp.int32), shape((1, face_count), jnp.int32),
                shape((LANES, inner_count), BF16), shape((LANES, face_count), BF16),
            ),
            (wide, conn, ham), (inside_field,), flops=4 * 10**9, moved=8 * 10**6,
        )
    with jax.named_scope("first_step"):
        current, upper, low, to_near, to_far = call(
            first_kernel, (own_field, *[face_field] * 4),
            (wide, slots, ghosts, hots, hosts, ham, face, ghost, part), (inner, top, outside),
            flops=4 * 10**9, moved=10**6,
        )
    domains = lax.axis_size("space")
    from_far = lax.ppermute(to_far, "space", [(i, ((i + 1 ^ 1) - 1) % domains) for i in range(domains)])
    from_near = lax.ppermute(to_near, "space", [(i, i ^ 1) for i in range(domains)])
    with jax.named_scope("off_face"):
        inside, high, faces = call(
            far_kernel,
            (shape((bands, inner_count), BF16), shape((1, inner_count), jnp.int32), shape((LANES, inner_count), BF16)),
            (current, slots, hots, face), flops=4 * 10**9, moved=10**6,
        )
    with jax.named_scope("second_step"):
        field, upper = call(
            second_kernel, (shape((bands, elements * size), BF16), face_field),
            (inside, high, faces, ghosts, hosts, ham, low, upper, from_near, from_far), (inside_field, top, outside),
            flops=4 * 10**9, moved=10**6,
        )
    from_below = from_behind(upper, "space", 1)
    with jax.named_scope("second_sums"):
        following = call(
            third_kernel, own_field, (wide, slots, hots, ham, face, current, from_near, from_far, field), (inner,),
            flops=4 * 10**9, moved=8 * 10**6,
        )
    with jax.named_scope("last_faces"):
        return call(last_kernel, (own_field, shape((bands, trimmed), BF16)), (following, face, from_below))


def gram_kernel(*refs):
    *blocks, terms_ref, gram_ref = refs
    bands = blocks[0].shape[0]
    total = bands * len(blocks)
    me = lax.axis_index("band")
    for distance, block in enumerate(blocks):
        source = me ^ distance if paired(len(blocks)) else lax.rem(me - distance + len(blocks), len(blocks))
        source = pl.multiple_of(source * bands, bands)
        if distance == 0:
            upper, lower = halves(block[...])
            terms_ref[total:, :] = lower
        else:
            upper = widened(block[...])
        terms_ref[pl.ds(source, bands), :] = upper
    terms = terms_ref[...]
    both = lax.dot_general(terms, terms, (((1,), (1,)), ((), ())), preferred_element_type=F32)
    down = jnp.concatenate([both[total:]] * len(blocks), axis=0)
    across = jnp.concatenate([both[:, total:]] * len(blocks), axis=1)
    corner = jnp.concatenate([down[:, total:]] * len(blocks), axis=1)
    own_row = lax.broadcasted_iota(jnp.int32, (total, total), 0) // bands == me
    own_column = lax.broadcasted_iota(jnp.int32, (total, total), 1) // bands == me
    cross = jnp.where(own_row, down[:, :total], 0.0) + jnp.where(own_column, across[:total], 0.0)
    gram = both[:total, :total] + (cross + jnp.where(own_row & own_column, corner, 0.0))
    gram_ref[...] = jnp.concatenate([gram[: total // 2], gram[total // 2 :]], axis=1)


def inverse_factor(matrix, block=8):
    size = matrix.shape[0]
    width = 2 * size
    lane = lax.broadcasted_iota(jnp.int32, (8, width), 1)
    row = lax.broadcasted_iota(jnp.int32, (8, width), 0)
    zero = jnp.zeros((size, size), F32)
    wide = jnp.concatenate([matrix, zero], axis=1)
    groups = [wide[8 * g : 8 * g + 8] + jnp.where(lane == row + (size + 8 * g), 1.0, 0.0) for g in range(size // 8)]
    for k in range(0, size, block):
        start = k // 8
        columns = [
            [jnp.broadcast_to(groups[g][:, k + q : k + q + 1], (8, width)) for g in range(start, size // 8)]
            for q in range(block)
        ]
        for q in range(block):
            at = k + q - 8 * start
            scale = 1.0 / columns[q][0][at : at + 1]
            column = [jnp.where(row > at, columns[q][0], 0.0)] + columns[q][1:]
            for p in range(q + 1, block):
                factor = columns[p][0][at : at + 1] * scale
                columns[p] = [value - weight * factor for value, weight in zip(columns[p], column)]
            factor = groups[start][at : at + 1] * scale
            for g, weight in enumerate(column):
                groups[start + g] = groups[start + g] - weight * factor
    out = []
    for g, rows in enumerate(groups):
        pivot = jnp.sum(jnp.where(lane == row + 8 * g, rows, 0.0), axis=1, keepdims=True)
        out.append(rows[:, size:] / jnp.sqrt(pivot))
    return jnp.concatenate(out, axis=0)


def ortho_kernel(nodes, count, gram_ref, terms_ref, out_ref, inverse_ref):
    bands = out_ref.shape[0]
    total = inverse_ref.shape[0]
    gram = jnp.concatenate([gram_ref[:, :total], gram_ref[:, total:]], axis=0)
    inverse_ref[...] = inverse_factor(gram / count)
    first = pl.multiple_of(lax.axis_index("band") * bands, bands)
    own = inverse_ref[pl.ds(first, bands), :]
    column = lax.broadcasted_iota(jnp.int32, own.shape, 1)
    diagonal = jnp.where(column // bands == lax.axis_index("band"), own, 0.0)
    diagonal = sum(diagonal[:, i : i + bands] for i in range(0, total, bands))
    rows = jnp.concatenate(halves(jnp.concatenate([own, diagonal], axis=1)), axis=0)
    both = jnp.dot(rows, terms_ref[...], preferred_element_type=F32)
    out_ref[...] = (both[:bands] + both[bands:])[:, :nodes]


def space_sum(block):
    size = lax.axis_size("space")
    if size & (size - 1):
        return lax.psum(block, "space")
    step = 1
    while step < size:
        span = 2 if step == 1 or step * 2 == size else 4
        parts = [
            lax.ppermute(block, "space", [(i, i ^ (step * k)) for i in range(size)]) for k in range(1, span)
        ]
        block = sum(parts, block)
        step *= span
    return block


def per_device(psi, ham, conn, face_rows):
    bands, nodes = psi.shape
    following, short = filter_field(psi, ham, conn, face_rows)
    groups = lax.axis_size("band")
    total = groups * bands
    own = round_up(nodes, LANES)
    shape = jax.ShapeDtypeStruct
    blocks = [following] + [partner(short, "band", i) for i in range(1, groups)]
    with jax.named_scope("gram"):
        terms, gram = call(gram_kernel, (shape((total + bands, own), BF16), shape((total // 2, 2 * total), F32)), blocks)
    with jax.named_scope("gram_sum"):
        gram = space_sum(gram)
    with jax.named_scope("orthonormal"):
        return call(
            functools.partial(ortho_kernel, nodes, nodes * lax.axis_size("space")),
            shape((bands, nodes), F32), (gram, terms), (pltpu.VMEM((total, total), F32),),
        )


def solution(mesh):
    placed = (P("band", "space"), P("space", None, None), P("space", None), P("space"))
    return jax.shard_map(
        per_device, mesh=mesh, in_specs=placed, out_specs=P("band", "space"), check_vma=False
    )
```

```python
import functools

import jax
import jax.numpy as jnp
from jax import lax
from jax.experimental import pallas as pl
from jax.experimental.pallas import tpu as pltpu
from jax.sharding import PartitionSpec as P

FACE_EL = 64
IN_EL = 448
LANES = 256

CENTER = 6.25
HALF_WIDTH = 7.5

F32 = jnp.float32
BF16 = jnp.bfloat16
VMEM = pl.BlockSpec(memory_space=pltpu.VMEM)
HBM = pl.BlockSpec(memory_space=pltpu.HBM)
LIMIT = 24 * 1024 * 1024


def round_up(count, unit):
    return -(-count // unit) * unit


def one_hot(low):
    rows = lax.broadcasted_iota(jnp.int32, (LANES, low.shape[1]), 0)
    return jnp.where(rows == low, 1.0, 0.0).astype(BF16)


def stacked(field):
    blocks = field.shape[1] // LANES
    return jnp.concatenate([field[:, i * LANES : (i + 1) * LANES] for i in range(blocks)], axis=0)


def unstacked(rows, bands):
    blocks = rows.shape[0] // bands
    return jnp.concatenate([rows[i * bands : (i + 1) * bands] for i in range(blocks)], axis=1)


def pick(rows, high, low_hot, bands, first=0):
    table = jnp.dot(rows, low_hot, preferred_element_type=F32)
    out = jnp.zeros((bands, low_hot.shape[1]), F32)
    for i in range(rows.shape[0] // bands):
        out = jnp.where(high == i + first, table[i * bands : (i + 1) * bands], out)
    return out


def halves(values):
    upper = values.astype(BF16)
    return upper, (values - upper.astype(F32)).astype(BF16)


def spread(values, high, blocks, first=0):
    rows = []
    for part in halves(values):
        wide = part.astype(F32)
        for i in range(blocks):
            rows.append(jnp.where(high == i + first, wide, 0.0).astype(BF16))
    return jnp.concatenate(rows, axis=0)


def lane_sums(rows, low_hot):
    return lax.dot_general(rows, low_hot, (((1,), (1,)), ((), ())), preferred_element_type=F32)


def tiles(count, width=LANES):
    return [slice(start, min(start + width, count)) for start in range(0, count, width)]


def hot_into(hots_ref, low):
    for tile in tiles(low.shape[1]):
        hots_ref[:, tile] = one_hot(low[:, tile])


def pick_into(out_ref, rows, high, hots_ref):
    for tile in tiles(high.shape[1]):
        out_ref[:, tile] = pick(rows, high[:, tile], hots_ref[:, tile], out_ref.shape[0]).astype(out_ref.dtype)


def spread_once(values, high, blocks):
    return jnp.concatenate([jnp.where(high == i, values, 0.0).astype(BF16) for i in range(blocks)], axis=0)


def scatter_sum(values_ref, high, hots_ref, blocks, once=False):
    total = None
    for tile in tiles(high.shape[1], 2 * LANES):
        rows = (spread_once if once else spread)(values_ref[:, tile], high[:, tile], blocks)
        part = lax.dot_general(
            rows, hots_ref[:, tile],
            (((1,), (1,)), ((), ())), preferred_element_type=F32,
        )
        total = part if total is None else total + part
    if once:
        return total
    count = total.shape[0] // 2
    return total[:count] + total[count:]


def split_products(products, inner_ref, top_ref, first):
    inner = jnp.concatenate([product[:, :IN_EL] for product in products], axis=1)
    top = jnp.concatenate([product[:, IN_EL:] for product in products], axis=1)
    inner_ref[:, first * IN_EL : first * IN_EL + inner.shape[1]] = inner
    if top_ref is not None:
        top_ref[:, first * FACE_EL : first * FACE_EL + top.shape[1]] = top


def pairs(elements):
    return [range(e, min(e + 2, elements)) for e in range(0, elements, 2)]


def packed(ref, width, first, last):
    return jnp.concatenate([ref[e : e + 1, first:last] for e in range(width)], axis=1)


def face_kernel(psi_hbm, conn_hbm, face_hbm, values_ref, psi_out, conn_out, face_out, psi_ref, face_ref, sems):
    bands, nodes = psi_hbm.shape
    copies = [
        pltpu.make_async_copy(face_hbm, face_ref, sems.at[0]),
        pltpu.make_async_copy(psi_hbm, psi_ref, sems.at[1]),
        pltpu.make_async_copy(conn_hbm, conn_out, sems.at[2]),
    ]
    for copy in copies:
        copy.start()
    psi_out[...] = jnp.zeros_like(psi_out)
    face_out[...] = jnp.full_like(face_out, -1)
    copies[0].wait()
    face_out[:, : face_ref.shape[0]] = face_ref[...].reshape(1, face_ref.shape[0])
    face = face_out[...]
    hot = one_hot(face & 255)
    copies[1].wait()
    psi_out[:, :nodes] = psi_ref[...]
    values_ref[...] = pick(stacked(psi_out[...]).astype(BF16), face >> 8, hot, bands).astype(BF16)
    copies[2].wait()


def interior_kernel(
    nodes, psi_ref, conn_ref, ham_ref, part_ref, slots_ref, ghosts_ref, hots_ref, hosts_ref, inside_ref
):
    elements, size = conn_ref.shape
    slots_ref[...] = packed(conn_ref, elements, 0, IN_EL)
    ghosts_ref[...] = packed(conn_ref, elements, IN_EL, size) - nodes
    hot_into(hosts_ref, ghosts_ref[...] & 255)
    slots = slots_ref[...]
    hot_into(hots_ref, slots & 255)
    pick_into(inside_ref, stacked(psi_ref[...]).astype(BF16), slots >> 8, hots_ref)
    for e in range(elements):
        part_ref[:, e * size : (e + 1) * size] = jnp.dot(
            inside_ref[:, e * IN_EL : (e + 1) * IN_EL], ham_ref[e, :IN_EL, :], preferred_element_type=F32
        )


def widened(values):
    bands, count = values.shape
    if count % LANES == 0:
        return values
    return jnp.concatenate([values, jnp.zeros((bands, round_up(count, LANES) - count), values.dtype)], axis=1)


def odd_domain():
    return lax.rem(lax.axis_index("space"), 2) == 1


def first_kernel(
    psi_ref, slots_ref, ghosts_ref, hots_ref, hosts_ref, ham_ref, face_ref, ghost_ref, part_ref,
    own_ref, upper_ref, near_ref, far_ref, inner, top, outside,
):
    bands, own = psi_ref.shape
    elements, size = ham_ref.shape[:2]
    face_count = ghost_ref.shape[1]
    ghosts = ghosts_ref[...]
    pick_into(outside, stacked(widened(ghost_ref[...])), ghosts >> 8, hosts_ref)
    for pair in pairs(elements):
        products = [
            part_ref[:, e * size : (e + 1) * size]
            + jnp.dot(outside[:, e * FACE_EL : (e + 1) * FACE_EL], ham_ref[e, IN_EL:, :], preferred_element_type=F32)
            for e in pair
        ]
        split_products(products, inner, top, pair[0])
    upper = scatter_sum(top, ghosts >> 8, hosts_ref, round_up(face_count, LANES) // LANES)
    upper = unstacked(upper, bands)[:, :face_count] / HALF_WIDTH
    upper_ref[...] = upper
    total = unstacked(scatter_sum(inner, slots_ref[...] >> 8, hots_ref, own // LANES, True), bands)
    current = (total - CENTER * psi_ref[...]) / HALF_WIDTH
    own_ref[...] = current
    face = face_ref[...]
    face_hot = one_hot(face & 255)
    low = pick(stacked(current).astype(BF16), face >> 8, face_hot, bands)
    odd = odd_domain()
    near_ref[...] = jnp.where(odd, low, upper).astype(BF16)
    far_ref[...] = jnp.where(odd, upper, low).astype(BF16)


def far_kernel(own_in, slots_ref, hots_ref, face_ref, low_ref, inside_ref, high_ref, faces_ref):
    bands, own = own_in.shape
    blocks = round_up(own // LANES, 16)
    face = face_ref[...]
    number = lax.broadcasted_iota(jnp.int32, (blocks, face.shape[1]), 1)
    held = lax.broadcasted_iota(jnp.int32, number.shape, 0) == (face >> 8)
    digits = [jnp.where(held, digit, 0).astype(F32).astype(BF16) for digit in ((number >> 8) + 1, number & 255)]
    face_hot = one_hot(face & 255)
    table = lax.dot_general(
        jnp.concatenate(digits, axis=0), face_hot, (((1,), (1,)), ((), ())), preferred_element_type=F32
    ).astype(BF16)
    rows, rest = halves(stacked(own_in[...]))
    low_ref[...] = pick(rows, face >> 8, face_hot, bands) + pick(rest, face >> 8, face_hot, bands)
    for tile in tiles(slots_ref.shape[1]):
        high = slots_ref[:, tile] >> 8
        hot = hots_ref[:, tile]
        both = jnp.dot(table, hot, preferred_element_type=F32)
        held = lax.broadcasted_iota(jnp.int32, (blocks, both.shape[1]), 0) == high
        block = jnp.sum(jnp.where(held, both[:blocks], 0.0), axis=0, keepdims=True).astype(jnp.int32)
        lane = jnp.sum(jnp.where(held, both[blocks:], 0.0), axis=0, keepdims=True).astype(jnp.int32)
        high_ref[:, tile] = block - 1
        faces_ref[:, tile] = one_hot(jnp.where(block > 0, lane, -1))
        inside_ref[:, tile] = jnp.where(block > 0, 0.0, pick(rows, high, hot, bands)).astype(BF16)


def second_kernel(
    inside_ref, high_ref, faces_ref, ghosts_ref, hosts_ref, ham_ref, low_in, upper_in, near_in, far_in,
    field_ref, upper_ref, inside, top, outside,
):
    bands, face_count = upper_in.shape
    elements, size = ham_ref.shape[:2]
    odd = odd_domain()
    near, far = near_in[...].astype(F32), far_in[...].astype(F32)
    below = jnp.where(odd, near, far)
    above = jnp.where(odd, far, near)
    faces = stacked(widened(low_in[...] + below)).astype(BF16)
    ghost = stacked(widened(upper_in[...] + above)).astype(BF16)
    ghosts = ghosts_ref[...]
    pick_into(outside, ghost, ghosts >> 8, hosts_ref)
    for tile in tiles(high_ref.shape[1]):
        extra = pick(faces, high_ref[:, tile], faces_ref[:, tile], bands)
        inside[:, tile] = inside_ref[:, tile] + extra.astype(BF16)
    for pair in pairs(elements):
        products = []
        for e in pair:
            values = jnp.concatenate(
                [inside[:, e * IN_EL : (e + 1) * IN_EL], outside[:, e * FACE_EL : (e + 1) * FACE_EL]], axis=1
            )
            field_ref[:, e * size : (e + 1) * size] = values
            product = jnp.dot(values, ham_ref[e, :, size - 128 :], preferred_element_type=F32)
            products.append(product[:, 128 - FACE_EL :])
        top[:, pair[0] * FACE_EL : (pair[-1] + 1) * FACE_EL] = jnp.concatenate(products, axis=1)
    total = unstacked(scatter_sum(top, ghosts >> 8, hosts_ref, round_up(face_count, LANES) // LANES), bands)
    upper_ref[...] = (total[:, :face_count] * (2.0 / HALF_WIDTH)).astype(BF16)


def third_kernel(
    psi_ref, slots_ref, hots_ref, ham_ref, face_ref, own_in, near_in, far_in, field_ref, own_ref, inner
):
    bands, own = own_in.shape
    elements, size = ham_ref.shape[:2]
    face = face_ref[...]
    below = jnp.where(odd_domain(), near_in[...].astype(F32), far_in[...].astype(F32))
    added = lane_sums(spread_once(below, face >> 8, own // LANES), one_hot(face & 255))
    for pair in pairs(elements):
        products = [
            jnp.dot(field_ref[:, e * size : (e + 1) * size], ham_ref[e], preferred_element_type=F32) for e in pair
        ]
        split_products(products, inner, None, pair[0])
    total = unstacked(scatter_sum(inner, slots_ref[...] >> 8, hots_ref, own // LANES, True), bands)
    current = own_in[...] + unstacked(added, bands)
    own_ref[...] = 2.0 * ((total - CENTER * current) / HALF_WIDTH) - psi_ref[...]


def last_kernel(own_in, face_ref, below_in, out_ref, short_ref):
    bands, own = own_in.shape
    face = face_ref[...]
    added = lane_sums(spread_once(below_in[...].astype(F32), face >> 8, own // LANES), one_hot(face & 255))
    total = own_in[...] + unstacked(added, bands)
    out_ref[...] = total
    short_ref[...] = total[:, : short_ref.shape[1]].astype(BF16)


def call(kernel, out_shape, inputs, scratch=(), flops=0, moved=0, far=()):
    return pl.pallas_call(
        kernel,
        out_shape=out_shape,
        in_specs=[HBM if i in far else VMEM for i in range(len(inputs))],
        out_specs=jax.tree.map(lambda _: VMEM, out_shape),
        scratch_shapes=list(scratch),
        compiler_params=pltpu.CompilerParams(vmem_limit_bytes=LIMIT),
        cost_estimate=pl.CostEstimate(flops=flops, bytes_accessed=moved, transcendentals=0),
    )(*inputs)


def from_behind(block, axis, distance):
    devices = range(lax.axis_size(axis))
    route = [((i - distance) % len(devices), i) for i in devices]
    return lax.ppermute(block, axis, route)


def paired(groups):
    return groups & (groups - 1) == 0


def partner(block, axis, distance):
    size = lax.axis_size(axis)
    if paired(size):
        return lax.ppermute(block, axis, [(i, i ^ distance) for i in range(size)])
    return from_behind(block, axis, distance)


def filter_field(psi, ham, conn, face_rows):
    bands, nodes = psi.shape
    elements, size = conn.shape
    own = round_up(nodes, LANES)
    faces = round_up(face_rows.shape[0], 128)
    trimmed = round_up(nodes, 128)
    face_count = elements * (size - IN_EL)
    inner_count = elements * IN_EL
    shape = jax.ShapeDtypeStruct
    face_field = shape((bands, faces), F32)
    own_field = shape((bands, own), F32)
    inner = pltpu.VMEM((bands, inner_count), F32)
    top = pltpu.VMEM((bands, face_count), F32)
    inside_field = pltpu.VMEM((bands, inner_count), BF16)
    outside = pltpu.VMEM((bands, face_count), BF16)

    with jax.named_scope("face_values"):
        values, wide, conn, face = call(
            face_kernel,
            (shape((bands, faces), BF16), own_field, shape(conn.shape, jnp.int32), shape((1, faces), jnp.int32)),
            [pltpu.with_memory_space_constraint(array, pltpu.HBM) for array in (psi, conn, face_rows)],
            (pltpu.VMEM(psi.shape, F32), pltpu.VMEM(face_rows.shape, jnp.int32), pltpu.SemaphoreType.DMA((3,))),
            far=(0, 1, 2), flops=2 * 10**10, moved=4 * 10**7,
        )
    ghost = from_behind(values, "space", -1)
    with jax.named_scope("interior"):
        part, slots, ghosts, hots, hosts = call(
            functools.partial(interior_kernel, nodes),
            (
                shape((bands, elements * size), F32),
                shape((1, inner_count), jnp.int32), shape((1, face_count), jnp.int32),
                shape((LANES, inner_count), BF16), shape((LANES, face_count), BF16),
            ),
            (wide, conn, ham), (inside_field,), flops=4 * 10**9, moved=8 * 10**6,
        )
    with jax.named_scope("first_step"):
        current, upper, to_near, to_far = call(
            first_kernel, (own_field, face_field, *[shape(face_field.shape, BF16)] * 2),
            (wide, slots, ghosts, hots, hosts, ham, face, ghost, part), (inner, top, outside),
            flops=4 * 10**9, moved=10**6,
        )
    domains = lax.axis_size("space")
    from_far = lax.ppermute(to_far, "space", [(i, ((i + 1 ^ 1) - 1) % domains) for i in range(domains)])
    from_near = lax.ppermute(to_near, "space", [(i, i ^ 1) for i in range(domains)])
    with jax.named_scope("off_face"):
        low, inside, high, faces = call(
            far_kernel,
            (face_field, shape((bands, inner_count), BF16), shape((1, inner_count), jnp.int32), shape((LANES, inner_count), BF16)),
            (current, slots, hots, face), flops=4 * 10**9, moved=10**6,
        )
    with jax.named_scope("second_step"):
        field, upper = call(
            second_kernel, (shape((bands, elements * size), BF16), shape(face_field.shape, BF16)),
            (inside, high, faces, ghosts, hosts, ham, low, upper, from_near, from_far), (inside_field, top, outside),
            flops=4 * 10**9, moved=10**6,
        )
    from_below = from_behind(upper, "space", 1)
    with jax.named_scope("second_sums"):
        following = call(
            third_kernel, own_field, (wide, slots, hots, ham, face, current, from_near, from_far, field), (inner,),
            flops=4 * 10**9, moved=8 * 10**6,
        )
    with jax.named_scope("last_faces"):
        return call(last_kernel, (own_field, shape((bands, trimmed), BF16)), (following, face, from_below))


def gram_kernel(*refs):
    *blocks, terms_ref, gram_ref = refs
    bands = blocks[0].shape[0]
    total = bands * len(blocks)
    me = lax.axis_index("band")
    for distance, block in enumerate(blocks):
        source = me ^ distance if paired(len(blocks)) else lax.rem(me - distance + len(blocks), len(blocks))
        source = pl.multiple_of(source * bands, bands)
        if distance == 0:
            upper, lower = halves(block[...])
            terms_ref[total:, :] = lower
        else:
            upper = widened(block[...])
        terms_ref[pl.ds(source, bands), :] = upper
    terms = terms_ref[...]
    both = lax.dot_general(terms, terms, (((1,), (1,)), ((), ())), preferred_element_type=F32)
    down = jnp.concatenate([both[total:]] * len(blocks), axis=0)
    across = jnp.concatenate([both[:, total:]] * len(blocks), axis=1)
    corner = jnp.concatenate([down[:, total:]] * len(blocks), axis=1)
    own_row = lax.broadcasted_iota(jnp.int32, (total, total), 0) // bands == me
    own_column = lax.broadcasted_iota(jnp.int32, (total, total), 1) // bands == me
    cross = jnp.where(own_row, down[:, :total], 0.0) + jnp.where(own_column, across[:total], 0.0)
    gram = both[:total, :total] + (cross + jnp.where(own_row & own_column, corner, 0.0))
    gram_ref[...] = jnp.concatenate([gram[: total // 2], gram[total // 2 :]], axis=1)


def inverse_factor(matrix, block=16):
    size = matrix.shape[0]
    width = 2 * size
    lane = lax.broadcasted_iota(jnp.int32, (8, width), 1)
    row = lax.broadcasted_iota(jnp.int32, (8, width), 0)
    wide = jnp.concatenate([matrix, jnp.zeros((size, size), F32)], axis=1)
    groups = [wide[8 * g : 8 * g + 8] + jnp.where(lane == row + (size + 8 * g), 1.0, 0.0) for g in range(size // 8)]
    for k in range(0, size, block):
        columns = [
            {g: jnp.broadcast_to(groups[g][:, j : j + 1], (8, width)) for g in range(k // 8, size // 8)}
            for j in range(k, k + block)
        ]
        for q in range(block):
            first, at = divmod(k + q, 8)
            scale = 1.0 / columns[q][first][at : at + 1]
            column = {g: rows for g, rows in columns[q].items() if g >= first}
            column[first] = jnp.where(row > at, column[first], 0.0)
            for p in range(q + 1, block):
                factor = columns[p][first][at : at + 1] * scale
                for g, weight in column.items():
                    columns[p][g] = columns[p][g] - weight * factor
            factor = groups[first][at : at + 1] * scale
            for g, weight in column.items():
                groups[g] = groups[g] - weight * factor
    out = []
    for g, rows in enumerate(groups):
        pivot = jnp.sum(jnp.where(lane == row + 8 * g, rows, 0.0), axis=1, keepdims=True)
        out.append(rows[:, size:] / jnp.sqrt(pivot))
    return jnp.concatenate(out, axis=0)


def ortho_kernel(nodes, count, gram_ref, terms_ref, out_ref, inverse_ref):
    bands = out_ref.shape[0]
    total = inverse_ref.shape[0]
    gram = jnp.concatenate([gram_ref[:, :total], gram_ref[:, total:]], axis=0)
    inverse_ref[...] = inverse_factor(gram / count)
    first = pl.multiple_of(lax.axis_index("band") * bands, bands)
    own = inverse_ref[pl.ds(first, bands), :]
    column = lax.broadcasted_iota(jnp.int32, own.shape, 1)
    diagonal = jnp.where(column // bands == lax.axis_index("band"), own, 0.0)
    diagonal = sum(diagonal[:, i : i + bands] for i in range(0, total, bands))
    rows = jnp.concatenate(halves(jnp.concatenate([own, diagonal], axis=1)), axis=0)
    both = jnp.dot(rows, terms_ref[...], preferred_element_type=F32)
    out_ref[...] = (both[:bands] + both[bands:])[:, :nodes]


def space_sum(block):
    size = lax.axis_size("space")
    if size & (size - 1):
        return lax.psum(block, "space")
    step = 1
    while step < size:
        span = 2 if step == 1 or step * 2 == size else 4
        parts = [
            lax.ppermute(block, "space", [(i, i ^ (step * k)) for i in range(size)]) for k in range(1, span)
        ]
        block = sum(parts, block)
        step *= span
    return block


def per_device(psi, ham, conn, face_rows):
    bands, nodes = psi.shape
    following, short = filter_field(psi, ham, conn, face_rows)
    groups = lax.axis_size("band")
    total = groups * bands
    own = round_up(nodes, LANES)
    shape = jax.ShapeDtypeStruct
    blocks = [following] + [partner(short, "band", i) for i in range(1, groups)]
    with jax.named_scope("gram"):
        terms, gram = call(gram_kernel, (shape((total + bands, own), BF16), shape((total // 2, 2 * total), F32)), blocks)
    with jax.named_scope("gram_sum"):
        gram = space_sum(gram)
    with jax.named_scope("orthonormal"):
        return call(
            functools.partial(ortho_kernel, nodes, nodes * lax.axis_size("space")),
            shape((bands, nodes), F32), (gram, terms), (pltpu.VMEM((total, total), F32),),
        )


def solution(mesh):
    placed = (P("band", "space"), P("space", None, None), P("space", None), P("space"))
    return jax.shard_map(
        per_device, mesh=mesh, in_specs=placed, out_specs=P("band", "space"), check_vma=False
    )
```

```python
import functools

import jax
import jax.numpy as jnp
from jax import lax
from jax.experimental import pallas as pl
from jax.experimental.pallas import tpu as pltpu
from jax.sharding import PartitionSpec as P

FACE_EL = 64
IN_EL = 448
LANES = 256

CENTER = 6.25
HALF_WIDTH = 7.5

F32 = jnp.float32
BF16 = jnp.bfloat16
VMEM = pl.BlockSpec(memory_space=pltpu.VMEM)
HBM = pl.BlockSpec(memory_space=pltpu.HBM)
LIMIT = 24 * 1024 * 1024


def round_up(count, unit):
    return -(-count // unit) * unit


def one_hot(low):
    rows = lax.broadcasted_iota(jnp.int32, (LANES, low.shape[1]), 0)
    return jnp.where(rows == low, 1.0, 0.0).astype(BF16)


def stacked(field):
    blocks = field.shape[1] // LANES
    return jnp.concatenate([field[:, i * LANES : (i + 1) * LANES] for i in range(blocks)], axis=0)


def unstacked(rows, bands):
    blocks = rows.shape[0] // bands
    return jnp.concatenate([rows[i * bands : (i + 1) * bands] for i in range(blocks)], axis=1)


def pick(rows, high, low_hot, bands, first=0):
    table = jnp.dot(rows, low_hot, preferred_element_type=F32)
    out = jnp.zeros((bands, low_hot.shape[1]), F32)
    for i in range(rows.shape[0] // bands):
        out = jnp.where(high == i + first, table[i * bands : (i + 1) * bands], out)
    return out


def halves(values):
    upper = values.astype(BF16)
    return upper, (values - upper.astype(F32)).astype(BF16)


def spread(values, high, blocks, first=0):
    rows = []
    for part in halves(values):
        wide = part.astype(F32)
        for i in range(blocks):
            rows.append(jnp.where(high == i + first, wide, 0.0).astype(BF16))
    return jnp.concatenate(rows, axis=0)


def lane_sums(rows, low_hot):
    return lax.dot_general(rows, low_hot, (((1,), (1,)), ((), ())), preferred_element_type=F32)


def tiles(count, width=LANES):
    return [slice(start, min(start + width, count)) for start in range(0, count, width)]


def hot_into(hots_ref, low):
    for tile in tiles(low.shape[1]):
        hots_ref[:, tile] = one_hot(low[:, tile])


def pick_into(out_ref, rows, high, hots_ref):
    for tile in tiles(high.shape[1]):
        out_ref[:, tile] = pick(rows, high[:, tile], hots_ref[:, tile], out_ref.shape[0]).astype(out_ref.dtype)


def spread_once(values, high, blocks):
    return jnp.concatenate([jnp.where(high == i, values, 0.0).astype(BF16) for i in range(blocks)], axis=0)


def scatter_sum(values_ref, high, hots_ref, blocks, once=False):
    total = None
    for tile in tiles(high.shape[1], 2 * LANES):
        rows = (spread_once if once else spread)(values_ref[:, tile], high[:, tile], blocks)
        part = lax.dot_general(
            rows, hots_ref[:, tile],
            (((1,), (1,)), ((), ())), preferred_element_type=F32,
        )
        total = part if total is None else total + part
    if once:
        return total
    count = total.shape[0] // 2
    return total[:count] + total[count:]


def split_products(products, inner_ref, top_ref, first):
    inner = jnp.concatenate([product[:, :IN_EL] for product in products], axis=1)
    top = jnp.concatenate([product[:, IN_EL:] for product in products], axis=1)
    inner_ref[:, first * IN_EL : first * IN_EL + inner.shape[1]] = inner
    if top_ref is not None:
        top_ref[:, first * FACE_EL : first * FACE_EL + top.shape[1]] = top


def pairs(elements):
    return [range(e, min(e + 2, elements)) for e in range(0, elements, 2)]


def packed(ref, width, first, last):
    return jnp.concatenate([ref[e : e + 1, first:last] for e in range(width)], axis=1)


def face_kernel(psi_hbm, conn_hbm, face_hbm, values_ref, psi_out, conn_out, face_out, psi_ref, face_ref, sems):
    bands, nodes = psi_hbm.shape
    copies = [
        pltpu.make_async_copy(face_hbm, face_ref, sems.at[0]),
        pltpu.make_async_copy(psi_hbm, psi_ref, sems.at[1]),
        pltpu.make_async_copy(conn_hbm, conn_out, sems.at[2]),
    ]
    for copy in copies:
        copy.start()
    psi_out[...] = jnp.zeros_like(psi_out)
    face_out[...] = jnp.full_like(face_out, -1)
    copies[0].wait()
    face_out[:, : face_ref.shape[0]] = face_ref[...].reshape(1, face_ref.shape[0])
    face = face_out[...]
    hot = one_hot(face & 255)
    copies[1].wait()
    psi_out[:, :nodes] = psi_ref[...]
    values_ref[...] = pick(stacked(psi_out[...]).astype(BF16), face >> 8, hot, bands).astype(BF16)
    copies[2].wait()


def near_kernel(nodes, psi_ref, conn_ref, inside_ref, slots_ref, ghosts_ref, hots_ref, hosts_ref):
    elements, size = conn_ref.shape
    slots_ref[...] = packed(conn_ref, elements, 0, IN_EL)
    ghosts_ref[...] = packed(conn_ref, elements, IN_EL, size) - nodes
    hot_into(hosts_ref, ghosts_ref[...] & 255)
    slots = slots_ref[...]
    hot_into(hots_ref, slots & 255)
    pick_into(inside_ref, stacked(psi_ref[...]).astype(BF16), slots >> 8, hots_ref)


def interior_kernel(inside_ref, ham_ref, part_ref):
    elements, size = ham_ref.shape[:2]
    for e in range(elements):
        part_ref[:, e * size : (e + 1) * size] = jnp.dot(
            inside_ref[:, e * IN_EL : (e + 1) * IN_EL], ham_ref[e, :IN_EL, :], preferred_element_type=F32
        )


def widened(values):
    bands, count = values.shape
    if count % LANES == 0:
        return values
    return jnp.concatenate([values, jnp.zeros((bands, round_up(count, LANES) - count), values.dtype)], axis=1)


def odd_domain():
    return lax.rem(lax.axis_index("space"), 2) == 1


def first_kernel(
    psi_ref, slots_ref, ghosts_ref, hots_ref, hosts_ref, ham_ref, face_ref, ghost_ref, part_ref,
    own_ref, upper_ref, near_ref, far_ref, inner, top, outside,
):
    bands, own = psi_ref.shape
    elements, size = ham_ref.shape[:2]
    face_count = ghost_ref.shape[1]
    ghosts = ghosts_ref[...]
    pick_into(outside, stacked(widened(ghost_ref[...])), ghosts >> 8, hosts_ref)
    for pair in pairs(elements):
        products = [
            part_ref[:, e * size : (e + 1) * size]
            + jnp.dot(outside[:, e * FACE_EL : (e + 1) * FACE_EL], ham_ref[e, IN_EL:, :], preferred_element_type=F32)
            for e in pair
        ]
        split_products(products, inner, top, pair[0])
    upper = scatter_sum(top, ghosts >> 8, hosts_ref, round_up(face_count, LANES) // LANES)
    upper = unstacked(upper, bands)[:, :face_count] / HALF_WIDTH
    upper_ref[...] = upper
    total = unstacked(scatter_sum(inner, slots_ref[...] >> 8, hots_ref, own // LANES, True), bands)
    current = (total - CENTER * psi_ref[...]) / HALF_WIDTH
    own_ref[...] = current
    face = face_ref[...]
    face_hot = one_hot(face & 255)
    low = pick(stacked(current).astype(BF16), face >> 8, face_hot, bands)
    odd = odd_domain()
    near_ref[...] = jnp.where(odd, low, upper).astype(BF16)
    far_ref[...] = jnp.where(odd, upper, low).astype(BF16)


def far_kernel(own_in, slots_ref, hots_ref, face_ref, low_ref, inside_ref, high_ref, faces_ref):
    bands, own = own_in.shape
    blocks = round_up(own // LANES, 16)
    face = face_ref[...]
    number = lax.broadcasted_iota(jnp.int32, (blocks, face.shape[1]), 1)
    held = lax.broadcasted_iota(jnp.int32, number.shape, 0) == (face >> 8)
    digits = [jnp.where(held, digit, 0).astype(F32).astype(BF16) for digit in ((number >> 8) + 1, number & 255)]
    face_hot = one_hot(face & 255)
    table = lax.dot_general(
        jnp.concatenate(digits, axis=0), face_hot, (((1,), (1,)), ((), ())), preferred_element_type=F32
    ).astype(BF16)
    rows, rest = halves(stacked(own_in[...]))
    low_ref[...] = pick(rows, face >> 8, face_hot, bands) + pick(rest, face >> 8, face_hot, bands)
    for tile in tiles(slots_ref.shape[1]):
        high = slots_ref[:, tile] >> 8
        hot = hots_ref[:, tile]
        both = jnp.dot(table, hot, preferred_element_type=F32)
        held = lax.broadcasted_iota(jnp.int32, (blocks, both.shape[1]), 0) == high
        block = jnp.sum(jnp.where(held, both[:blocks], 0.0), axis=0, keepdims=True).astype(jnp.int32)
        lane = jnp.sum(jnp.where(held, both[blocks:], 0.0), axis=0, keepdims=True).astype(jnp.int32)
        high_ref[:, tile] = block - 1
        faces_ref[:, tile] = one_hot(jnp.where(block > 0, lane, -1))
        inside_ref[:, tile] = jnp.where(block > 0, 0.0, pick(rows, high, hot, bands)).astype(BF16)


def second_kernel(
    inside_ref, high_ref, faces_ref, ghosts_ref, hosts_ref, ham_ref, low_in, upper_in, near_in, far_in,
    field_ref, upper_ref, inside, top, outside,
):
    bands, face_count = upper_in.shape
    elements, size = ham_ref.shape[:2]
    odd = odd_domain()
    near, far = near_in[...].astype(F32), far_in[...].astype(F32)
    below = jnp.where(odd, near, far)
    above = jnp.where(odd, far, near)
    faces = stacked(widened(low_in[...] + below)).astype(BF16)
    ghost = stacked(widened(upper_in[...] + above)).astype(BF16)
    ghosts = ghosts_ref[...]
    pick_into(outside, ghost, ghosts >> 8, hosts_ref)
    for tile in tiles(high_ref.shape[1]):
        extra = pick(faces, high_ref[:, tile], faces_ref[:, tile], bands)
        inside[:, tile] = inside_ref[:, tile] + extra.astype(BF16)
    for pair in pairs(elements):
        products = []
        for e in pair:
            values = jnp.concatenate(
                [inside[:, e * IN_EL : (e + 1) * IN_EL], outside[:, e * FACE_EL : (e + 1) * FACE_EL]], axis=1
            )
            field_ref[:, e * size : (e + 1) * size] = values
            product = jnp.dot(values, ham_ref[e, :, size - 128 :], preferred_element_type=F32)
            products.append(product[:, 128 - FACE_EL :])
        top[:, pair[0] * FACE_EL : (pair[-1] + 1) * FACE_EL] = jnp.concatenate(products, axis=1)
    total = unstacked(scatter_sum(top, ghosts >> 8, hosts_ref, round_up(face_count, LANES) // LANES), bands)
    upper_ref[...] = (total[:, :face_count] * (2.0 / HALF_WIDTH)).astype(BF16)


def third_kernel(
    psi_ref, slots_ref, hots_ref, ham_ref, face_ref, own_in, near_in, far_in, field_ref, own_ref, inner
):
    bands, own = own_in.shape
    elements, size = ham_ref.shape[:2]
    face = face_ref[...]
    below = jnp.where(odd_domain(), near_in[...].astype(F32), far_in[...].astype(F32))
    added = lane_sums(spread_once(below, face >> 8, own // LANES), one_hot(face & 255))
    for pair in pairs(elements):
        products = [
            jnp.dot(field_ref[:, e * size : (e + 1) * size], ham_ref[e], preferred_element_type=F32) for e in pair
        ]
        split_products(products, inner, None, pair[0])
    total = unstacked(scatter_sum(inner, slots_ref[...] >> 8, hots_ref, own // LANES, True), bands)
    current = own_in[...] + unstacked(added, bands)
    own_ref[...] = 2.0 * ((total - CENTER * current) / HALF_WIDTH) - psi_ref[...]


def last_kernel(own_in, face_ref, below_in, out_ref, short_ref):
    bands, own = own_in.shape
    face = face_ref[...]
    added = lane_sums(spread_once(below_in[...].astype(F32), face >> 8, own // LANES), one_hot(face & 255))
    total = own_in[...] + unstacked(added, bands)
    out_ref[...] = total
    short_ref[...] = total[:, : short_ref.shape[1]].astype(BF16)


def call(kernel, out_shape, inputs, scratch=(), flops=0, moved=0, far=()):
    return pl.pallas_call(
        kernel,
        out_shape=out_shape,
        in_specs=[HBM if i in far else VMEM for i in range(len(inputs))],
        out_specs=jax.tree.map(lambda _: VMEM, out_shape),
        scratch_shapes=list(scratch),
        compiler_params=pltpu.CompilerParams(vmem_limit_bytes=LIMIT),
        cost_estimate=pl.CostEstimate(flops=flops, bytes_accessed=moved, transcendentals=0),
    )(*inputs)


def from_behind(block, axis, distance):
    devices = range(lax.axis_size(axis))
    route = [((i - distance) % len(devices), i) for i in devices]
    return lax.ppermute(block, axis, route)


def paired(groups):
    return groups & (groups - 1) == 0


def partner(block, axis, distance):
    size = lax.axis_size(axis)
    if paired(size):
        return lax.ppermute(block, axis, [(i, i ^ distance) for i in range(size)])
    return from_behind(block, axis, distance)


def filter_field(psi, ham, conn, face_rows):
    bands, nodes = psi.shape
    elements, size = conn.shape
    own = round_up(nodes, LANES)
    faces = round_up(face_rows.shape[0], 128)
    trimmed = round_up(nodes, 128)
    face_count = elements * (size - IN_EL)
    inner_count = elements * IN_EL
    shape = jax.ShapeDtypeStruct
    face_field = shape((bands, faces), F32)
    own_field = shape((bands, own), F32)
    inner = pltpu.VMEM((bands, inner_count), F32)
    top = pltpu.VMEM((bands, face_count), F32)
    inside_field = pltpu.VMEM((bands, inner_count), BF16)
    outside = pltpu.VMEM((bands, face_count), BF16)

    with jax.named_scope("face_values"):
        values, wide, conn, face = call(
            face_kernel,
            (shape((bands, faces), BF16), own_field, shape(conn.shape, jnp.int32), shape((1, faces), jnp.int32)),
            [pltpu.with_memory_space_constraint(array, pltpu.HBM) for array in (psi, conn, face_rows)],
            (pltpu.VMEM(psi.shape, F32), pltpu.VMEM(face_rows.shape, jnp.int32), pltpu.SemaphoreType.DMA((3,))),
            far=(0, 1, 2), flops=2 * 10**10, moved=4 * 10**7,
        )
    ghost = from_behind(values, "space", -1)
    with jax.named_scope("near_values"):
        inside, slots, ghosts, hots, hosts = call(
            functools.partial(near_kernel, nodes),
            (
                shape((bands, inner_count), BF16), shape((1, inner_count), jnp.int32), shape((1, face_count), jnp.int32),
                shape((LANES, inner_count), BF16), shape((LANES, face_count), BF16),
            ),
            (wide, conn),
        )
    with jax.named_scope("interior"):
        part = call(
            interior_kernel, shape((bands, elements * size), F32), (inside, ham), flops=4 * 10**9, moved=8 * 10**6
        )
    with jax.named_scope("first_step"):
        current, upper, to_near, to_far = call(
            first_kernel, (own_field, face_field, *[shape(face_field.shape, BF16)] * 2),
            (wide, slots, ghosts, hots, hosts, ham, face, ghost, part), (inner, top, outside),
            flops=4 * 10**9, moved=10**6,
        )
    domains = lax.axis_size("space")
    from_far = lax.ppermute(to_far, "space", [(i, ((i + 1 ^ 1) - 1) % domains) for i in range(domains)])
    from_near = lax.ppermute(to_near, "space", [(i, i ^ 1) for i in range(domains)])
    with jax.named_scope("off_face"):
        low, inside, high, faces = call(
            far_kernel,
            (face_field, shape((bands, inner_count), BF16), shape((1, inner_count), jnp.int32), shape((LANES, inner_count), BF16)),
            (current, slots, hots, face), flops=4 * 10**9, moved=10**6,
        )
    with jax.named_scope("second_step"):
        field, upper = call(
            second_kernel, (shape((bands, elements * size), BF16), shape(face_field.shape, BF16)),
            (inside, high, faces, ghosts, hosts, ham, low, upper, from_near, from_far), (inside_field, top, outside),
            flops=4 * 10**9, moved=10**6,
        )
    from_below = from_behind(upper, "space", 1)
    with jax.named_scope("second_sums"):
        following = call(
            third_kernel, own_field, (wide, slots, hots, ham, face, current, from_near, from_far, field), (inner,),
            flops=4 * 10**9, moved=8 * 10**6,
        )
    with jax.named_scope("last_faces"):
        return call(last_kernel, (own_field, shape((bands, trimmed), BF16)), (following, face, from_below))


def gram_kernel(*refs):
    *blocks, terms_ref, gram_ref = refs
    bands = blocks[0].shape[0]
    total = bands * len(blocks)
    me = lax.axis_index("band")
    for distance, block in enumerate(blocks):
        source = me ^ distance if paired(len(blocks)) else lax.rem(me - distance + len(blocks), len(blocks))
        source = pl.multiple_of(source * bands, bands)
        if distance == 0:
            upper, lower = halves(block[...])
            terms_ref[total:, :] = lower
        else:
            upper = widened(block[...])
        terms_ref[pl.ds(source, bands), :] = upper
    terms = terms_ref[...]
    both = lax.dot_general(terms, terms, (((1,), (1,)), ((), ())), preferred_element_type=F32)
    down = jnp.concatenate([both[total:]] * len(blocks), axis=0)
    across = jnp.concatenate([both[:, total:]] * len(blocks), axis=1)
    corner = jnp.concatenate([down[:, total:]] * len(blocks), axis=1)
    own_row = lax.broadcasted_iota(jnp.int32, (total, total), 0) // bands == me
    own_column = lax.broadcasted_iota(jnp.int32, (total, total), 1) // bands == me
    cross = jnp.where(own_row, down[:, :total], 0.0) + jnp.where(own_column, across[:total], 0.0)
    gram = both[:total, :total] + (cross + jnp.where(own_row & own_column, corner, 0.0))
    gram_ref[...] = jnp.concatenate([gram[: total // 2], gram[total // 2 :]], axis=1)


def inverse_factor(matrix, block=16):
    size = matrix.shape[0]
    width = 2 * size
    lane = lax.broadcasted_iota(jnp.int32, (8, width), 1)
    row = lax.broadcasted_iota(jnp.int32, (8, width), 0)
    wide = jnp.concatenate([matrix, jnp.zeros((size, size), F32)], axis=1)
    groups = [wide[8 * g : 8 * g + 8] + jnp.where(lane == row + (size + 8 * g), 1.0, 0.0) for g in range(size // 8)]
    for k in range(0, size, block):
        columns = [
            {g: jnp.broadcast_to(groups[g][:, j : j + 1], (8, width)) for g in range(k // 8, size // 8)}
            for j in range(k, k + block)
        ]
        for q in range(block):
            first, at = divmod(k + q, 8)
            scale = 1.0 / columns[q][first][at : at + 1]
            column = {g: rows for g, rows in columns[q].items() if g >= first}
            column[first] = jnp.where(row > at, column[first], 0.0)
            for p in range(q + 1, block):
                factor = columns[p][first][at : at + 1] * scale
                for g, weight in column.items():
                    columns[p][g] = columns[p][g] - weight * factor
            factor = groups[first][at : at + 1] * scale
            for g, weight in column.items():
                groups[g] = groups[g] - weight * factor
    out = []
    for g, rows in enumerate(groups):
        pivot = jnp.sum(jnp.where(lane == row + 8 * g, rows, 0.0), axis=1, keepdims=True)
        out.append(rows[:, size:] / jnp.sqrt(pivot))
    return jnp.concatenate(out, axis=0)


def ortho_kernel(nodes, count, gram_ref, terms_ref, out_ref, inverse_ref):
    bands = out_ref.shape[0]
    total = inverse_ref.shape[0]
    gram = jnp.concatenate([gram_ref[:, :total], gram_ref[:, total:]], axis=0)
    inverse_ref[...] = inverse_factor(gram / count)
    first = pl.multiple_of(lax.axis_index("band") * bands, bands)
    own = inverse_ref[pl.ds(first, bands), :]
    column = lax.broadcasted_iota(jnp.int32, own.shape, 1)
    diagonal = jnp.where(column // bands == lax.axis_index("band"), own, 0.0)
    diagonal = sum(diagonal[:, i : i + bands] for i in range(0, total, bands))
    rows = jnp.concatenate(halves(jnp.concatenate([own, diagonal], axis=1)), axis=0)
    both = jnp.dot(rows, terms_ref[...], preferred_element_type=F32)
    out_ref[...] = (both[:bands] + both[bands:])[:, :nodes]


def space_sum(block):
    size = lax.axis_size("space")
    if size & (size - 1):
        return lax.psum(block, "space")
    step = 1
    while step < size:
        span = 2 if step == 1 or step * 2 == size else 4
        parts = [
            lax.ppermute(block, "space", [(i, i ^ (step * k)) for i in range(size)]) for k in range(1, span)
        ]
        block = sum(parts, block)
        step *= span
    return block


def per_device(psi, ham, conn, face_rows):
    bands, nodes = psi.shape
    following, short = filter_field(psi, ham, conn, face_rows)
    groups = lax.axis_size("band")
    total = groups * bands
    own = round_up(nodes, LANES)
    shape = jax.ShapeDtypeStruct
    blocks = [following] + [partner(short, "band", i) for i in range(1, groups)]
    with jax.named_scope("gram"):
        terms, gram = call(gram_kernel, (shape((total + bands, own), BF16), shape((total // 2, 2 * total), F32)), blocks)
    with jax.named_scope("gram_sum"):
        gram = space_sum(gram)
    with jax.named_scope("orthonormal"):
        return call(
            functools.partial(ortho_kernel, nodes, nodes * lax.axis_size("space")),
            shape((bands, nodes), F32), (gram, terms), (pltpu.VMEM((total, total), F32),),
        )


def solution(mesh):
    placed = (P("band", "space"), P("space", None, None), P("space", None), P("space"))
    return jax.shard_map(
        per_device, mesh=mesh, in_specs=placed, out_specs=P("band", "space"), check_vma=False
    )
```

```python
import functools

import jax
import jax.numpy as jnp
from jax import lax
from jax.experimental import pallas as pl
from jax.experimental.pallas import tpu as pltpu
from jax.sharding import PartitionSpec as P

FACE_EL = 64
IN_EL = 448
LANES = 256
FACE_LANES = 128

CENTER = 6.25
HALF_WIDTH = 7.5

F32 = jnp.float32
BF16 = jnp.bfloat16
VMEM = pl.BlockSpec(memory_space=pltpu.VMEM)
HBM = pl.BlockSpec(memory_space=pltpu.HBM)
LIMIT = 24 * 1024 * 1024


def round_up(count, unit):
    return -(-count // unit) * unit


def one_hot(low, lanes=LANES):
    rows = lax.broadcasted_iota(jnp.int32, (lanes, low.shape[1]), 0)
    return jnp.where(rows == low, 1.0, 0.0).astype(BF16)


def stacked(field, lanes=LANES):
    blocks = field.shape[1] // lanes
    return jnp.concatenate([field[:, i * lanes : (i + 1) * lanes] for i in range(blocks)], axis=0)


def unstacked(rows, bands):
    blocks = rows.shape[0] // bands
    return jnp.concatenate([rows[i * bands : (i + 1) * bands] for i in range(blocks)], axis=1)


def pick(rows, high, low_hot, bands, first=0):
    table = jnp.dot(rows, low_hot, preferred_element_type=F32)
    out = jnp.zeros((bands, low_hot.shape[1]), F32)
    for i in range(rows.shape[0] // bands):
        out = jnp.where(high == i + first, table[i * bands : (i + 1) * bands], out)
    return out


def halves(values):
    upper = values.astype(BF16)
    return upper, (values - upper.astype(F32)).astype(BF16)


def spread(values, high, blocks, first=0):
    rows = []
    for part in halves(values):
        wide = part.astype(F32)
        for i in range(blocks):
            rows.append(jnp.where(high == i + first, wide, 0.0).astype(BF16))
    return jnp.concatenate(rows, axis=0)


def lane_sums(rows, low_hot):
    return lax.dot_general(rows, low_hot, (((1,), (1,)), ((), ())), preferred_element_type=F32)


def tiles(count, width=LANES):
    return [slice(start, min(start + width, count)) for start in range(0, count, width)]


def hot_into(hots_ref, low):
    for tile in tiles(low.shape[1]):
        hots_ref[:, tile] = one_hot(low[:, tile])


def pick_into(out_ref, rows, high, hots_ref):
    for tile in tiles(high.shape[1]):
        out_ref[:, tile] = pick(rows, high[:, tile], hots_ref[:, tile], out_ref.shape[0]).astype(out_ref.dtype)


def spread_once(values, high, blocks):
    return jnp.concatenate([jnp.where(high == i, values, 0.0).astype(BF16) for i in range(blocks)], axis=0)


def scatter_sum(values_ref, high, hots_ref, blocks, once=False):
    total = None
    for tile in tiles(high.shape[1], 2 * LANES):
        rows = (spread_once if once else spread)(values_ref[:, tile], high[:, tile], blocks)
        part = lax.dot_general(
            rows, hots_ref[:, tile],
            (((1,), (1,)), ((), ())), preferred_element_type=F32,
        )
        total = part if total is None else total + part
    if once:
        return total
    count = total.shape[0] // 2
    return total[:count] + total[count:]


def split_products(products, inner_ref, top_ref, first):
    inner = jnp.concatenate([product[:, :IN_EL] for product in products], axis=1)
    top = jnp.concatenate([product[:, IN_EL:] for product in products], axis=1)
    inner_ref[:, first * IN_EL : first * IN_EL + inner.shape[1]] = inner
    if top_ref is not None:
        top_ref[:, first * FACE_EL : first * FACE_EL + top.shape[1]] = top


def pairs(elements):
    return [range(e, min(e + 2, elements)) for e in range(0, elements, 2)]


def packed(ref, width, first, last):
    return jnp.concatenate([ref[e : e + 1, first:last] for e in range(width)], axis=1)


def face_kernel(psi_hbm, conn_hbm, face_hbm, values_ref, psi_out, conn_out, face_out, psi_ref, face_ref, sems):
    bands, nodes = psi_hbm.shape
    copies = [
        pltpu.make_async_copy(face_hbm, face_ref, sems.at[0]),
        pltpu.make_async_copy(psi_hbm, psi_ref, sems.at[1]),
        pltpu.make_async_copy(conn_hbm, conn_out, sems.at[2]),
    ]
    for copy in copies:
        copy.start()
    psi_out[...] = jnp.zeros_like(psi_out)
    face_out[...] = jnp.full_like(face_out, -1)
    copies[0].wait()
    face_out[:, : face_ref.shape[0]] = face_ref[...].reshape(1, face_ref.shape[0])
    face = face_out[...]
    hot = one_hot(face & 255)
    copies[1].wait()
    psi_out[:, :nodes] = psi_ref[...]
    values_ref[...] = pick(stacked(psi_out[...]).astype(BF16), face >> 8, hot, bands).astype(BF16)
    copies[2].wait()


def near_kernel(nodes, psi_ref, conn_ref, inside_ref, slots_ref, ghosts_ref, hots_ref, hosts_ref):
    elements, size = conn_ref.shape
    slots_ref[...] = packed(conn_ref, elements, 0, IN_EL)
    ghosts_ref[...] = packed(conn_ref, elements, IN_EL, size) - nodes
    hot_into(hosts_ref, ghosts_ref[...] & 255)
    slots = slots_ref[...]
    hot_into(hots_ref, slots & 255)
    pick_into(inside_ref, stacked(psi_ref[...]).astype(BF16), slots >> 8, hots_ref)


def interior_kernel(inside_ref, ham_ref, part_ref):
    elements, size = ham_ref.shape[:2]
    for e in range(elements):
        part_ref[:, e * size : (e + 1) * size] = jnp.dot(
            inside_ref[:, e * IN_EL : (e + 1) * IN_EL], ham_ref[e, :IN_EL, :], preferred_element_type=F32
        )


def widened(values):
    bands, count = values.shape
    if count % LANES == 0:
        return values
    return jnp.concatenate([values, jnp.zeros((bands, round_up(count, LANES) - count), values.dtype)], axis=1)


def odd_domain():
    return lax.rem(lax.axis_index("space"), 2) == 1


def first_kernel(
    psi_ref, slots_ref, ghosts_ref, hots_ref, hosts_ref, ham_ref, face_ref, ghost_ref, part_ref,
    own_ref, upper_ref, near_ref, far_ref, inner, top, outside,
):
    bands, own = psi_ref.shape
    elements, size = ham_ref.shape[:2]
    face_count = ghost_ref.shape[1]
    ghosts = ghosts_ref[...]
    pick_into(outside, stacked(widened(ghost_ref[...])), ghosts >> 8, hosts_ref)
    for pair in pairs(elements):
        products = [
            part_ref[:, e * size : (e + 1) * size]
            + jnp.dot(outside[:, e * FACE_EL : (e + 1) * FACE_EL], ham_ref[e, IN_EL:, :], preferred_element_type=F32)
            for e in pair
        ]
        split_products(products, inner, top, pair[0])
    upper = scatter_sum(top, ghosts >> 8, hosts_ref, round_up(face_count, LANES) // LANES)
    upper = unstacked(upper, bands)[:, :face_count] / HALF_WIDTH
    upper_ref[...] = upper
    total = unstacked(scatter_sum(inner, slots_ref[...] >> 8, hots_ref, own // LANES, True), bands)
    current = (total - CENTER * psi_ref[...]) / HALF_WIDTH
    own_ref[...] = current
    face = face_ref[...]
    face_hot = one_hot(face & 255)
    low = pick(stacked(current).astype(BF16), face >> 8, face_hot, bands)
    odd = odd_domain()
    near_ref[...] = jnp.where(odd, low, upper).astype(BF16)
    far_ref[...] = jnp.where(odd, upper, low).astype(BF16)


def far_kernel(own_in, slots_ref, hots_ref, face_ref, low_ref, inside_ref, high_ref, faces_ref):
    bands, own = own_in.shape
    blocks = round_up(own // LANES, 16)
    face = face_ref[...]
    number = lax.broadcasted_iota(jnp.int32, (blocks, face.shape[1]), 1)
    held = lax.broadcasted_iota(jnp.int32, number.shape, 0) == (face >> 8)
    digits = [jnp.where(held, digit, 0).astype(F32).astype(BF16) for digit in (number // FACE_LANES + 1, number % FACE_LANES)]
    face_hot = one_hot(face & 255)
    table = lax.dot_general(
        jnp.concatenate(digits, axis=0), face_hot, (((1,), (1,)), ((), ())), preferred_element_type=F32
    ).astype(BF16)
    rows, rest = halves(stacked(own_in[...]))
    low_ref[...] = pick(rows, face >> 8, face_hot, bands) + pick(rest, face >> 8, face_hot, bands)
    for tile in tiles(slots_ref.shape[1]):
        high = slots_ref[:, tile] >> 8
        hot = hots_ref[:, tile]
        both = jnp.dot(table, hot, preferred_element_type=F32)
        held = lax.broadcasted_iota(jnp.int32, (blocks, both.shape[1]), 0) == high
        block = jnp.sum(jnp.where(held, both[:blocks], 0.0), axis=0, keepdims=True).astype(jnp.int32)
        lane = jnp.sum(jnp.where(held, both[blocks:], 0.0), axis=0, keepdims=True).astype(jnp.int32)
        high_ref[:, tile] = block - 1
        faces_ref[:, tile] = one_hot(jnp.where(block > 0, lane, -1), FACE_LANES)
        inside_ref[:, tile] = jnp.where(block > 0, 0.0, pick(rows, high, hot, bands)).astype(BF16)


def second_kernel(
    inside_ref, high_ref, faces_ref, ghosts_ref, hosts_ref, ham_ref, low_in, upper_in, near_in, far_in,
    field_ref, upper_ref, inside, top, outside,
):
    bands, face_count = upper_in.shape
    elements, size = ham_ref.shape[:2]
    odd = odd_domain()
    near, far = near_in[...].astype(F32), far_in[...].astype(F32)
    below = jnp.where(odd, near, far)
    above = jnp.where(odd, far, near)
    faces = stacked(low_in[...] + below, FACE_LANES).astype(BF16)
    ghost = stacked(widened(upper_in[...] + above)).astype(BF16)
    ghosts = ghosts_ref[...]
    pick_into(outside, ghost, ghosts >> 8, hosts_ref)
    for tile in tiles(high_ref.shape[1]):
        extra = pick(faces, high_ref[:, tile], faces_ref[:, tile], bands)
        inside[:, tile] = inside_ref[:, tile] + extra.astype(BF16)
    for pair in pairs(elements):
        products = []
        for e in pair:
            values = jnp.concatenate(
                [inside[:, e * IN_EL : (e + 1) * IN_EL], outside[:, e * FACE_EL : (e + 1) * FACE_EL]], axis=1
            )
            field_ref[:, e * size : (e + 1) * size] = values
            product = jnp.dot(values, ham_ref[e, :, size - 128 :], preferred_element_type=F32)
            products.append(product[:, 128 - FACE_EL :])
        top[:, pair[0] * FACE_EL : (pair[-1] + 1) * FACE_EL] = jnp.concatenate(products, axis=1)
    total = unstacked(scatter_sum(top, ghosts >> 8, hosts_ref, round_up(face_count, LANES) // LANES), bands)
    upper_ref[...] = (total[:, :face_count] * (2.0 / HALF_WIDTH)).astype(BF16)


def third_kernel(
    psi_ref, slots_ref, hots_ref, ham_ref, face_ref, own_in, near_in, far_in, field_ref, own_ref, inner
):
    bands, own = own_in.shape
    elements, size = ham_ref.shape[:2]
    face = face_ref[...]
    below = jnp.where(odd_domain(), near_in[...].astype(F32), far_in[...].astype(F32))
    added = lane_sums(spread_once(below, face >> 8, own // LANES), one_hot(face & 255))
    for pair in pairs(elements):
        products = [
            jnp.dot(field_ref[:, e * size : (e + 1) * size], ham_ref[e], preferred_element_type=F32) for e in pair
        ]
        split_products(products, inner, None, pair[0])
    total = unstacked(scatter_sum(inner, slots_ref[...] >> 8, hots_ref, own // LANES, True), bands)
    current = own_in[...] + unstacked(added, bands)
    own_ref[...] = 2.0 * ((total - CENTER * current) / HALF_WIDTH) - psi_ref[...]


def last_kernel(own_in, face_ref, below_in, out_ref, short_ref):
    bands, own = own_in.shape
    face = face_ref[...]
    added = lane_sums(spread_once(below_in[...].astype(F32), face >> 8, own // LANES), one_hot(face & 255))
    total = own_in[...] + unstacked(added, bands)
    out_ref[...] = total
    short_ref[...] = total[:, : short_ref.shape[1]].astype(BF16)


def call(kernel, out_shape, inputs, scratch=(), flops=0, moved=0, far=()):
    return pl.pallas_call(
        kernel,
        out_shape=out_shape,
        in_specs=[HBM if i in far else VMEM for i in range(len(inputs))],
        out_specs=jax.tree.map(lambda _: VMEM, out_shape),
        scratch_shapes=list(scratch),
        compiler_params=pltpu.CompilerParams(vmem_limit_bytes=LIMIT),
        cost_estimate=pl.CostEstimate(flops=flops, bytes_accessed=moved, transcendentals=0),
    )(*inputs)


def from_behind(block, axis, distance):
    devices = range(lax.axis_size(axis))
    route = [((i - distance) % len(devices), i) for i in devices]
    return lax.ppermute(block, axis, route)


def paired(groups):
    return groups & (groups - 1) == 0


def partner(block, axis, distance):
    size = lax.axis_size(axis)
    if paired(size):
        return lax.ppermute(block, axis, [(i, i ^ distance) for i in range(size)])
    return from_behind(block, axis, distance)


def filter_field(psi, ham, conn, face_rows):
    bands, nodes = psi.shape
    elements, size = conn.shape
    own = round_up(nodes, LANES)
    faces = round_up(face_rows.shape[0], 128)
    trimmed = round_up(nodes, 128)
    face_count = elements * (size - IN_EL)
    inner_count = elements * IN_EL
    shape = jax.ShapeDtypeStruct
    face_field = shape((bands, faces), F32)
    own_field = shape((bands, own), F32)
    inner = pltpu.VMEM((bands, inner_count), F32)
    top = pltpu.VMEM((bands, face_count), F32)
    inside_field = pltpu.VMEM((bands, inner_count), BF16)
    outside = pltpu.VMEM((bands, face_count), BF16)

    with jax.named_scope("face_values"):
        values, wide, conn, face = call(
            face_kernel,
            (shape((bands, faces), BF16), own_field, shape(conn.shape, jnp.int32), shape((1, faces), jnp.int32)),
            [pltpu.with_memory_space_constraint(array, pltpu.HBM) for array in (psi, conn, face_rows)],
            (pltpu.VMEM(psi.shape, F32), pltpu.VMEM(face_rows.shape, jnp.int32), pltpu.SemaphoreType.DMA((3,))),
            far=(0, 1, 2), flops=2 * 10**10, moved=4 * 10**7,
        )
    ghost = from_behind(values, "space", -1)
    with jax.named_scope("near_values"):
        inside, slots, ghosts, hots, hosts = call(
            functools.partial(near_kernel, nodes),
            (
                shape((bands, inner_count), BF16), shape((1, inner_count), jnp.int32), shape((1, face_count), jnp.int32),
                shape((LANES, inner_count), BF16), shape((LANES, face_count), BF16),
            ),
            (wide, conn),
        )
    with jax.named_scope("interior"):
        part = call(
            interior_kernel, shape((bands, elements * size), F32), (inside, ham), flops=4 * 10**9, moved=8 * 10**6
        )
    with jax.named_scope("first_step"):
        current, upper, to_near, to_far = call(
            first_kernel, (own_field, face_field, *[shape(face_field.shape, BF16)] * 2),
            (wide, slots, ghosts, hots, hosts, ham, face, ghost, part), (inner, top, outside),
            flops=4 * 10**9, moved=10**6,
        )
    domains = lax.axis_size("space")
    from_far = lax.ppermute(to_far, "space", [(i, ((i + 1 ^ 1) - 1) % domains) for i in range(domains)])
    from_near = lax.ppermute(to_near, "space", [(i, i ^ 1) for i in range(domains)])
    with jax.named_scope("off_face"):
        low, inside, high, faces = call(
            far_kernel,
            (face_field, shape((bands, inner_count), BF16), shape((1, inner_count), jnp.int32), shape((FACE_LANES, inner_count), BF16)),
            (current, slots, hots, face), flops=4 * 10**9, moved=10**6,
        )
    with jax.named_scope("second_step"):
        field, upper = call(
            second_kernel, (shape((bands, elements * size), BF16), shape(face_field.shape, BF16)),
            (inside, high, faces, ghosts, hosts, ham, low, upper, from_near, from_far), (inside_field, top, outside),
            flops=4 * 10**9, moved=10**6,
        )
    from_below = from_behind(upper, "space", 1)
    with jax.named_scope("second_sums"):
        following = call(
            third_kernel, own_field, (wide, slots, hots, ham, face, current, from_near, from_far, field), (inner,),
            flops=4 * 10**9, moved=8 * 10**6,
        )
    with jax.named_scope("last_faces"):
        return call(last_kernel, (own_field, shape((bands, trimmed), BF16)), (following, face, from_below))


def gram_kernel(*refs):
    *blocks, terms_ref, gram_ref = refs
    bands = blocks[0].shape[0]
    total = bands * len(blocks)
    me = lax.axis_index("band")
    for distance, block in enumerate(blocks):
        source = me ^ distance if paired(len(blocks)) else lax.rem(me - distance + len(blocks), len(blocks))
        source = pl.multiple_of(source * bands, bands)
        if distance == 0:
            upper, lower = halves(block[...])
            terms_ref[total:, :] = lower
        else:
            upper = widened(block[...])
        terms_ref[pl.ds(source, bands), :] = upper
    terms = terms_ref[...]
    both = lax.dot_general(terms, terms, (((1,), (1,)), ((), ())), preferred_element_type=F32)
    down = jnp.concatenate([both[total:]] * len(blocks), axis=0)
    across = jnp.concatenate([both[:, total:]] * len(blocks), axis=1)
    corner = jnp.concatenate([down[:, total:]] * len(blocks), axis=1)
    own_row = lax.broadcasted_iota(jnp.int32, (total, total), 0) // bands == me
    own_column = lax.broadcasted_iota(jnp.int32, (total, total), 1) // bands == me
    cross = jnp.where(own_row, down[:, :total], 0.0) + jnp.where(own_column, across[:total], 0.0)
    gram = both[:total, :total] + (cross + jnp.where(own_row & own_column, corner, 0.0))
    gram_ref[...] = jnp.concatenate([gram[: total // 2], gram[total // 2 :]], axis=1)


def inverse_factor(matrix, block=16):
    size = matrix.shape[0]
    width = 2 * size
    lane = lax.broadcasted_iota(jnp.int32, (8, width), 1)
    row = lax.broadcasted_iota(jnp.int32, (8, width), 0)
    wide = jnp.concatenate([matrix, jnp.zeros((size, size), F32)], axis=1)
    groups = [wide[8 * g : 8 * g + 8] + jnp.where(lane == row + (size + 8 * g), 1.0, 0.0) for g in range(size // 8)]
    for k in range(0, size, block):
        columns = [
            {g: jnp.broadcast_to(groups[g][:, j : j + 1], (8, width)) for g in range(k // 8, size // 8)}
            for j in range(k, k + block)
        ]
        for q in range(block):
            first, at = divmod(k + q, 8)
            scale = 1.0 / columns[q][first][at : at + 1]
            column = {g: rows for g, rows in columns[q].items() if g >= first}
            column[first] = jnp.where(row > at, column[first], 0.0)
            for p in range(q + 1, block):
                factor = columns[p][first][at : at + 1] * scale
                for g, weight in column.items():
                    columns[p][g] = columns[p][g] - weight * factor
            factor = groups[first][at : at + 1] * scale
            for g, weight in column.items():
                groups[g] = groups[g] - weight * factor
    out = []
    for g, rows in enumerate(groups):
        pivot = jnp.sum(jnp.where(lane == row + 8 * g, rows, 0.0), axis=1, keepdims=True)
        out.append(rows[:, size:] / jnp.sqrt(pivot))
    return jnp.concatenate(out, axis=0)


def ortho_kernel(nodes, count, gram_ref, terms_ref, out_ref, inverse_ref):
    bands = out_ref.shape[0]
    total = inverse_ref.shape[0]
    gram = jnp.concatenate([gram_ref[:, :total], gram_ref[:, total:]], axis=0)
    inverse_ref[...] = inverse_factor(gram / count)
    first = pl.multiple_of(lax.axis_index("band") * bands, bands)
    own = inverse_ref[pl.ds(first, bands), :]
    column = lax.broadcasted_iota(jnp.int32, own.shape, 1)
    diagonal = jnp.where(column // bands == lax.axis_index("band"), own, 0.0)
    diagonal = sum(diagonal[:, i : i + bands] for i in range(0, total, bands))
    rows = jnp.concatenate(halves(jnp.concatenate([own, diagonal], axis=1)), axis=0)
    for tile in tiles(nodes, 2 * LANES):
        both = jnp.dot(rows, terms_ref[:, tile], preferred_element_type=F32)
        out_ref[:, tile] = both[:bands] + both[bands:]


def space_sum(block):
    size = lax.axis_size("space")
    if size & (size - 1):
        return lax.psum(block, "space")
    step = 1
    while step < size:
        span = 2 if step == 1 or step * 2 == size else 4
        parts = [
            lax.ppermute(block, "space", [(i, i ^ (step * k)) for i in range(size)]) for k in range(1, span)
        ]
        block = sum(parts, block)
        step *= span
    return block


def per_device(psi, ham, conn, face_rows):
    bands, nodes = psi.shape
    following, short = filter_field(psi, ham, conn, face_rows)
    groups = lax.axis_size("band")
    total = groups * bands
    own = round_up(nodes, LANES)
    shape = jax.ShapeDtypeStruct
    blocks = [following] + [partner(short, "band", i) for i in range(1, groups)]
    with jax.named_scope("gram"):
        terms, gram = call(gram_kernel, (shape((total + bands, own), BF16), shape((total // 2, 2 * total), F32)), blocks)
    with jax.named_scope("gram_sum"):
        gram = space_sum(gram)
    with jax.named_scope("orthonormal"):
        return call(
            functools.partial(ortho_kernel, nodes, nodes * lax.axis_size("space")),
            shape((bands, nodes), F32), (gram, terms), (pltpu.VMEM((total, total), F32),),
        )


def solution(mesh):
    placed = (P("band", "space"), P("space", None, None), P("space", None), P("space"))
    return jax.shard_map(
        per_device, mesh=mesh, in_specs=placed, out_specs=P("band", "space"), check_vma=False
    )
```

```python
import functools

import jax
import jax.numpy as jnp
from jax import lax
from jax.experimental import pallas as pl
from jax.experimental.pallas import tpu as pltpu
from jax.sharding import PartitionSpec as P

FACE_EL = 64
IN_EL = 448
LANES = 256
FACE_LANES = 128

CENTER = 6.25
HALF_WIDTH = 7.5

F32 = jnp.float32
BF16 = jnp.bfloat16
VMEM = pl.BlockSpec(memory_space=pltpu.VMEM)
HBM = pl.BlockSpec(memory_space=pltpu.HBM)
LIMIT = 24 * 1024 * 1024


def round_up(count, unit):
    return -(-count // unit) * unit


def one_hot(low, lanes=LANES):
    shape = (lanes, low.shape[1])
    rows = lax.broadcasted_iota(jnp.int32, shape, 0).astype(jnp.int16)
    low = jnp.broadcast_to(low, (16, low.shape[1])).astype(jnp.int16)
    low = jnp.concatenate([low] * (lanes // 16), axis=0)
    return jnp.where(rows == low, jnp.ones(shape, BF16), jnp.zeros(shape, BF16))


def stacked(field, lanes=LANES):
    blocks = field.shape[1] // lanes
    return jnp.concatenate([field[:, i * lanes : (i + 1) * lanes] for i in range(blocks)], axis=0)


def unstacked(rows, bands):
    blocks = rows.shape[0] // bands
    return jnp.concatenate([rows[i * bands : (i + 1) * bands] for i in range(blocks)], axis=1)


def pick(rows, high, low_hot, bands, first=0):
    table = jnp.dot(rows, low_hot, preferred_element_type=F32)
    out = jnp.zeros((bands, low_hot.shape[1]), F32)
    for i in range(rows.shape[0] // bands):
        out = jnp.where(high == i + first, table[i * bands : (i + 1) * bands], out)
    return out


def halves(values):
    upper = values.astype(BF16)
    return upper, (values - upper.astype(F32)).astype(BF16)


def spread(values, high, blocks, first=0):
    rows = []
    for part in halves(values):
        wide = part.astype(F32)
        for i in range(blocks):
            rows.append(jnp.where(high == i + first, wide, 0.0).astype(BF16))
    return jnp.concatenate(rows, axis=0)


def lane_sums(rows, low_hot):
    return lax.dot_general(rows, low_hot, (((1,), (1,)), ((), ())), preferred_element_type=F32)


def tiles(count, width=LANES):
    return [slice(start, min(start + width, count)) for start in range(0, count, width)]


def hot_into(hots_ref, low):
    for tile in tiles(low.shape[1]):
        hots_ref[:, tile] = one_hot(low[:, tile])


def pick_into(out_ref, rows, high, hots_ref):
    for tile in tiles(high.shape[1]):
        out_ref[:, tile] = pick(rows, high[:, tile], hots_ref[:, tile], out_ref.shape[0]).astype(out_ref.dtype)


def spread_once(values, high, blocks):
    return jnp.concatenate([jnp.where(high == i, values, 0.0).astype(BF16) for i in range(blocks)], axis=0)


def scatter_sum(values_ref, high, hots_ref, blocks, once=False):
    total = None
    for tile in tiles(high.shape[1], 2 * LANES):
        rows = (spread_once if once else spread)(values_ref[:, tile], high[:, tile], blocks)
        part = lax.dot_general(
            rows, hots_ref[:, tile],
            (((1,), (1,)), ((), ())), preferred_element_type=F32,
        )
        total = part if total is None else total + part
    if once:
        return total
    count = total.shape[0] // 2
    return total[:count] + total[count:]


def split_products(products, inner_ref, top_ref, first):
    inner = jnp.concatenate([product[:, :IN_EL] for product in products], axis=1)
    top = jnp.concatenate([product[:, IN_EL:] for product in products], axis=1)
    inner_ref[:, first * IN_EL : first * IN_EL + inner.shape[1]] = inner
    if top_ref is not None:
        top_ref[:, first * FACE_EL : first * FACE_EL + top.shape[1]] = top


def pairs(elements):
    return [range(e, min(e + 2, elements)) for e in range(0, elements, 2)]


def packed(ref, width, first, last):
    return jnp.concatenate([ref[e : e + 1, first:last] for e in range(width)], axis=1)


def face_kernel(psi_hbm, conn_hbm, face_hbm, values_ref, psi_out, conn_out, face_out, psi_ref, face_ref, sems):
    bands, nodes = psi_hbm.shape
    copies = [
        pltpu.make_async_copy(face_hbm, face_ref, sems.at[0]),
        pltpu.make_async_copy(psi_hbm, psi_ref, sems.at[1]),
        pltpu.make_async_copy(conn_hbm, conn_out, sems.at[2]),
    ]
    for copy in copies:
        copy.start()
    psi_out[...] = jnp.zeros_like(psi_out)
    face_out[...] = jnp.full_like(face_out, -1)
    copies[0].wait()
    face_out[:, : face_ref.shape[0]] = face_ref[...].reshape(1, face_ref.shape[0])
    face = face_out[...]
    hot = one_hot(face & 255)
    copies[1].wait()
    psi_out[:, :nodes] = psi_ref[...]
    values_ref[...] = pick(stacked(psi_out[...]).astype(BF16), face >> 8, hot, bands).astype(BF16)
    copies[2].wait()


def near_kernel(nodes, psi_ref, conn_ref, inside_ref, slots_ref, ghosts_ref, hots_ref, hosts_ref):
    elements, size = conn_ref.shape
    slots_ref[...] = packed(conn_ref, elements, 0, IN_EL)
    ghosts_ref[...] = packed(conn_ref, elements, IN_EL, size) - nodes
    hot_into(hosts_ref, ghosts_ref[...] & 255)
    slots = slots_ref[...]
    hot_into(hots_ref, slots & 255)
    pick_into(inside_ref, stacked(psi_ref[...]).astype(BF16), slots >> 8, hots_ref)


def interior_kernel(inside_ref, ham_ref, part_ref):
    elements, size = ham_ref.shape[:2]
    for e in range(elements):
        part_ref[:, e * size : (e + 1) * size] = jnp.dot(
            inside_ref[:, e * IN_EL : (e + 1) * IN_EL], ham_ref[e, :IN_EL, :], preferred_element_type=F32
        )


def widened(values):
    bands, count = values.shape
    if count % LANES == 0:
        return values
    return jnp.concatenate([values, jnp.zeros((bands, round_up(count, LANES) - count), values.dtype)], axis=1)


def odd_domain():
    return lax.rem(lax.axis_index("space"), 2) == 1


def first_kernel(
    psi_ref, slots_ref, ghosts_ref, hots_ref, hosts_ref, ham_ref, face_ref, ghost_ref, part_ref,
    own_ref, upper_ref, near_ref, far_ref, inner, top, outside,
):
    bands, own = psi_ref.shape
    elements, size = ham_ref.shape[:2]
    face_count = ghost_ref.shape[1]
    ghosts = ghosts_ref[...]
    pick_into(outside, stacked(widened(ghost_ref[...])), ghosts >> 8, hosts_ref)
    for pair in pairs(elements):
        products = [
            part_ref[:, e * size : (e + 1) * size]
            + jnp.dot(outside[:, e * FACE_EL : (e + 1) * FACE_EL], ham_ref[e, IN_EL:, :], preferred_element_type=F32)
            for e in pair
        ]
        split_products(products, inner, top, pair[0])
    upper = scatter_sum(top, ghosts >> 8, hosts_ref, round_up(face_count, LANES) // LANES)
    upper = unstacked(upper, bands)[:, :face_count] / HALF_WIDTH
    upper_ref[...] = upper
    total = unstacked(scatter_sum(inner, slots_ref[...] >> 8, hots_ref, own // LANES, True), bands)
    current = (total - CENTER * psi_ref[...]) / HALF_WIDTH
    own_ref[...] = current
    face = face_ref[...]
    face_hot = one_hot(face & 255)
    low = pick(stacked(current).astype(BF16), face >> 8, face_hot, bands)
    odd = odd_domain()
    near_ref[...] = jnp.where(odd, low, upper).astype(BF16)
    far_ref[...] = jnp.where(odd, upper, low).astype(BF16)


def far_kernel(own_in, slots_ref, hots_ref, face_ref, low_ref, inside_ref, high_ref, faces_ref):
    bands, own = own_in.shape
    blocks = round_up(own // LANES, 16)
    face = face_ref[...]
    number = lax.broadcasted_iota(jnp.int32, (blocks, face.shape[1]), 1)
    held = lax.broadcasted_iota(jnp.int32, number.shape, 0) == (face >> 8)
    digits = [jnp.where(held, digit, 0).astype(F32).astype(BF16) for digit in (number // FACE_LANES + 1, number % FACE_LANES)]
    face_hot = one_hot(face & 255)
    table = lax.dot_general(
        jnp.concatenate(digits, axis=0), face_hot, (((1,), (1,)), ((), ())), preferred_element_type=F32
    ).astype(BF16)
    rows, rest = halves(stacked(own_in[...]))
    low_ref[...] = pick(rows, face >> 8, face_hot, bands) + pick(rest, face >> 8, face_hot, bands)
    for tile in tiles(slots_ref.shape[1]):
        high = slots_ref[:, tile] >> 8
        hot = hots_ref[:, tile]
        both = jnp.dot(table, hot, preferred_element_type=F32)
        held = lax.broadcasted_iota(jnp.int32, (blocks, both.shape[1]), 0) == high
        block = jnp.sum(jnp.where(held, both[:blocks], 0.0), axis=0, keepdims=True).astype(jnp.int32)
        lane = jnp.sum(jnp.where(held, both[blocks:], 0.0), axis=0, keepdims=True).astype(jnp.int32)
        high_ref[:, tile] = block - 1
        faces_ref[:, tile] = one_hot(jnp.where(block > 0, lane, -1), FACE_LANES)
        inside_ref[:, tile] = jnp.where(block > 0, 0.0, pick(rows, high, hot, bands)).astype(BF16)


def second_kernel(
    inside_ref, high_ref, faces_ref, ghosts_ref, hosts_ref, ham_ref, low_in, upper_in, near_in, far_in,
    field_ref, upper_ref, inside, top, outside,
):
    bands, face_count = upper_in.shape
    elements, size = ham_ref.shape[:2]
    odd = odd_domain()
    near, far = near_in[...].astype(F32), far_in[...].astype(F32)
    below = jnp.where(odd, near, far)
    above = jnp.where(odd, far, near)
    faces = stacked(low_in[...] + below, FACE_LANES).astype(BF16)
    ghost = stacked(widened(upper_in[...] + above)).astype(BF16)
    ghosts = ghosts_ref[...]
    pick_into(outside, ghost, ghosts >> 8, hosts_ref)
    for tile in tiles(high_ref.shape[1]):
        extra = pick(faces, high_ref[:, tile], faces_ref[:, tile], bands)
        inside[:, tile] = inside_ref[:, tile] + extra.astype(BF16)
    for pair in pairs(elements):
        products = []
        for e in pair:
            values = jnp.concatenate(
                [inside[:, e * IN_EL : (e + 1) * IN_EL], outside[:, e * FACE_EL : (e + 1) * FACE_EL]], axis=1
            )
            field_ref[:, e * size : (e + 1) * size] = values
            product = jnp.dot(values, ham_ref[e, :, size - 128 :], preferred_element_type=F32)
            products.append(product[:, 128 - FACE_EL :])
        top[:, pair[0] * FACE_EL : (pair[-1] + 1) * FACE_EL] = jnp.concatenate(products, axis=1)
    total = unstacked(scatter_sum(top, ghosts >> 8, hosts_ref, round_up(face_count, LANES) // LANES), bands)
    upper_ref[...] = (total[:, :face_count] * (2.0 / HALF_WIDTH)).astype(BF16)


def third_kernel(
    psi_ref, slots_ref, hots_ref, ham_ref, face_ref, own_in, near_in, far_in, field_ref, own_ref, inner
):
    bands, own = own_in.shape
    elements, size = ham_ref.shape[:2]
    face = face_ref[...]
    below = jnp.where(odd_domain(), near_in[...].astype(F32), far_in[...].astype(F32))
    added = lane_sums(spread_once(below, face >> 8, own // LANES), one_hot(face & 255))
    for pair in pairs(elements):
        products = [
            jnp.dot(field_ref[:, e * size : (e + 1) * size], ham_ref[e], preferred_element_type=F32) for e in pair
        ]
        split_products(products, inner, None, pair[0])
    total = unstacked(scatter_sum(inner, slots_ref[...] >> 8, hots_ref, own // LANES, True), bands)
    current = own_in[...] + unstacked(added, bands)
    own_ref[...] = 2.0 * ((total - CENTER * current) / HALF_WIDTH) - psi_ref[...]


def last_kernel(own_in, face_ref, below_in, out_ref, short_ref):
    bands, own = own_in.shape
    face = face_ref[...]
    added = lane_sums(spread_once(below_in[...].astype(F32), face >> 8, own // LANES), one_hot(face & 255))
    total = own_in[...] + unstacked(added, bands)
    out_ref[...] = total
    short_ref[...] = total[:, : short_ref.shape[1]].astype(BF16)


def call(kernel, out_shape, inputs, scratch=(), flops=0, moved=0, far=()):
    return pl.pallas_call(
        kernel,
        out_shape=out_shape,
        in_specs=[HBM if i in far else VMEM for i in range(len(inputs))],
        out_specs=jax.tree.map(lambda _: VMEM, out_shape),
        scratch_shapes=list(scratch),
        compiler_params=pltpu.CompilerParams(vmem_limit_bytes=LIMIT),
        cost_estimate=pl.CostEstimate(flops=flops, bytes_accessed=moved, transcendentals=0),
    )(*inputs)


def from_behind(block, axis, distance):
    devices = range(lax.axis_size(axis))
    route = [((i - distance) % len(devices), i) for i in devices]
    return lax.ppermute(block, axis, route)


def paired(groups):
    return groups & (groups - 1) == 0


def partner(block, axis, distance):
    size = lax.axis_size(axis)
    if paired(size):
        return lax.ppermute(block, axis, [(i, i ^ distance) for i in range(size)])
    return from_behind(block, axis, distance)


def filter_field(psi, ham, conn, face_rows):
    bands, nodes = psi.shape
    elements, size = conn.shape
    own = round_up(nodes, LANES)
    faces = round_up(face_rows.shape[0], 128)
    trimmed = round_up(nodes, 128)
    face_count = elements * (size - IN_EL)
    inner_count = elements * IN_EL
    shape = jax.ShapeDtypeStruct
    face_field = shape((bands, faces), F32)
    own_field = shape((bands, own), F32)
    inner = pltpu.VMEM((bands, inner_count), F32)
    top = pltpu.VMEM((bands, face_count), F32)
    inside_field = pltpu.VMEM((bands, inner_count), BF16)
    outside = pltpu.VMEM((bands, face_count), BF16)

    with jax.named_scope("face_values"):
        values, wide, conn, face = call(
            face_kernel,
            (shape((bands, faces), BF16), own_field, shape(conn.shape, jnp.int32), shape((1, faces), jnp.int32)),
            [pltpu.with_memory_space_constraint(array, pltpu.HBM) for array in (psi, conn, face_rows)],
            (pltpu.VMEM(psi.shape, F32), pltpu.VMEM(face_rows.shape, jnp.int32), pltpu.SemaphoreType.DMA((3,))),
            far=(0, 1, 2), flops=2 * 10**10, moved=4 * 10**7,
        )
    ghost = from_behind(values, "space", -1)
    with jax.named_scope("near_values"):
        inside, slots, ghosts, hots, hosts = call(
            functools.partial(near_kernel, nodes),
            (
                shape((bands, inner_count), BF16), shape((1, inner_count), jnp.int32), shape((1, face_count), jnp.int32),
                shape((LANES, inner_count), BF16), shape((LANES, face_count), BF16),
            ),
            (wide, conn),
        )
    with jax.named_scope("interior"):
        part = call(
            interior_kernel, shape((bands, elements * size), F32), (inside, ham), flops=4 * 10**9, moved=8 * 10**6
        )
    with jax.named_scope("first_step"):
        current, upper, to_near, to_far = call(
            first_kernel, (own_field, face_field, *[shape(face_field.shape, BF16)] * 2),
            (wide, slots, ghosts, hots, hosts, ham, face, ghost, part), (inner, top, outside),
            flops=4 * 10**9, moved=10**6,
        )
    domains = lax.axis_size("space")
    from_far = lax.ppermute(to_far, "space", [(i, ((i + 1 ^ 1) - 1) % domains) for i in range(domains)])
    from_near = lax.ppermute(to_near, "space", [(i, i ^ 1) for i in range(domains)])
    with jax.named_scope("off_face"):
        low, inside, high, faces = call(
            far_kernel,
            (face_field, shape((bands, inner_count), BF16), shape((1, inner_count), jnp.int32), shape((FACE_LANES, inner_count), BF16)),
            (current, slots, hots, face), flops=4 * 10**9, moved=10**6,
        )
    with jax.named_scope("second_step"):
        field, upper = call(
            second_kernel, (shape((bands, elements * size), BF16), shape(face_field.shape, BF16)),
            (inside, high, faces, ghosts, hosts, ham, low, upper, from_near, from_far), (inside_field, top, outside),
            flops=4 * 10**9, moved=10**6,
        )
    from_below = from_behind(upper, "space", 1)
    with jax.named_scope("second_sums"):
        following = call(
            third_kernel, own_field, (wide, slots, hots, ham, face, current, from_near, from_far, field), (inner,),
            flops=4 * 10**9, moved=8 * 10**6,
        )
    with jax.named_scope("last_faces"):
        return call(last_kernel, (own_field, shape((bands, trimmed), BF16)), (following, face, from_below))


def gram_kernel(*refs):
    *blocks, terms_ref, gram_ref = refs
    bands = blocks[0].shape[0]
    total = bands * len(blocks)
    me = lax.axis_index("band")
    for distance, block in enumerate(blocks):
        source = me ^ distance if paired(len(blocks)) else lax.rem(me - distance + len(blocks), len(blocks))
        source = pl.multiple_of(source * bands, bands)
        if distance == 0:
            upper, lower = halves(block[...])
            terms_ref[total:, :] = lower
        else:
            upper = widened(block[...])
        terms_ref[pl.ds(source, bands), :] = upper
    terms = terms_ref[...]
    both = lax.dot_general(terms, terms, (((1,), (1,)), ((), ())), preferred_element_type=F32)
    down = jnp.concatenate([both[total:]] * len(blocks), axis=0)
    across = jnp.concatenate([both[:, total:]] * len(blocks), axis=1)
    corner = jnp.concatenate([down[:, total:]] * len(blocks), axis=1)
    own_row = lax.broadcasted_iota(jnp.int32, (total, total), 0) // bands == me
    own_column = lax.broadcasted_iota(jnp.int32, (total, total), 1) // bands == me
    cross = jnp.where(own_row, down[:, :total], 0.0) + jnp.where(own_column, across[:total], 0.0)
    gram = both[:total, :total] + (cross + jnp.where(own_row & own_column, corner, 0.0))
    gram_ref[...] = jnp.concatenate([gram[: total // 2], gram[total // 2 :]], axis=1)


def inverse_factor(matrix, block=16):
    size = matrix.shape[0]
    width = 2 * size
    lane = lax.broadcasted_iota(jnp.int32, (8, width), 1)
    row = lax.broadcasted_iota(jnp.int32, (8, width), 0)
    wide = jnp.concatenate([matrix, jnp.zeros((size, size), F32)], axis=1)
    groups = [wide[8 * g : 8 * g + 8] + jnp.where(lane == row + (size + 8 * g), 1.0, 0.0) for g in range(size // 8)]
    for k in range(0, size, block):
        columns = [
            {g: jnp.broadcast_to(groups[g][:, j : j + 1], (8, width)) for g in range(k // 8, size // 8)}
            for j in range(k, k + block)
        ]
        for q in range(block):
            first, at = divmod(k + q, 8)
            scale = 1.0 / columns[q][first][at : at + 1]
            column = {g: rows for g, rows in columns[q].items() if g >= first}
            column[first] = jnp.where(row > at, column[first], 0.0)
            for p in range(q + 1, block):
                factor = columns[p][first][at : at + 1] * scale
                for g, weight in column.items():
                    columns[p][g] = columns[p][g] - weight * factor
            factor = groups[first][at : at + 1] * scale
            for g, weight in column.items():
                groups[g] = groups[g] - weight * factor
    out = []
    for g, rows in enumerate(groups):
        pivot = jnp.sum(jnp.where(lane == row + 8 * g, rows, 0.0), axis=1, keepdims=True)
        out.append(rows[:, size:] / jnp.sqrt(pivot))
    return jnp.concatenate(out, axis=0)


def ortho_kernel(nodes, count, gram_ref, terms_ref, out_ref, inverse_ref):
    bands = out_ref.shape[0]
    total = inverse_ref.shape[0]
    gram = jnp.concatenate([gram_ref[:, :total], gram_ref[:, total:]], axis=0)
    inverse_ref[...] = inverse_factor(gram / count)
    first = pl.multiple_of(lax.axis_index("band") * bands, bands)
    own = inverse_ref[pl.ds(first, bands), :]
    column = lax.broadcasted_iota(jnp.int32, own.shape, 1)
    diagonal = jnp.where(column // bands == lax.axis_index("band"), own, 0.0)
    diagonal = sum(diagonal[:, i : i + bands] for i in range(0, total, bands))
    rows = jnp.concatenate(halves(jnp.concatenate([own, diagonal], axis=1)), axis=0)
    for tile in tiles(nodes, 2 * LANES):
        both = jnp.dot(rows, terms_ref[:, tile], preferred_element_type=F32)
        out_ref[:, tile] = both[:bands] + both[bands:]


def space_sum(block):
    size = lax.axis_size("space")
    if size & (size - 1):
        return lax.psum(block, "space")
    step = 1
    while step < size:
        span = 2 if step == 1 or step * 2 == size else 4
        parts = [
            lax.ppermute(block, "space", [(i, i ^ (step * k)) for i in range(size)]) for k in range(1, span)
        ]
        block = sum(parts, block)
        step *= span
    return block


def per_device(psi, ham, conn, face_rows):
    bands, nodes = psi.shape
    following, short = filter_field(psi, ham, conn, face_rows)
    groups = lax.axis_size("band")
    total = groups * bands
    own = round_up(nodes, LANES)
    shape = jax.ShapeDtypeStruct
    blocks = [following] + [partner(short, "band", i) for i in range(1, groups)]
    with jax.named_scope("gram"):
        terms, gram = call(gram_kernel, (shape((total + bands, own), BF16), shape((total // 2, 2 * total), F32)), blocks)
    with jax.named_scope("gram_sum"):
        gram = space_sum(gram)
    with jax.named_scope("orthonormal"):
        return call(
            functools.partial(ortho_kernel, nodes, nodes * lax.axis_size("space")),
            shape((bands, nodes), F32), (gram, terms), (pltpu.VMEM((total, total), F32),),
        )


def solution(mesh):
    placed = (P("band", "space"), P("space", None, None), P("space", None), P("space"))
    return jax.shard_map(
        per_device, mesh=mesh, in_specs=placed, out_specs=P("band", "space"), check_vma=False
    )
```

```python
import functools

import jax
import jax.numpy as jnp
from jax import lax
from jax.experimental import pallas as pl
from jax.experimental.pallas import tpu as pltpu
from jax.sharding import PartitionSpec as P

FACE_EL = 64
IN_EL = 448
LANES = 256
FACE_LANES = 128

CENTER = 6.25
HALF_WIDTH = 7.5

F32 = jnp.float32
BF16 = jnp.bfloat16
VMEM = pl.BlockSpec(memory_space=pltpu.VMEM)
HBM = pl.BlockSpec(memory_space=pltpu.HBM)
LIMIT = 24 * 1024 * 1024


def round_up(count, unit):
    return -(-count // unit) * unit


def one_hot(low, lanes=LANES):
    shape = (lanes, low.shape[1])
    rows = lax.broadcasted_iota(jnp.int32, shape, 0).astype(jnp.int16)
    low = jnp.broadcast_to(low, (16, low.shape[1])).astype(jnp.int16)
    low = jnp.concatenate([low] * (lanes // 16), axis=0)
    return jnp.where(rows == low, jnp.ones(shape, BF16), jnp.zeros(shape, BF16))


def stacked(field, lanes=LANES):
    blocks = field.shape[1] // lanes
    return jnp.concatenate([field[:, i * lanes : (i + 1) * lanes] for i in range(blocks)], axis=0)


def unstacked(rows, bands):
    blocks = rows.shape[0] // bands
    return jnp.concatenate([rows[i * bands : (i + 1) * bands] for i in range(blocks)], axis=1)


def pick(rows, high, low_hot, bands, first=0):
    table = jnp.dot(rows, low_hot, preferred_element_type=F32)
    out = jnp.zeros((bands, low_hot.shape[1]), F32)
    for i in range(rows.shape[0] // bands):
        out = jnp.where(high == i + first, table[i * bands : (i + 1) * bands], out)
    return out


def halves(values):
    upper = values.astype(BF16)
    return upper, (values - upper.astype(F32)).astype(BF16)


def spread(values, high, blocks, first=0):
    rows = []
    for part in halves(values):
        wide = part.astype(F32)
        for i in range(blocks):
            rows.append(jnp.where(high == i + first, wide, 0.0).astype(BF16))
    return jnp.concatenate(rows, axis=0)


def lane_sums(rows, low_hot):
    return lax.dot_general(rows, low_hot, (((1,), (1,)), ((), ())), preferred_element_type=F32)


def tiles(count, width=LANES):
    return [slice(start, min(start + width, count)) for start in range(0, count, width)]


def hot_into(hots_ref, low):
    for tile in tiles(low.shape[1]):
        hots_ref[:, tile] = one_hot(low[:, tile])


def pick_into(out_ref, rows, high, hots_ref):
    for tile in tiles(high.shape[1]):
        out_ref[:, tile] = pick(rows, high[:, tile], hots_ref[:, tile], out_ref.shape[0]).astype(out_ref.dtype)


def spread_once(values, high, blocks):
    values = values.astype(BF16)
    high = jnp.broadcast_to(high, values.shape).astype(jnp.int16)
    zero = jnp.zeros_like(values)
    return jnp.concatenate([jnp.where(high == jnp.int16(i), values, zero) for i in range(blocks)], axis=0)


def scatter_sum(values_ref, high, hots_ref, blocks, once=False):
    total = None
    for tile in tiles(high.shape[1], 2 * LANES):
        rows = (spread_once if once else spread)(values_ref[:, tile], high[:, tile], blocks)
        part = lax.dot_general(
            rows, hots_ref[:, tile],
            (((1,), (1,)), ((), ())), preferred_element_type=F32,
        )
        total = part if total is None else total + part
    if once:
        return total
    count = total.shape[0] // 2
    return total[:count] + total[count:]


def split_products(products, inner_ref, top_ref, first):
    inner = jnp.concatenate([product[:, :IN_EL] for product in products], axis=1)
    top = jnp.concatenate([product[:, IN_EL:] for product in products], axis=1)
    inner_ref[:, first * IN_EL : first * IN_EL + inner.shape[1]] = inner
    if top_ref is not None:
        top_ref[:, first * FACE_EL : first * FACE_EL + top.shape[1]] = top


def pairs(elements):
    return [range(e, min(e + 2, elements)) for e in range(0, elements, 2)]


def packed(ref, width, first, last):
    return jnp.concatenate([ref[e : e + 1, first:last] for e in range(width)], axis=1)


def face_kernel(psi_hbm, conn_hbm, face_hbm, values_ref, psi_out, conn_out, face_out, psi_ref, face_ref, sems):
    bands, nodes = psi_hbm.shape
    copies = [
        pltpu.make_async_copy(face_hbm, face_ref, sems.at[0]),
        pltpu.make_async_copy(psi_hbm, psi_ref, sems.at[1]),
        pltpu.make_async_copy(conn_hbm, conn_out, sems.at[2]),
    ]
    for copy in copies:
        copy.start()
    psi_out[...] = jnp.zeros_like(psi_out)
    face_out[...] = jnp.full_like(face_out, -1)
    copies[0].wait()
    face_out[:, : face_ref.shape[0]] = face_ref[...].reshape(1, face_ref.shape[0])
    face = face_out[...]
    hot = one_hot(face & 255)
    copies[1].wait()
    psi_out[:, :nodes] = psi_ref[...]
    values_ref[...] = pick(stacked(psi_out[...]).astype(BF16), face >> 8, hot, bands).astype(BF16)
    copies[2].wait()


def near_kernel(nodes, psi_ref, conn_ref, inside_ref, slots_ref, ghosts_ref, hots_ref, hosts_ref):
    elements, size = conn_ref.shape
    slots_ref[...] = packed(conn_ref, elements, 0, IN_EL)
    ghosts_ref[...] = packed(conn_ref, elements, IN_EL, size) - nodes
    hot_into(hosts_ref, ghosts_ref[...] & 255)
    slots = slots_ref[...]
    hot_into(hots_ref, slots & 255)
    pick_into(inside_ref, stacked(psi_ref[...]).astype(BF16), slots >> 8, hots_ref)


def interior_kernel(inside_ref, ham_ref, part_ref):
    elements, size = ham_ref.shape[:2]
    for e in range(elements):
        part_ref[:, e * size : (e + 1) * size] = jnp.dot(
            inside_ref[:, e * IN_EL : (e + 1) * IN_EL], ham_ref[e, :IN_EL, :], preferred_element_type=F32
        )


def widened(values):
    bands, count = values.shape
    if count % LANES == 0:
        return values
    return jnp.concatenate([values, jnp.zeros((bands, round_up(count, LANES) - count), values.dtype)], axis=1)


def odd_domain():
    return lax.rem(lax.axis_index("space"), 2) == 1


def first_kernel(
    psi_ref, slots_ref, ghosts_ref, hots_ref, hosts_ref, ham_ref, face_ref, ghost_ref, part_ref,
    own_ref, upper_ref, near_ref, far_ref, inner, top, outside,
):
    bands, own = psi_ref.shape
    elements, size = ham_ref.shape[:2]
    face_count = ghost_ref.shape[1]
    ghosts = ghosts_ref[...]
    pick_into(outside, stacked(widened(ghost_ref[...])), ghosts >> 8, hosts_ref)
    for pair in pairs(elements):
        products = [
            part_ref[:, e * size : (e + 1) * size]
            + jnp.dot(outside[:, e * FACE_EL : (e + 1) * FACE_EL], ham_ref[e, IN_EL:, :], preferred_element_type=F32)
            for e in pair
        ]
        split_products(products, inner, top, pair[0])
    upper = scatter_sum(top, ghosts >> 8, hosts_ref, round_up(face_count, LANES) // LANES)
    upper = unstacked(upper, bands)[:, :face_count] / HALF_WIDTH
    upper_ref[...] = upper
    total = unstacked(scatter_sum(inner, slots_ref[...] >> 8, hots_ref, own // LANES, True), bands)
    current = (total - CENTER * psi_ref[...]) / HALF_WIDTH
    own_ref[...] = current
    face = face_ref[...]
    face_hot = one_hot(face & 255)
    low = pick(stacked(current).astype(BF16), face >> 8, face_hot, bands)
    odd = odd_domain()
    near_ref[...] = jnp.where(odd, low, upper).astype(BF16)
    far_ref[...] = jnp.where(odd, upper, low).astype(BF16)


def far_kernel(own_in, slots_ref, hots_ref, face_ref, low_ref, inside_ref, high_ref, faces_ref):
    bands, own = own_in.shape
    blocks = round_up(own // LANES, 16)
    face = face_ref[...]
    number = lax.broadcasted_iota(jnp.int32, (blocks, face.shape[1]), 1)
    held = lax.broadcasted_iota(jnp.int32, number.shape, 0) == (face >> 8)
    digits = [jnp.where(held, digit, 0).astype(F32).astype(BF16) for digit in (number // FACE_LANES + 1, number % FACE_LANES)]
    face_hot = one_hot(face & 255)
    table = lax.dot_general(
        jnp.concatenate(digits, axis=0), face_hot, (((1,), (1,)), ((), ())), preferred_element_type=F32
    ).astype(BF16)
    rows, rest = halves(stacked(own_in[...]))
    low_ref[...] = pick(rows, face >> 8, face_hot, bands) + pick(rest, face >> 8, face_hot, bands)
    for tile in tiles(slots_ref.shape[1]):
        high = slots_ref[:, tile] >> 8
        hot = hots_ref[:, tile]
        both = jnp.dot(table, hot, preferred_element_type=F32)
        held = lax.broadcasted_iota(jnp.int32, (blocks, both.shape[1]), 0) == high
        block = jnp.sum(jnp.where(held, both[:blocks], 0.0), axis=0, keepdims=True).astype(jnp.int32)
        lane = jnp.sum(jnp.where(held, both[blocks:], 0.0), axis=0, keepdims=True).astype(jnp.int32)
        high_ref[:, tile] = block - 1
        faces_ref[:, tile] = one_hot(jnp.where(block > 0, lane, -1), FACE_LANES)
        inside_ref[:, tile] = jnp.where(block > 0, 0.0, pick(rows, high, hot, bands)).astype(BF16)


def second_kernel(
    inside_ref, high_ref, faces_ref, ghosts_ref, hosts_ref, ham_ref, low_in, upper_in, near_in, far_in,
    field_ref, upper_ref, inside, top, outside,
):
    bands, face_count = upper_in.shape
    elements, size = ham_ref.shape[:2]
    odd = odd_domain()
    near, far = near_in[...].astype(F32), far_in[...].astype(F32)
    below = jnp.where(odd, near, far)
    above = jnp.where(odd, far, near)
    faces = stacked(low_in[...] + below, FACE_LANES).astype(BF16)
    ghost = stacked(widened(upper_in[...] + above)).astype(BF16)
    ghosts = ghosts_ref[...]
    pick_into(outside, ghost, ghosts >> 8, hosts_ref)
    for tile in tiles(high_ref.shape[1]):
        extra = pick(faces, high_ref[:, tile], faces_ref[:, tile], bands)
        inside[:, tile] = inside_ref[:, tile] + extra.astype(BF16)
    for pair in pairs(elements):
        products = []
        for e in pair:
            values = jnp.concatenate(
                [inside[:, e * IN_EL : (e + 1) * IN_EL], outside[:, e * FACE_EL : (e + 1) * FACE_EL]], axis=1
            )
            field_ref[:, e * size : (e + 1) * size] = values
            product = jnp.dot(values, ham_ref[e, :, size - 128 :], preferred_element_type=F32)
            products.append(product[:, 128 - FACE_EL :])
        top[:, pair[0] * FACE_EL : (pair[-1] + 1) * FACE_EL] = jnp.concatenate(products, axis=1)
    total = unstacked(scatter_sum(top, ghosts >> 8, hosts_ref, round_up(face_count, LANES) // LANES), bands)
    upper_ref[...] = (total[:, :face_count] * (2.0 / HALF_WIDTH)).astype(BF16)


def third_kernel(
    psi_ref, slots_ref, hots_ref, ham_ref, face_ref, own_in, near_in, far_in, field_ref, own_ref, inner
):
    bands, own = own_in.shape
    elements, size = ham_ref.shape[:2]
    face = face_ref[...]
    below = jnp.where(odd_domain(), near_in[...].astype(F32), far_in[...].astype(F32))
    added = lane_sums(spread_once(below, face >> 8, own // LANES), one_hot(face & 255))
    for pair in pairs(elements):
        products = [
            jnp.dot(field_ref[:, e * size : (e + 1) * size], ham_ref[e], preferred_element_type=F32) for e in pair
        ]
        split_products(products, inner, None, pair[0])
    total = unstacked(scatter_sum(inner, slots_ref[...] >> 8, hots_ref, own // LANES, True), bands)
    current = own_in[...] + unstacked(added, bands)
    own_ref[...] = 2.0 * ((total - CENTER * current) / HALF_WIDTH) - psi_ref[...]


def last_kernel(own_in, face_ref, below_in, out_ref, short_ref):
    bands, own = own_in.shape
    face = face_ref[...]
    added = lane_sums(spread_once(below_in[...].astype(F32), face >> 8, own // LANES), one_hot(face & 255))
    total = own_in[...] + unstacked(added, bands)
    out_ref[...] = total
    short_ref[...] = total[:, : short_ref.shape[1]].astype(BF16)


def call(kernel, out_shape, inputs, scratch=(), flops=0, moved=0, far=()):
    return pl.pallas_call(
        kernel,
        out_shape=out_shape,
        in_specs=[HBM if i in far else VMEM for i in range(len(inputs))],
        out_specs=jax.tree.map(lambda _: VMEM, out_shape),
        scratch_shapes=list(scratch),
        compiler_params=pltpu.CompilerParams(vmem_limit_bytes=LIMIT),
        cost_estimate=pl.CostEstimate(flops=flops, bytes_accessed=moved, transcendentals=0),
    )(*inputs)


def from_behind(block, axis, distance):
    devices = range(lax.axis_size(axis))
    route = [((i - distance) % len(devices), i) for i in devices]
    return lax.ppermute(block, axis, route)


def paired(groups):
    return groups & (groups - 1) == 0


def partner(block, axis, distance):
    size = lax.axis_size(axis)
    if paired(size):
        return lax.ppermute(block, axis, [(i, i ^ distance) for i in range(size)])
    return from_behind(block, axis, distance)


def filter_field(psi, ham, conn, face_rows):
    bands, nodes = psi.shape
    elements, size = conn.shape
    own = round_up(nodes, LANES)
    faces = round_up(face_rows.shape[0], 128)
    trimmed = round_up(nodes, 128)
    face_count = elements * (size - IN_EL)
    inner_count = elements * IN_EL
    shape = jax.ShapeDtypeStruct
    face_field = shape((bands, faces), F32)
    own_field = shape((bands, own), F32)
    inner = pltpu.VMEM((bands, inner_count), F32)
    top = pltpu.VMEM((bands, face_count), F32)
    inside_field = pltpu.VMEM((bands, inner_count), BF16)
    outside = pltpu.VMEM((bands, face_count), BF16)

    with jax.named_scope("face_values"):
        values, wide, conn, face = call(
            face_kernel,
            (shape((bands, faces), BF16), own_field, shape(conn.shape, jnp.int32), shape((1, faces), jnp.int32)),
            [pltpu.with_memory_space_constraint(array, pltpu.HBM) for array in (psi, conn, face_rows)],
            (pltpu.VMEM(psi.shape, F32), pltpu.VMEM(face_rows.shape, jnp.int32), pltpu.SemaphoreType.DMA((3,))),
            far=(0, 1, 2), flops=2 * 10**10, moved=4 * 10**7,
        )
    ghost = from_behind(values, "space", -1)
    with jax.named_scope("near_values"):
        inside, slots, ghosts, hots, hosts = call(
            functools.partial(near_kernel, nodes),
            (
                shape((bands, inner_count), BF16), shape((1, inner_count), jnp.int32), shape((1, face_count), jnp.int32),
                shape((LANES, inner_count), BF16), shape((LANES, face_count), BF16),
            ),
            (wide, conn),
        )
    with jax.named_scope("interior"):
        part = call(
            interior_kernel, shape((bands, elements * size), F32), (inside, ham), flops=4 * 10**9, moved=8 * 10**6
        )
    with jax.named_scope("first_step"):
        current, upper, to_near, to_far = call(
            first_kernel, (own_field, face_field, *[shape(face_field.shape, BF16)] * 2),
            (wide, slots, ghosts, hots, hosts, ham, face, ghost, part), (inner, top, outside),
            flops=4 * 10**9, moved=10**6,
        )
    domains = lax.axis_size("space")
    from_far = lax.ppermute(to_far, "space", [(i, ((i + 1 ^ 1) - 1) % domains) for i in range(domains)])
    from_near = lax.ppermute(to_near, "space", [(i, i ^ 1) for i in range(domains)])
    with jax.named_scope("off_face"):
        low, inside, high, faces = call(
            far_kernel,
            (face_field, shape((bands, inner_count), BF16), shape((1, inner_count), jnp.int32), shape((FACE_LANES, inner_count), BF16)),
            (current, slots, hots, face), flops=4 * 10**9, moved=10**6,
        )
    with jax.named_scope("second_step"):
        field, upper = call(
            second_kernel, (shape((bands, elements * size), BF16), shape(face_field.shape, BF16)),
            (inside, high, faces, ghosts, hosts, ham, low, upper, from_near, from_far), (inside_field, top, outside),
            flops=4 * 10**9, moved=10**6,
        )
    from_below = from_behind(upper, "space", 1)
    with jax.named_scope("second_sums"):
        following = call(
            third_kernel, own_field, (wide, slots, hots, ham, face, current, from_near, from_far, field), (inner,),
            flops=4 * 10**9, moved=8 * 10**6,
        )
    with jax.named_scope("last_faces"):
        return call(last_kernel, (own_field, shape((bands, trimmed), BF16)), (following, face, from_below))


def gram_kernel(*refs):
    *blocks, terms_ref, gram_ref = refs
    bands = blocks[0].shape[0]
    total = bands * len(blocks)
    me = lax.axis_index("band")
    for distance, block in enumerate(blocks):
        source = me ^ distance if paired(len(blocks)) else lax.rem(me - distance + len(blocks), len(blocks))
        source = pl.multiple_of(source * bands, bands)
        if distance == 0:
            upper, lower = halves(block[...])
            terms_ref[total:, :] = lower
        else:
            upper = widened(block[...])
        terms_ref[pl.ds(source, bands), :] = upper
    terms = terms_ref[...]
    both = lax.dot_general(terms, terms, (((1,), (1,)), ((), ())), preferred_element_type=F32)
    down = jnp.concatenate([both[total:]] * len(blocks), axis=0)
    across = jnp.concatenate([both[:, total:]] * len(blocks), axis=1)
    corner = jnp.concatenate([down[:, total:]] * len(blocks), axis=1)
    own_row = lax.broadcasted_iota(jnp.int32, (total, total), 0) // bands == me
    own_column = lax.broadcasted_iota(jnp.int32, (total, total), 1) // bands == me
    cross = jnp.where(own_row, down[:, :total], 0.0) + jnp.where(own_column, across[:total], 0.0)
    gram = both[:total, :total] + (cross + jnp.where(own_row & own_column, corner, 0.0))
    gram_ref[...] = jnp.concatenate([gram[: total // 2], gram[total // 2 :]], axis=1)


def inverse_factor(matrix, block=16):
    size = matrix.shape[0]
    width = 2 * size
    lane = lax.broadcasted_iota(jnp.int32, (8, width), 1)
    row = lax.broadcasted_iota(jnp.int32, (8, width), 0)
    wide = jnp.concatenate([matrix, jnp.zeros((size, size), F32)], axis=1)
    groups = [wide[8 * g : 8 * g + 8] + jnp.where(lane == row + (size + 8 * g), 1.0, 0.0) for g in range(size // 8)]
    for k in range(0, size, block):
        columns = [
            {g: jnp.broadcast_to(groups[g][:, j : j + 1], (8, width)) for g in range(k // 8, size // 8)}
            for j in range(k, k + block)
        ]
        for q in range(block):
            first, at = divmod(k + q, 8)
            scale = 1.0 / columns[q][first][at : at + 1]
            column = {g: rows for g, rows in columns[q].items() if g >= first}
            column[first] = jnp.where(row > at, column[first], 0.0)
            for p in range(q + 1, block):
                factor = columns[p][first][at : at + 1] * scale
                for g, weight in column.items():
                    columns[p][g] = columns[p][g] - weight * factor
            factor = groups[first][at : at + 1] * scale
            for g, weight in column.items():
                groups[g] = groups[g] - weight * factor
    out = []
    for g, rows in enumerate(groups):
        pivot = jnp.sum(jnp.where(lane == row + 8 * g, rows, 0.0), axis=1, keepdims=True)
        out.append(rows[:, size:] / jnp.sqrt(pivot))
    return jnp.concatenate(out, axis=0)


def ortho_kernel(nodes, count, gram_ref, terms_ref, out_ref, inverse_ref):
    bands = out_ref.shape[0]
    total = inverse_ref.shape[0]
    gram = jnp.concatenate([gram_ref[:, :total], gram_ref[:, total:]], axis=0)
    inverse_ref[...] = inverse_factor(gram / count)
    first = pl.multiple_of(lax.axis_index("band") * bands, bands)
    own = inverse_ref[pl.ds(first, bands), :]
    column = lax.broadcasted_iota(jnp.int32, own.shape, 1)
    diagonal = jnp.where(column // bands == lax.axis_index("band"), own, 0.0)
    diagonal = sum(diagonal[:, i : i + bands] for i in range(0, total, bands))
    rows = jnp.concatenate(halves(jnp.concatenate([own, diagonal], axis=1)), axis=0)
    for tile in tiles(nodes, 2 * LANES):
        both = jnp.dot(rows, terms_ref[:, tile], preferred_element_type=F32)
        out_ref[:, tile] = both[:bands] + both[bands:]


def space_sum(block):
    size = lax.axis_size("space")
    if size & (size - 1):
        return lax.psum(block, "space")
    step = 1
    while step < size:
        span = 2 if step == 1 or step * 2 == size else 4
        parts = [
            lax.ppermute(block, "space", [(i, i ^ (step * k)) for i in range(size)]) for k in range(1, span)
        ]
        block = sum(parts, block)
        step *= span
    return block


def per_device(psi, ham, conn, face_rows):
    bands, nodes = psi.shape
    following, short = filter_field(psi, ham, conn, face_rows)
    groups = lax.axis_size("band")
    total = groups * bands
    own = round_up(nodes, LANES)
    shape = jax.ShapeDtypeStruct
    blocks = [following] + [partner(short, "band", i) for i in range(1, groups)]
    with jax.named_scope("gram"):
        terms, gram = call(gram_kernel, (shape((total + bands, own), BF16), shape((total // 2, 2 * total), F32)), blocks)
    with jax.named_scope("gram_sum"):
        gram = space_sum(gram)
    with jax.named_scope("orthonormal"):
        return call(
            functools.partial(ortho_kernel, nodes, nodes * lax.axis_size("space")),
            shape((bands, nodes), F32), (gram, terms), (pltpu.VMEM((total, total), F32),),
        )


def solution(mesh):
    placed = (P("band", "space"), P("space", None, None), P("space", None), P("space"))
    return jax.shard_map(
        per_device, mesh=mesh, in_specs=placed, out_specs=P("band", "space"), check_vma=False
    )
```
